32 devices in a mesh: group: 2 (over y), dom: 4 (over z), tm: 4 (over x, core).
Axes of the slice: x: 2, y: 2, z: 4, core: 2. Of those that a mesh axis runs over, the one named last changes fastest.
Arguments:
- state: float32 [192, 2, 4096], P(('group', 'tm'), None, 'dom'), parts along dimension 0, may hold values from 0 to 1
- dir_one: float32 [192, 2, 4096], P(('group', 'tm'), None, 'dom'), parts along dimension 0, may hold values from -6 to 6
- dir_two: float32 [192, 2, 4096], P(('group', 'tm'), None, 'dom'), parts along dimension 0, may hold values from -6 to 6
- feed: float32 [4096], P('dom'), may hold values from 0.02 to 0.5
- kill: float32 [4096], P('dom'), may hold values from 0.02 to 0.5
- tiles: float32 [32, 3, 128, 128], P('dom'), may hold values from -0.3125 to 0.3125
- tile_cols: int32 [32, 3], P('dom'), may hold values from 0 to 15, as said below
- send_rows: int32 [4, 4, 256], P('dom'), may hold values from 0 to 1023, as said below
- send_count: int32 [4, 4], P('dom'), may hold values from 171 to 256, as said below
Outputs:
- residual: float32 [192, 2, 4096], P(('group', 'tm'), None, 'dom'), parts along dimension 0
- jvp_one: float32 [192, 2, 4096], P(('group', 'tm'), None, 'dom'), parts along dimension 0
- jvp_two: float32 [192, 2, 4096], P(('group', 'tm'), None, 'dom'), parts along dimension 0
The draws below stay inside these ranges and needn't reach their ends.
There are 2 independent parts, one for each index of `group`. The reference program is written for one: setup_inputs(seed, part) draws one part's arguments, and reference() takes and returns one part's arrays. A program takes and returns all parts, laid end to end along the dimension named above; an argument that names none is the same for every part. Nothing has to cross between parts.
Inputs may be any that keep to these rules, and one draw needn't show every extreme that they name: `tile_cols`: column blocks below 8 are the partition's own blocks; 8 + j * 2 + b is block b of received slot j. Every received block is named by some tile of its partition. `send_rows`: entries are local cells of the sending partition; entries at or past the list's count are not read. `send_count`: some list is full in every draw.
All inputs are finite; a program needn't handle non-finite values.
Results may differ from the reference program's by a relative error of at most 0.0003.
Values sent between devices are 32-bit elements; how exact they have to be, the bound alone decides.
No kernel may reach another device: no remote copies, remote signals or barrier semaphores. Data moves between devices by JAX's collectives and lax.ppermute only.
A program may use at most 64 MiB of HBM per device.

```python
import math
import jax
import jax.numpy as jnp
from jax import lax

NB = 8
KT = 3
HB = 2
CELLS_DEV = 1024
NCELLS = 4096
NT = 96
ROWS_SEND = 256
N_DOM = 4


def draw_tile_cols(key, part):
    key = jax.random.fold_in(key, 11)
    first_key, second_key = jax.random.split(key)
    total_rows = N_DOM * NB
    halo_blocks = 4 * HB
    local_cols = jax.random.randint(first_key, (total_rows,), 0, NB)
    starts = jax.random.randint(second_key, (N_DOM, 1), 0, halo_blocks)
    starts = jnp.broadcast_to(starts, (N_DOM, NB)).reshape(total_rows)
    row_pos = jnp.arange(total_rows) % NB
    halo_one = NB + (row_pos + starts) % halo_blocks
    halo_two = NB + (row_pos + 2 * HB + starts) % halo_blocks
    return jnp.stack([local_cols, halo_one, halo_two], axis=1).astype(jnp.int32)


def draw_send_rows(key, part):
    key = jax.random.fold_in(key, 13)
    keys = jax.random.split(key, N_DOM * 4)
    perms = jax.vmap(lambda single: jax.random.permutation(single, CELLS_DEV))(keys)
    rows = perms[:, :ROWS_SEND].reshape(N_DOM, 4, ROWS_SEND)
    return rows.at[0, 0, 0].set(CELLS_DEV - 1).astype(jnp.int32)


def draw_send_count(key, part):
    key = jax.random.fold_in(key, 12)
    lowest = (2 * ROWS_SEND + 2) // 3
    counts = jax.random.randint(key, (N_DOM, 4), lowest, ROWS_SEND + 1)
    return counts.at[0, 0].set(ROWS_SEND).astype(jnp.int32)


def level_of(rng, extent, cuts, smallest, high):
    gain, own = 1.0, jax.random.fold_in(rng, 6)
    for dim, shards_of in cuts:
        heights = jnp.exp(jax.random.uniform(jax.random.fold_in(own, dim), (shards_of,), jnp.float32, smallest / len(cuts), high / len(cuts)))
        gain = gain * jnp.repeat(heights, extent[dim] // shards_of).reshape([-1 if axis == dim else 1 for axis in range(len(extent))])
    return gain


def scatter_about(key, dims, width, reach, shards=(), kind=jnp.bfloat16):
    gain = level_of(key, dims, shards, -0.22, 0.18) if shards else 1.0
    array = jax.random.normal(key, dims, jnp.float32) * width * gain
    return jnp.minimum(jnp.maximum(array, -reach), reach).astype(kind)


def setup_inputs(seed: int = 0, part: int = 0) -> dict:
    key_of = jax.random.split(jax.random.key(seed), 10)
    part_splits = jax.random.split(jax.random.fold_in(key_of[9], part), 10)
    return {
        "state": jnp.clip(1.0 * jax.random.uniform(part_splits[0], (NT, 2, NCELLS), jnp.float32) ** level_of(part_splits[0], (NT, 2, NCELLS), ((0, 4), (2, 4)), -0.2, 0.2), 0.0, 1.0),
        "dir_one": scatter_about(part_splits[1], (NT, 2, NCELLS), 1.0, 6.0, ((0, 4), (2, 4)), jnp.float32),
        "dir_two": scatter_about(part_splits[2], (NT, 2, NCELLS), 1.0, 6.0, ((0, 4), (2, 4)), jnp.float32),
        "feed": jnp.clip(jnp.exp(math.log(0.5) - 3.218876 * jax.random.uniform(key_of[3], (NCELLS,), jnp.float32) ** level_of(key_of[3], (NCELLS,), ((0, 4),), -0.2, 0.2)), 0.02, 0.5),
        "kill": jnp.clip(jnp.exp(math.log(0.5) - 3.218876 * jax.random.uniform(key_of[4], (NCELLS,), jnp.float32) ** level_of(key_of[4], (NCELLS,), ((0, 4),), -0.2, 0.2)), 0.02, 0.5),
        "tiles": scatter_about(key_of[5], (N_DOM * NB, KT, 128, 128), (KT * 128) ** -0.5, 0.3125, ((0, 4),), jnp.float32),
        "tile_cols": draw_tile_cols(jax.random.fold_in(key_of[9], 71), part),
        "send_rows": draw_send_rows(jax.random.fold_in(key_of[9], 71), part),
        "send_count": draw_send_count(jax.random.fold_in(key_of[9], 71), part),
    }


OFFSETS = (1, -1, 2, -2)
time_step = 0.5
spread_u = 1.0
spread_v = 0.5


def laplace_part(flat, part_index, tiles, tile_cols, send_rows, send_count):
    channels = flat.shape[0]
    own = lax.dynamic_slice_in_dim(flat, part_index * CELLS_DEV, CELLS_DEV, 1)
    pieces = [own]
    for slot, offset in enumerate(OFFSETS):
        source = ((part_index - offset) % N_DOM).astype(jnp.int32)
        rows = lax.dynamic_index_in_dim(send_rows, source, 0, keepdims=False)[slot]
        count = lax.dynamic_index_in_dim(send_count, source, 0, keepdims=False)[slot]
        block = lax.dynamic_slice_in_dim(flat, source * CELLS_DEV, CELLS_DEV, 1)
        values = jnp.take(block, rows, axis=1)
        live = jnp.arange(ROWS_SEND) < count
        pieces.append(jnp.where(live[None, :], values, jnp.zeros_like(values)))
    extended = jnp.concatenate(pieces, axis=1).reshape(channels, NB + 4 * HB, 128)
    tile_block = lax.dynamic_slice_in_dim(tiles, part_index * NB, NB, 0)
    col_block = lax.dynamic_slice_in_dim(tile_cols, part_index * NB, NB, 0)
    chosen = extended[:, col_block]
    result = jnp.einsum("rkij,crkj->cri", tile_block, chosen, precision=lax.Precision.HIGHEST)
    return result.reshape(channels, CELLS_DEV)


def tendency(stacked, lap, feed, kill):
    conc_u = stacked[:, 0]
    conc_v = stacked[:, 1]
    square_v = conc_v * conc_v
    product_uv = conc_u * square_v
    outs = [spread_u * lap[:, 0] - product_uv + feed * (1.0 - conc_u),
            spread_v * lap[:, 1] + product_uv - (feed + kill) * conc_v]
    for first in (2, 4):
        delta_u = stacked[:, first]
        delta_v = stacked[:, first + 1]
        react = square_v * delta_u + 2.0 * conc_u * conc_v * delta_v
        outs.append(spread_u * lap[:, first] - react - feed * delta_u)
        outs.append(spread_v * lap[:, first + 1] + react - (feed + kill) * delta_v)
    return jnp.stack(outs, axis=1)


def reference(state, dir_one, dir_two, feed, kill, tiles, tile_cols, send_rows, send_count):
    stacked = jnp.concatenate([state, dir_one, dir_two], axis=1)
    flat = stacked.reshape(NT * 6, NCELLS)

    def one_part(part_index):
        return laplace_part(flat, part_index, tiles, tile_cols, send_rows, send_count)

    parts = lax.map(one_part, jnp.arange(N_DOM, dtype=jnp.int32))
    lap = jnp.transpose(parts, (1, 0, 2)).reshape(NT, 6, NCELLS)
    rates = tendency(stacked, lap, feed, kill)
    earlier = jnp.roll(stacked, 1, axis=0)
    rate_earlier = jnp.roll(rates, 1, axis=0)
    out = (stacked - earlier) / time_step - 0.5 * (rates + rate_earlier)
    return out[:, 0:2], out[:, 2:4], out[:, 4:6]
```

```python
import functools

import jax
import jax.numpy as jnp
from jax import lax
from jax.experimental import pallas as pl
from jax.experimental.pallas import tpu as pltpu
from jax.sharding import PartitionSpec as P

OFFSETS = (1, -1, 2, -2)
time_step = 0.5
spread_u = 1.0
spread_v = 0.5
LANES = 128
STEPS = 8
FIELDS = 3
CHUNKS = ((1, 2), (0,))
VMEM = pltpu.VMEM
SMEM = pltpu.SMEM
F32 = jnp.float32
BF16 = jnp.bfloat16


def shift_along(block, axis, distance):
    size = lax.axis_size(axis)
    return lax.ppermute(block, axis, [((i - distance) % size, i) for i in range(size)])


def steps_at(ref, group, cell_block, species, stride):
    return ref[pl.ds(group * STEPS * stride + cell_block * 2 + species, STEPS, stride=stride), :]


def steps_before(ref, prev_ref, field, group, cell_block, species, stride):
    offset = cell_block * 2 + species
    if group > 0:
        return ref[pl.ds((group * STEPS - 1) * stride + offset, STEPS, stride=stride), :]
    now = steps_at(ref, 0, cell_block, species, stride)
    row = field * stride + offset
    first = jnp.broadcast_to(prev_ref[row : row + 1, :], now.shape)
    index = lax.broadcasted_iota(jnp.int32, now.shape, 0)
    return jnp.where(index == 0, first, pltpu.roll(now, 1, 0))


def split(values):
    high = values.astype(BF16)
    return high, (values - high.astype(F32)).astype(BF16)


def gather_kernel(chunk, slot_groups, cell_blocks, *refs):
    refs = list(refs)
    fields = [refs.pop(0) for _ in range(FIELDS)]
    prev = refs.pop(0) if 0 in chunk else None
    rows_ref, count_ref = refs.pop(0), refs.pop(0)
    sends = [refs.pop(0) for _ in slot_groups]
    parts_ref = refs.pop(0)
    last = None if 0 in chunk else refs.pop(0)
    (choose,) = refs
    stride = 2 * cell_blocks
    size = len(chunk) * FIELDS * 2 * STEPS
    if last is not None:
        for field in range(FIELDS):
            last[field * stride : (field + 1) * stride, :] = fields[field][-stride:, :]
    for place, group in enumerate(chunk):
        for field in range(FIELDS):
            row = (place * FIELDS + field) * 2 * STEPS
            for block in range(cell_blocks):
                both = []
                for species, scale in enumerate((-0.5 * spread_u, -0.5 * spread_v)):
                    now = steps_at(fields[field], group, block, species, stride)
                    before = steps_before(fields[field], prev, field, group, block, species, stride)
                    both.append((now + before) * scale)
                high, low = split(jnp.concatenate(both, axis=0))
                parts_ref[block, row : row + 2 * STEPS, :] = high
                parts_ref[block, size + row : size + row + 2 * STEPS, :] = low
    slot_rows = rows_ref.shape[1]
    parts = jnp.concatenate([parts_ref[b] for b in range(cell_blocks)], axis=1)
    lane = lax.broadcasted_iota(jnp.int32, (1, slot_rows), 1)
    cell = lax.broadcasted_iota(jnp.int32, (LANES, slot_rows), 0)
    for send, slots in zip(sends, slot_groups):
        for place, slot in enumerate(slots):
            listed = jnp.where(lane < count_ref[slot], rows_ref[slot : slot + 1, :], -1)
            for block in range(cell_blocks):
                hit = cell == listed - block * LANES
                choose[block * LANES : (block + 1) * LANES, :] = jnp.where(hit, 1.0, 0.0).astype(BF16)
            taken = jnp.dot(parts, choose[...], preferred_element_type=F32)
            send[:, place * slot_rows : (place + 1) * slot_rows] = taken[:size] + taken[size:]


def pointwise(u, v, du, dv, ddu, ddv, feed, total):
    square = v * v
    product = u * square
    twice = 2.0 * u * v
    outs = [feed * (1.0 - u) - product, product - total * v]
    for first, second in ((du, dv), (ddu, ddv)):
        react = square * first + twice * second
        outs += [-react - feed * first, react - total * second]
    return outs


def local_kernel(chunks, cell_blocks, *refs):
    refs = list(refs)
    fields = [refs.pop(0) for _ in range(FIELDS)]
    prev, feed_ref, kill_ref, tiles = [refs.pop(0) for _ in range(4)]
    bases = [refs.pop(0) for _ in chunks]
    (split_tiles,) = refs
    stride = 2 * cell_blocks
    for base, chunk in zip(bases, chunks):
        for place, group in enumerate(chunk):
            for block in range(cell_blocks):
                feed = feed_ref[block : block + 1, :]
                total = feed + kill_ref[block : block + 1, :]
                now = [steps_at(fields[f], group, block, s, stride) for f in range(FIELDS) for s in range(2)]
                before = [
                    steps_before(fields[f], prev, f, group, block, s, stride)
                    for f in range(FIELDS)
                    for s in range(2)
                ]
                rate_now = pointwise(*now, feed, total)
                rate_before = pointwise(*before, feed, total)
                for index in range(2 * FIELDS):
                    row = (place * FIELDS * 2 + index) * STEPS
                    base[block, row : row + STEPS, :] = (now[index] - before[index]) * (1.0 / time_step) - 0.5 * (
                        rate_now[index] + rate_before[index]
                    )
    blocks, per_row = tiles.shape[:2]
    for block in range(blocks):
        for k in range(per_row):
            high, low = split(jnp.transpose(tiles[block, k]))
            split_tiles[block, k * LANES : (k + 1) * LANES, :LANES] = high
            split_tiles[block, k * LANES : (k + 1) * LANES, LANES:] = low


def apply_kernel(chunk, slot_groups, cell_blocks, blocks, per_row, first, *refs):
    refs = list(refs)
    cols, split_tiles, base, parts_ref = [refs.pop(0) for _ in range(4)]
    arrived = [refs.pop(0) for _ in slot_groups]
    if not first:
        refs = refs[FIELDS:]
    outs = [refs.pop(0) for _ in range(FIELDS)]
    extended, made, sems = refs
    stride = 2 * cell_blocks
    size = base.shape[1]
    extended[:cell_blocks] = parts_ref[...]
    for ref, slots in zip(arrived, slot_groups):
        per_slot = ref.shape[1] // len(slots) // LANES
        for place, slot in enumerate(slots):
            for b in range(per_slot):
                lane = (place * per_slot + b) * LANES
                high, low = split(ref[:, lane : lane + LANES])
                extended[cell_blocks + slot * per_slot + b, :size, :] = high
                extended[cell_blocks + slot * per_slot + b, size:, :] = low
    for block in range(blocks):
        chosen = jnp.concatenate([extended[cols[k, block]] for k in range(per_row)], axis=1)
        product = jnp.dot(chosen, split_tiles[block], preferred_element_type=F32)
        product = product[:, :LANES] + product[:, LANES:]
        result = base[block] + (product[:size] + product[size:])
        for place in range(len(chunk)):
            for index in range(2 * FIELDS):
                row = (place * FIELDS * 2 + index) * STEPS
                at = place * STEPS * stride + block * 2 + index % 2
                made[index // 2, pl.ds(at, STEPS, stride=stride), :] = result[row : row + STEPS, :]
    span = len(chunk) * STEPS * stride
    copies = [
        pltpu.make_async_copy(made.at[f], outs[f].at[pl.ds(chunk[0] * STEPS * stride, span), :], sems.at[f])
        for f in range(FIELDS)
    ]
    for copy in copies:
        copy.start()
    for copy in copies:
        copy.wait()


def per_device(state, dir_one, dir_two, feed, kill, tiles, tile_cols, send_rows, send_count):
    steps, _, cells = state.shape
    cell_blocks = cells // LANES
    stride = 2 * cell_blocks
    blocks, per_row = tiles.shape[:2]
    slot_rows = send_rows.shape[2]
    size_dom = lax.axis_size("dom")

    by_route = {}
    for slot, offset in enumerate(OFFSETS):
        by_route.setdefault(offset % size_dom, []).append(slot)
    slot_groups = sorted(by_route.values(), key=lambda slots: -len(slots))

    def view(array):
        array = array.reshape(steps, 2, cell_blocks, LANES).transpose(0, 2, 1, 3)
        return array.reshape(steps * stride, LANES)

    def unview(array):
        array = array.reshape(steps, cell_blocks, 2, LANES).transpose(0, 2, 1, 3)
        return array.reshape(steps, 2, cells)

    fields = [view(state), view(dir_one), view(dir_two)]
    rows = send_rows.reshape(send_rows.shape[1:])
    counts = send_count.reshape(send_count.shape[1:])
    cols = tile_cols.T
    feed = feed.reshape(cell_blocks, LANES)
    kill = kill.reshape(cell_blocks, LANES)

    vmem = pl.BlockSpec(memory_space=VMEM)
    smem = pl.BlockSpec(memory_space=SMEM)
    anywhere = pl.BlockSpec(memory_space=pl.ANY)
    params = pltpu.CompilerParams(vmem_limit_bytes=16 * 1024 * 1024)

    prev = None
    parts, arrived = [], []
    for chunk in CHUNKS:
        size = len(chunk) * FIELDS * 2 * STEPS
        widths = [len(slots) * slot_rows for slots in slot_groups]
        shapes = [jax.ShapeDtypeStruct((size, width), F32) for width in widths]
        shapes.append(jax.ShapeDtypeStruct((cell_blocks, 2 * size, LANES), BF16))
        inputs = list(fields)
        if 0 in chunk:
            inputs.append(prev)
        else:
            shapes.append(jax.ShapeDtypeStruct((FIELDS * stride, LANES), F32))
        results = pl.pallas_call(
            functools.partial(gather_kernel, chunk, slot_groups, cell_blocks),
            out_shape=shapes,
            in_specs=[vmem] * len(inputs) + [vmem, smem],
            out_specs=[vmem] * len(shapes),
            scratch_shapes=[VMEM((cells, slot_rows), BF16)],
            compiler_params=params,
            cost_estimate=pl.CostEstimate(
                flops=4 * size * cells * sum(widths), bytes_accessed=4 * size * (cells + sum(widths)), transcendentals=0
            ),
            name="gather_rows",
        )(*inputs, rows, counts)
        if 0 not in chunk and prev is None:
            prev = shift_along(results[-1], "tm", 1)
        arrived.append(
            [shift_along(send, "dom", OFFSETS[slots[0]]) for send, slots in zip(results, slot_groups)]
        )
        parts.append(results[len(slot_groups)])

    *bases, split_tiles = pl.pallas_call(
        functools.partial(local_kernel, CHUNKS, cell_blocks),
        out_shape=[jax.ShapeDtypeStruct((cell_blocks, p.shape[1] // 2, LANES), F32) for p in parts]
        + [jax.ShapeDtypeStruct((blocks, per_row * LANES, 2 * LANES), BF16)],
        in_specs=[vmem] * 7,
        out_specs=[vmem] * (len(parts) + 1),
        compiler_params=params,
        cost_estimate=pl.CostEstimate(flops=60 * steps * 6 * cells, bytes_accessed=4 * tiles.size, transcendentals=0),
        name="local_terms",
    )(*fields, prev, feed, kill, tiles)

    outs = []
    for number, chunk in enumerate(CHUNKS):
        size = len(chunk) * FIELDS * 2 * STEPS
        inputs = [cols, split_tiles, bases[number], parts[number], *arrived[number]]
        specs = [smem] + [vmem] * (len(inputs) - 1)
        aliases = {len(inputs) + f: f for f in range(FIELDS)} if outs else {}
        outs = pl.pallas_call(
            functools.partial(apply_kernel, chunk, slot_groups, cell_blocks, blocks, per_row, not outs),
            out_shape=[jax.ShapeDtypeStruct((steps * stride, LANES), F32)] * FIELDS,
            in_specs=specs + [anywhere] * len(outs),
            out_specs=[anywhere] * FIELDS,
            input_output_aliases=aliases,
            scratch_shapes=[
                VMEM((cell_blocks + len(OFFSETS) * slot_rows // LANES, 2 * size, LANES), BF16),
                VMEM((FIELDS, len(chunk) * STEPS * stride, LANES), F32),
                pltpu.SemaphoreType.DMA((FIELDS,)),
            ],
            compiler_params=params,
            cost_estimate=pl.CostEstimate(
                flops=8 * size * blocks * per_row * LANES * LANES, bytes_accessed=8 * size * cells, transcendentals=0
            ),
            name="apply_tiles",
        )(*inputs, *outs)
    return tuple(unview(out) for out in outs)


def solution(mesh):
    fields = P(("group", "tm"), None, "dom")
    in_specs = (
        fields,
        fields,
        fields,
        P("dom"),
        P("dom"),
        P("dom", None, None, None),
        P("dom", None),
        P("dom", None, None),
        P("dom", None),
    )
    return jax.shard_map(
        per_device, mesh=mesh, in_specs=in_specs, out_specs=(fields, fields, fields), check_vma=False
    )
```

```python
import functools

import jax
import jax.numpy as jnp
from jax import lax
from jax.experimental import pallas as pl
from jax.experimental.pallas import tpu as pltpu
from jax.sharding import PartitionSpec as P

OFFSETS = (1, -1, 2, -2)
time_step = 0.5
spread_u = 1.0
spread_v = 0.5
LANES = 128
STEPS = 8
FIELDS = 3
CHUNKS = ((1, 2), (0,))
VMEM = pltpu.VMEM
SMEM = pltpu.SMEM
F32 = jnp.float32
BF16 = jnp.bfloat16


def shift_along(block, axis, distance):
    size = lax.axis_size(axis)
    return lax.ppermute(block, axis, [((i - distance) % size, i) for i in range(size)])


def steps_at(ref, group, cell_block, species, stride):
    return ref[pl.ds(group * STEPS * stride + cell_block * 2 + species, STEPS, stride=stride), :]


def steps_before(ref, prev_ref, field, group, cell_block, species, stride):
    offset = cell_block * 2 + species
    if group > 0:
        return ref[pl.ds((group * STEPS - 1) * stride + offset, STEPS, stride=stride), :]
    now = steps_at(ref, 0, cell_block, species, stride)
    row = field * stride + offset
    first = jnp.broadcast_to(prev_ref[row : row + 1, :], now.shape)
    index = lax.broadcasted_iota(jnp.int32, now.shape, 0)
    return jnp.where(index == 0, first, pltpu.roll(now, 1, 0))


def split(values):
    high = values.astype(BF16)
    return high, (values - high.astype(F32)).astype(BF16)


def summed_parts(chunk, cell_blocks, field_at, prev, parts_ref):
    stride = 2 * cell_blocks
    size = parts_ref.shape[1] // 2
    for place, group in enumerate(chunk):
        for field in range(FIELDS):
            row = (place * FIELDS + field) * 2 * STEPS
            for block in range(cell_blocks):
                both = []
                for species, scale in enumerate((-0.5 * spread_u, -0.5 * spread_v)):
                    now = steps_at(field_at[field], group, block, species, stride)
                    before = steps_before(field_at[field], prev, field, group, block, species, stride)
                    both.append((now + before) * scale)
                high, low = split(jnp.concatenate(both, axis=0))
                parts_ref[block, row : row + 2 * STEPS, :] = high
                parts_ref[block, size + row : size + row + 2 * STEPS, :] = low


def choose_rows(slots, listed_ref, choose):
    cells = choose.shape[0]
    slot_rows = listed_ref.shape[1]
    cell = lax.broadcasted_iota(jnp.int32, (LANES, slot_rows), 0)
    for place, slot in enumerate(slots):
        listed = listed_ref[slot : slot + 1, :]
        for start in range(0, cells, LANES):
            hit = cell == listed - start
            choose[start : start + LANES, place * slot_rows : (place + 1) * slot_rows] = jnp.where(
                hit, 1.0, 0.0
            ).astype(BF16)


def take_rows(parts_ref, choose, sends):
    size = parts_ref.shape[1] // 2
    parts = jnp.concatenate([parts_ref[b] for b in range(parts_ref.shape[0])], axis=1)
    start = 0
    for send in sends:
        width = send.shape[1]
        taken = jnp.dot(parts, choose[:, start : start + width], preferred_element_type=F32)
        send[...] = taken[:size] + taken[size:]
        start += width


def first_kernel(chunk, slots, cell_blocks, *refs):
    refs = list(refs)
    sources = [refs.pop(0) for _ in range(FIELDS)]
    rows_hbm, count_hbm, send, parts_ref, held, listed, last, choose, rows_ref, count_ref, sems = refs
    stride = 2 * cell_blocks
    early = (chunk[0] * STEPS - 1) * stride
    late = held.shape[1] - early
    small = [
        pltpu.make_async_copy(rows_hbm, rows_ref, sems.at[2 * FIELDS]),
        pltpu.make_async_copy(count_hbm, count_ref, sems.at[2 * FIELDS + 1]),
    ]
    needed = [
        pltpu.make_async_copy(sources[f].at[pl.ds(early, late), :], held.at[f, pl.ds(early, late), :], sems.at[f])
        for f in range(FIELDS)
    ]
    others = [
        pltpu.make_async_copy(sources[f].at[pl.ds(0, early), :], held.at[f, pl.ds(0, early), :], sems.at[FIELDS + f])
        for f in range(FIELDS)
    ]
    for copy in small + needed + others:
        copy.start()
    for copy in small:
        copy.wait()
    lane = lax.broadcasted_iota(jnp.int32, rows_ref.shape, 1)
    for slot in range(rows_ref.shape[0]):
        listed[slot : slot + 1, :] = jnp.where(
            lane[slot : slot + 1] < count_ref[:, slot : slot + 1], rows_ref[slot : slot + 1, :], -1
        )
    choose_rows(slots, listed, choose)
    for copy in needed:
        copy.wait()
    summed_parts(chunk, cell_blocks, [held.at[f] for f in range(FIELDS)], None, parts_ref)
    take_rows(parts_ref, choose, [send])
    for field in range(FIELDS):
        last[field * stride : (field + 1) * stride, :] = held[field, -stride:, :]
    for copy in others:
        copy.wait()


def rest_kernel(slots, parts_ref, listed, *refs):
    *sends, choose = refs
    choose_rows(slots, listed, choose)
    take_rows(parts_ref, choose, sends)


def gather_kernel(chunk, slots, cell_blocks, held, prev, listed, *refs):
    *sends, parts_ref, choose = refs
    choose_rows(slots, listed, choose)
    summed_parts(chunk, cell_blocks, [held.at[f] for f in range(FIELDS)], prev, parts_ref)
    take_rows(parts_ref, choose, sends)


def pointwise(u, v, du, dv, ddu, ddv, feed, total):
    square = v * v
    product = u * square
    twice = 2.0 * u * v
    outs = [feed * (1.0 - u) - product, product - total * v]
    for first, second in ((du, dv), (ddu, ddv)):
        react = square * first + twice * second
        outs += [-react - feed * first, react - total * second]
    return outs


def local_kernel(chunks, cell_blocks, *refs):
    refs = list(refs)
    held, prev, feed_ref, kill_ref, tiles = [refs.pop(0) for _ in range(5)]
    fields = [held.at[f] for f in range(FIELDS)]
    bases = [refs.pop(0) for _ in chunks]
    (split_tiles,) = refs
    stride = 2 * cell_blocks
    for base, chunk in zip(bases, chunks):
        for place, group in enumerate(chunk):
            for block in range(cell_blocks):
                feed = feed_ref[block : block + 1, :]
                total = feed + kill_ref[block : block + 1, :]
                now = [steps_at(fields[f], group, block, s, stride) for f in range(FIELDS) for s in range(2)]
                before = [
                    steps_before(fields[f], prev, f, group, block, s, stride)
                    for f in range(FIELDS)
                    for s in range(2)
                ]
                rate_now = pointwise(*now, feed, total)
                rate_before = pointwise(*before, feed, total)
                for index in range(2 * FIELDS):
                    row = (place * FIELDS * 2 + index) * STEPS
                    base[block, row : row + STEPS, :] = (now[index] - before[index]) * (1.0 / time_step) - 0.5 * (
                        rate_now[index] + rate_before[index]
                    )
    blocks, per_row = tiles.shape[:2]
    for block in range(blocks):
        for k in range(per_row):
            high, low = split(jnp.transpose(tiles[block, k]))
            split_tiles[block, k * LANES : (k + 1) * LANES, :LANES] = high
            split_tiles[block, k * LANES : (k + 1) * LANES, LANES:] = low


def apply_kernel(chunk, slot_groups, cell_blocks, blocks, per_row, first, *refs):
    refs = list(refs)
    cols, split_tiles, base, parts_ref = [refs.pop(0) for _ in range(4)]
    arrived = [refs.pop(0) for _ in slot_groups]
    if not first:
        refs = refs[FIELDS:]
    outs = [refs.pop(0) for _ in range(FIELDS)]
    extended, made, sems = refs
    stride = 2 * cell_blocks
    size = base.shape[1]
    extended[:cell_blocks] = parts_ref[...]
    for ref, slots in zip(arrived, slot_groups):
        per_slot = ref.shape[1] // len(slots) // LANES
        for place, slot in enumerate(slots):
            for b in range(per_slot):
                lane = (place * per_slot + b) * LANES
                high, low = split(ref[:, lane : lane + LANES])
                extended[cell_blocks + slot * per_slot + b, :size, :] = high
                extended[cell_blocks + slot * per_slot + b, size:, :] = low
    for block in range(blocks):
        chosen = jnp.concatenate([extended[cols[k, block]] for k in range(per_row)], axis=1)
        product = jnp.dot(chosen, split_tiles[block], preferred_element_type=F32)
        product = product[:, :LANES] + product[:, LANES:]
        result = base[block] + (product[:size] + product[size:])
        for place in range(len(chunk)):
            for index in range(2 * FIELDS):
                row = (place * FIELDS * 2 + index) * STEPS
                at = place * STEPS * stride + block * 2 + index % 2
                made[index // 2, pl.ds(at, STEPS, stride=stride), :] = result[row : row + STEPS, :]
    span = len(chunk) * STEPS * stride
    copies = [
        pltpu.make_async_copy(made.at[f], outs[f].at[pl.ds(chunk[0] * STEPS * stride, span), :], sems.at[f])
        for f in range(FIELDS)
    ]
    for copy in copies:
        copy.start()
    for copy in copies:
        copy.wait()


def per_device(state, dir_one, dir_two, feed, kill, tiles, tile_cols, send_rows, send_count):
    steps, _, cells = state.shape
    cell_blocks = cells // LANES
    stride = 2 * cell_blocks
    blocks, per_row = tiles.shape[:2]
    slot_rows = send_rows.shape[2]
    size_dom = lax.axis_size("dom")

    by_route = {}
    for slot, offset in enumerate(OFFSETS):
        by_route.setdefault(offset % size_dom, []).append(slot)
    slot_groups = sorted(by_route.values(), key=lambda slots: -len(slots))

    def view(array):
        array = array.reshape(steps, 2, cell_blocks, LANES).transpose(0, 2, 1, 3)
        return array.reshape(steps * stride, LANES)

    def unview(array):
        array = array.reshape(steps, cell_blocks, 2, LANES).transpose(0, 2, 1, 3)
        return array.reshape(steps, 2, cells)

    fields = [view(state), view(dir_one), view(dir_two)]
    rows = send_rows.reshape(send_rows.shape[1:])
    counts = send_count
    cols = tile_cols.T
    feed = feed.reshape(cell_blocks, LANES)
    kill = kill.reshape(cell_blocks, LANES)

    vmem = pl.BlockSpec(memory_space=VMEM)
    smem = pl.BlockSpec(memory_space=SMEM)
    anywhere = pl.BlockSpec(memory_space=pl.ANY)
    params = pltpu.CompilerParams(vmem_limit_bytes=16 * 1024 * 1024)

    def rows_of(chunk):
        return len(chunk) * FIELDS * 2 * STEPS

    def f32(*shape):
        return jax.ShapeDtypeStruct(shape, F32)

    def parts_of(chunk):
        return jax.ShapeDtypeStruct((cell_blocks, 2 * rows_of(chunk), LANES), BF16)

    def gather_cost(chunk, slots):
        width = len(slots) * slot_rows
        size = rows_of(chunk)
        return pl.CostEstimate(
            flops=4 * size * cells * width, bytes_accessed=4 * size * (cells + width), transcendentals=0
        )

    def send_all(sends, groups):
        return [shift_along(send, "dom", OFFSETS[slots[0]]) for send, slots in zip(sends, groups)]

    hbm = pl.BlockSpec(memory_space=pltpu.HBM)
    lead, later = CHUNKS
    wide, *narrow = slot_groups
    others = [slot for slots in narrow for slot in slots]
    every = wide + others
    send, lead_parts, held, listed, last = pl.pallas_call(
        functools.partial(first_kernel, lead, wide, cell_blocks),
        out_shape=[
            f32(rows_of(lead), len(wide) * slot_rows),
            parts_of(lead),
            f32(FIELDS, steps * stride, LANES),
            jax.ShapeDtypeStruct(rows.shape, jnp.int32),
            f32(FIELDS * stride, LANES),
        ],
        in_specs=[hbm] * (FIELDS + 2),
        out_specs=[vmem] * 5,
        scratch_shapes=[
            VMEM((cells, len(wide) * slot_rows), BF16),
            VMEM(rows.shape, jnp.int32),
            VMEM(counts.shape, jnp.int32),
            pltpu.SemaphoreType.DMA((2 * FIELDS + 2,)),
        ],
        compiler_params=params,
        cost_estimate=gather_cost(lead, wide),
        name="gather_first",
    )(*[pltpu.with_memory_space_constraint(x, pltpu.HBM) for x in (*fields, rows, counts)])
    lead_arrived = send_all([send], [wide])
    prev = shift_along(last, "tm", 1)
    sends = pl.pallas_call(
        functools.partial(rest_kernel, others),
        out_shape=[f32(rows_of(lead), len(slots) * slot_rows) for slots in narrow],
        in_specs=[vmem] * 2,
        out_specs=[vmem] * len(narrow),
        scratch_shapes=[VMEM((cells, len(others) * slot_rows), BF16)],
        compiler_params=params,
        cost_estimate=gather_cost(lead, others),
        name="gather_rest",
    )(lead_parts, listed)
    lead_arrived += send_all(sends, narrow)
    *sends, later_parts = pl.pallas_call(
        functools.partial(gather_kernel, later, every, cell_blocks),
        out_shape=[f32(rows_of(later), len(slots) * slot_rows) for slots in slot_groups] + [parts_of(later)],
        in_specs=[vmem] * 3,
        out_specs=[vmem] * (len(slot_groups) + 1),
        scratch_shapes=[VMEM((cells, len(every) * slot_rows), BF16)],
        compiler_params=params,
        cost_estimate=gather_cost(later, every),
        name="gather_later",
    )(held, prev, listed)
    later_arrived = send_all(sends, slot_groups)
    arrived = [lead_arrived, later_arrived]
    parts = [lead_parts, later_parts]

    *bases, split_tiles = pl.pallas_call(
        functools.partial(local_kernel, CHUNKS, cell_blocks),
        out_shape=[jax.ShapeDtypeStruct((cell_blocks, p.shape[1] // 2, LANES), F32) for p in parts]
        + [jax.ShapeDtypeStruct((blocks, per_row * LANES, 2 * LANES), BF16)],
        in_specs=[vmem] * 5,
        out_specs=[vmem] * (len(parts) + 1),
        compiler_params=params,
        cost_estimate=pl.CostEstimate(flops=60 * steps * 6 * cells, bytes_accessed=4 * tiles.size, transcendentals=0),
        name="local_terms",
    )(held, prev, feed, kill, tiles)

    outs = []
    for number, chunk in enumerate(CHUNKS):
        size = len(chunk) * FIELDS * 2 * STEPS
        inputs = [cols, split_tiles, bases[number], parts[number], *arrived[number]]
        specs = [smem] + [vmem] * (len(inputs) - 1)
        aliases = {len(inputs) + f: f for f in range(FIELDS)} if outs else {}
        outs = pl.pallas_call(
            functools.partial(apply_kernel, chunk, slot_groups, cell_blocks, blocks, per_row, not outs),
            out_shape=[jax.ShapeDtypeStruct((steps * stride, LANES), F32)] * FIELDS,
            in_specs=specs + [anywhere] * len(outs),
            out_specs=[anywhere] * FIELDS,
            input_output_aliases=aliases,
            scratch_shapes=[
                VMEM((cell_blocks + len(OFFSETS) * slot_rows // LANES, 2 * size, LANES), BF16),
                VMEM((FIELDS, len(chunk) * STEPS * stride, LANES), F32),
                pltpu.SemaphoreType.DMA((FIELDS,)),
            ],
            compiler_params=params,
            cost_estimate=pl.CostEstimate(
                flops=8 * size * blocks * per_row * LANES * LANES, bytes_accessed=8 * size * cells, transcendentals=0
            ),
            name="apply_tiles",
        )(*inputs, *outs)
    return tuple(unview(out) for out in outs)


def solution(mesh):
    fields = P(("group", "tm"), None, "dom")
    in_specs = (
        fields,
        fields,
        fields,
        P("dom"),
        P("dom"),
        P("dom", None, None, None),
        P("dom", None),
        P("dom", None, None),
        P("dom", None),
    )
    return jax.shard_map(
        per_device, mesh=mesh, in_specs=in_specs, out_specs=(fields, fields, fields), check_vma=False
    )
```

```python
import functools

import jax
import jax.numpy as jnp
from jax import lax
from jax.experimental import pallas as pl
from jax.experimental.pallas import tpu as pltpu
from jax.sharding import PartitionSpec as P

OFFSETS = (1, -1, 2, -2)
time_step = 0.5
spread_u = 1.0
spread_v = 0.5
LANES = 128
STEPS = 8
FIELDS = 3
VMEM = pltpu.VMEM
SMEM = pltpu.SMEM
F32 = jnp.float32
BF16 = jnp.bfloat16


def shift_along(block, axis, distance):
    size = lax.axis_size(axis)
    return lax.ppermute(block, axis, [((i - distance) % size, i) for i in range(size)])


def steps_at(ref, group, cell_block, species, stride):
    return ref[pl.ds(group * STEPS * stride + cell_block * 2 + species, STEPS, stride=stride), :]


def steps_before(ref, prev_ref, field, group, cell_block, species, stride):
    offset = cell_block * 2 + species
    if group > 0:
        return ref[pl.ds((group * STEPS - 1) * stride + offset, STEPS, stride=stride), :]
    now = steps_at(ref, 0, cell_block, species, stride)
    row = field * stride + offset
    first = jnp.broadcast_to(prev_ref[row : row + 1, :], now.shape)
    index = lax.broadcasted_iota(jnp.int32, now.shape, 0)
    return jnp.where(index == 0, first, pltpu.roll(now, 1, 0))


def split(values):
    high = values.astype(BF16)
    return high, (values - high.astype(F32)).astype(BF16)


def summed_parts(groups, cell_blocks, fields, prev, parts_ref, high_row, low_row):
    stride = 2 * cell_blocks
    for place, group in enumerate(groups):
        for field in range(FIELDS):
            row = (place * FIELDS + field) * 2 * STEPS
            for block in range(cell_blocks):
                both = []
                for species, scale in enumerate((-0.5 * spread_u, -0.5 * spread_v)):
                    now = steps_at(fields[field], group, block, species, stride)
                    before = steps_before(fields[field], prev, field, group, block, species, stride)
                    both.append((now + before) * scale)
                high, low = split(jnp.concatenate(both, axis=0))
                parts_ref[block, high_row + row : high_row + row + 2 * STEPS, :] = high
                parts_ref[block, low_row + row : low_row + row + 2 * STEPS, :] = low


def choose_rows(slots, listed_ref, choose):
    cells = choose.shape[0]
    slot_rows = listed_ref.shape[1]
    cell = lax.broadcasted_iota(jnp.int32, (LANES, slot_rows), 0)
    for place, slot in enumerate(slots):
        listed = listed_ref[slot : slot + 1, :]
        for start in range(0, cells, LANES):
            hit = cell == listed - start
            choose[start : start + LANES, place * slot_rows : (place + 1) * slot_rows] = jnp.where(
                hit, 1.0, 0.0
            ).astype(BF16)


def take_rows(parts, choose, sends):
    size = parts.shape[0] // 2
    start = 0
    for send in sends:
        width = send.shape[1]
        taken = jnp.dot(parts, choose[:, start : start + width], preferred_element_type=F32)
        send[...] = taken[:size] + taken[size:]
        start += width


def side_by_side(parts_ref, rows):
    blocks = [
        jnp.concatenate([parts_ref[b, start : start + count, :] for start, count in rows], axis=0)
        for b in range(parts_ref.shape[0])
    ]
    return jnp.concatenate(blocks, axis=1)


def first_kernel(lead, slots, cell_blocks, *refs):
    refs = list(refs)
    sources = [refs.pop(0) for _ in range(FIELDS)]
    rows_hbm, count_hbm, send, parts_ref, held, listed, last, choose, rows_ref, count_ref, sems = refs
    stride = 2 * cell_blocks
    early = (lead[0] * STEPS - 1) * stride
    late = held.shape[1] - early
    small = [
        pltpu.make_async_copy(rows_hbm, rows_ref, sems.at[2 * FIELDS]),
        pltpu.make_async_copy(count_hbm, count_ref, sems.at[2 * FIELDS + 1]),
    ]
    needed = [
        pltpu.make_async_copy(sources[f].at[pl.ds(early, late), :], held.at[f, pl.ds(early, late), :], sems.at[f])
        for f in range(FIELDS)
    ]
    others = [
        pltpu.make_async_copy(sources[f].at[pl.ds(0, early), :], held.at[f, pl.ds(0, early), :], sems.at[FIELDS + f])
        for f in range(FIELDS)
    ]
    for copy in small + needed + others:
        copy.start()
    for copy in small:
        copy.wait()
    lane = lax.broadcasted_iota(jnp.int32, rows_ref.shape, 1)
    for slot in range(rows_ref.shape[0]):
        listed[slot : slot + 1, :] = jnp.where(
            lane[slot : slot + 1] < count_ref[:, slot : slot + 1], rows_ref[slot : slot + 1, :], -1
        )
    choose_rows(slots, listed, choose)
    for copy in needed:
        copy.wait()
    size = parts_ref.shape[1] // 2
    summed_parts(lead, cell_blocks, [held.at[f] for f in range(FIELDS)], None, parts_ref, 0, size)
    take_rows(side_by_side(parts_ref, [(0, 2 * size)]), choose, [send])
    for field in range(FIELDS):
        last[field * stride : (field + 1) * stride, :] = held[field, -stride:, :]
    for copy in others:
        copy.wait()


def rest_kernel(late, wide, others, cell_blocks, held, prev, listed, lead_parts, send, *refs):
    *sends, parts_ref, choose = refs
    size = parts_ref.shape[1] // 2
    lead_size = lead_parts.shape[1] // 2
    late_size = size - lead_size
    choose_rows(others + wide, listed, choose)
    parts_ref[:, late_size:size, :] = lead_parts[:, :lead_size, :]
    parts_ref[:, size + late_size :, :] = lead_parts[:, lead_size:, :]
    summed_parts(late, cell_blocks, [held.at[f] for f in range(FIELDS)], prev, parts_ref, 0, size)
    take_rows(side_by_side(parts_ref, [(0, 2 * size)]), choose, sends)
    narrow_width = choose.shape[1] - send.shape[1]
    late_parts = side_by_side(parts_ref, [(0, late_size), (size, late_size)])
    take_rows(late_parts, choose.at[:, narrow_width:], [send])


def pointwise(u, v, du, dv, ddu, ddv, feed, total):
    square = v * v
    product = u * square
    twice = 2.0 * u * v
    outs = [feed * (1.0 - u) - product, product - total * v]
    for first, second in ((du, dv), (ddu, ddv)):
        react = square * first + twice * second
        outs += [-react - feed * first, react - total * second]
    return outs


def local_kernel(groups, cell_blocks, held, prev, feed_ref, kill_ref, tiles, base, split_tiles):
    fields = [held.at[f] for f in range(FIELDS)]
    stride = 2 * cell_blocks
    pairs = [(f, s) for f in range(FIELDS) for s in range(2)]
    for place, group in enumerate(groups):
        for block in range(cell_blocks):
            feed = feed_ref[block : block + 1, :]
            total = feed + kill_ref[block : block + 1, :]
            now = [steps_at(fields[f], group, block, s, stride) for f, s in pairs]
            before = [steps_before(fields[f], prev, f, group, block, s, stride) for f, s in pairs]
            rate_now = pointwise(*now, feed, total)
            rate_before = pointwise(*before, feed, total)
            for index in range(2 * FIELDS):
                row = (place * FIELDS * 2 + index) * STEPS
                base[block, row : row + STEPS, :] = (now[index] - before[index]) * (1.0 / time_step) - 0.5 * (
                    rate_now[index] + rate_before[index]
                )
    blocks, per_row = tiles.shape[:2]
    for block in range(blocks):
        for k in range(per_row):
            high, low = split(jnp.transpose(tiles[block, k]))
            split_tiles[block, k * LANES : (k + 1) * LANES, :LANES] = high
            split_tiles[block, k * LANES : (k + 1) * LANES, LANES:] = low


def apply_kernel(wide, narrow, cell_blocks, blocks, per_row, *refs):
    refs = list(refs)
    cols, split_tiles, base, parts_ref, wide_lead, wide_late = [refs.pop(0) for _ in range(6)]
    arrived = [refs.pop(0) for _ in narrow]
    outs = [refs.pop(0) for _ in range(FIELDS)]
    extended, made, sems = refs
    stride = 2 * cell_blocks
    size = base.shape[1]
    late_size = wide_late.shape[0]
    extended[:cell_blocks] = parts_ref[...]
    received = [(wide_late, wide, 0), (wide_lead, wide, late_size)]
    received += [(ref, slots, 0) for ref, slots in zip(arrived, narrow)]
    for ref, slots, row in received:
        count, width = ref.shape
        per_slot = width // len(slots) // LANES
        for place, slot in enumerate(slots):
            for b in range(per_slot):
                lane = (place * per_slot + b) * LANES
                high, low = split(ref[:, lane : lane + LANES])
                extended[cell_blocks + slot * per_slot + b, row : row + count, :] = high
                extended[cell_blocks + slot * per_slot + b, size + row : size + row + count, :] = low
    for block in range(blocks):
        chosen = jnp.concatenate([extended[cols[k, block]] for k in range(per_row)], axis=1)
        product = jnp.dot(chosen, split_tiles[block], preferred_element_type=F32)
        product = product[:, :LANES] + product[:, LANES:]
        result = base[block] + (product[:size] + product[size:])
        for index in range(size // STEPS):
            group, field, species = index // (2 * FIELDS), index // 2 % FIELDS, index % 2
            at = group * STEPS * stride + block * 2 + species
            made[field, pl.ds(at, STEPS, stride=stride), :] = result[index * STEPS : (index + 1) * STEPS, :]
    copies = [pltpu.make_async_copy(made.at[f], outs[f], sems.at[f]) for f in range(FIELDS)]
    for copy in copies:
        copy.start()
    for copy in copies:
        copy.wait()


def per_device(state, dir_one, dir_two, feed, kill, tiles, tile_cols, send_rows, send_count):
    steps, _, cells = state.shape
    cell_blocks = cells // LANES
    stride = 2 * cell_blocks
    blocks, per_row = tiles.shape[:2]
    slot_rows = send_rows.shape[2]
    size_dom = lax.axis_size("dom")

    by_route = {}
    for slot, offset in enumerate(OFFSETS):
        by_route.setdefault(offset % size_dom, []).append(slot)
    slot_groups = sorted(by_route.values(), key=lambda slots: -len(slots))

    def view(array):
        array = array.reshape(steps, 2, cell_blocks, LANES).transpose(0, 2, 1, 3)
        return array.reshape(steps * stride, LANES)

    def unview(array):
        array = array.reshape(steps, cell_blocks, 2, LANES).transpose(0, 2, 1, 3)
        return array.reshape(steps, 2, cells)

    fields = [view(state), view(dir_one), view(dir_two)]
    rows = send_rows.reshape(send_rows.shape[1:])
    counts = send_count
    cols = tile_cols.T
    feed = feed.reshape(cell_blocks, LANES)
    kill = kill.reshape(cell_blocks, LANES)

    vmem = pl.BlockSpec(memory_space=VMEM)
    smem = pl.BlockSpec(memory_space=SMEM)
    anywhere = pl.BlockSpec(memory_space=pl.ANY)
    params = pltpu.CompilerParams(vmem_limit_bytes=16 * 1024 * 1024)

    groups = tuple(range(steps // STEPS))
    late, lead = groups[:1], groups[1:]
    wide, *narrow = slot_groups
    others = [slot for slots in narrow for slot in slots]

    def rows_of(part):
        return len(part) * FIELDS * 2 * STEPS

    def f32(*shape):
        return jax.ShapeDtypeStruct(shape, F32)

    def bf16(*shape):
        return jax.ShapeDtypeStruct(shape, BF16)

    def cost(flops, moved):
        return pl.CostEstimate(flops=flops, bytes_accessed=moved, transcendentals=0)

    hbm = pl.BlockSpec(memory_space=pltpu.HBM)
    size = rows_of(groups)
    wide_width = len(wide) * slot_rows
    in_hbm = [pltpu.with_memory_space_constraint(x, pltpu.HBM) for x in (*fields, rows, counts)]
    send, lead_parts, held, listed, last = pl.pallas_call(
        functools.partial(first_kernel, lead, wide, cell_blocks),
        out_shape=[
            f32(rows_of(lead), wide_width),
            bf16(cell_blocks, 2 * rows_of(lead), LANES),
            f32(FIELDS, steps * stride, LANES),
            jax.ShapeDtypeStruct(rows.shape, jnp.int32),
            f32(FIELDS * stride, LANES),
        ],
        in_specs=[hbm] * (FIELDS + 2),
        out_specs=[vmem] * 5,
        scratch_shapes=[
            VMEM((cells, wide_width), BF16),
            VMEM(rows.shape, jnp.int32),
            VMEM(counts.shape, jnp.int32),
            pltpu.SemaphoreType.DMA((2 * FIELDS + 2,)),
        ],
        compiler_params=params,
        cost_estimate=cost(4 * rows_of(lead) * cells * wide_width, 8 * size * cells),
        name="gather_first",
    )(*in_hbm)
    wide_lead = shift_along(send, "dom", OFFSETS[wide[0]])
    prev = shift_along(last, "tm", 1)
    send, *sends, parts = pl.pallas_call(
        functools.partial(rest_kernel, late, wide, others, cell_blocks),
        out_shape=[f32(rows_of(late), wide_width)]
        + [f32(size, len(slots) * slot_rows) for slots in narrow]
        + [bf16(cell_blocks, 2 * size, LANES)],
        in_specs=[vmem] * 4,
        out_specs=[vmem] * (len(narrow) + 2),
        scratch_shapes=[VMEM((cells, len(OFFSETS) * slot_rows), BF16)],
        compiler_params=params,
        cost_estimate=cost(4 * size * cells * len(OFFSETS) * slot_rows, 8 * size * cells),
        name="gather_rest",
    )(held, prev, listed, lead_parts)
    arrived = [shift_along(part, "dom", OFFSETS[slots[0]]) for part, slots in zip(sends, narrow)]
    wide_late = shift_along(send, "dom", OFFSETS[wide[0]])

    base, split_tiles = pl.pallas_call(
        functools.partial(local_kernel, groups, cell_blocks),
        out_shape=[f32(cell_blocks, size, LANES), bf16(blocks, per_row * LANES, 2 * LANES)],
        in_specs=[vmem] * 5,
        out_specs=[vmem] * 2,
        compiler_params=params,
        cost_estimate=cost(60 * size * cells, 8 * tiles.size),
        name="local_terms",
    )(held, prev, feed, kill, tiles)

    outs = pl.pallas_call(
        functools.partial(apply_kernel, wide, narrow, cell_blocks, blocks, per_row),
        out_shape=[f32(steps * stride, LANES)] * FIELDS,
        in_specs=[smem] + [vmem] * (5 + len(narrow)),
        out_specs=[anywhere] * FIELDS,
        scratch_shapes=[
            VMEM((cell_blocks + len(OFFSETS) * slot_rows // LANES, 2 * size, LANES), BF16),
            VMEM((FIELDS, steps * stride, LANES), F32),
            pltpu.SemaphoreType.DMA((FIELDS,)),
        ],
        compiler_params=params,
        cost_estimate=cost(8 * size * blocks * per_row * LANES * LANES, 16 * size * cells),
        name="apply_tiles",
    )(cols, split_tiles, base, parts, wide_lead, wide_late, *arrived)
    return tuple(unview(out) for out in outs)


def solution(mesh):
    fields = P(("group", "tm"), None, "dom")
    in_specs = (
        fields,
        fields,
        fields,
        P("dom"),
        P("dom"),
        P("dom", None, None, None),
        P("dom", None),
        P("dom", None, None),
        P("dom", None),
    )
    return jax.shard_map(
        per_device, mesh=mesh, in_specs=in_specs, out_specs=(fields, fields, fields), check_vma=False
    )
```

```python
import functools

import jax
import jax.numpy as jnp
from jax import lax
from jax.experimental import pallas as pl
from jax.experimental.pallas import tpu as pltpu
from jax.sharding import PartitionSpec as P

OFFSETS = (1, -1, 2, -2)
time_step = 0.5
spread_u = 1.0
spread_v = 0.5
LANES = 128
STEPS = 8
FIELDS = 3
VMEM = pltpu.VMEM
SMEM = pltpu.SMEM
F32 = jnp.float32
BF16 = jnp.bfloat16


def shift_along(block, axis, distance):
    size = lax.axis_size(axis)
    return lax.ppermute(block, axis, [((i - distance) % size, i) for i in range(size)])


def steps_at(ref, group, cell_block, species, stride):
    return ref[pl.ds(group * STEPS * stride + cell_block * 2 + species, STEPS, stride=stride), :]


def steps_before(ref, prev_ref, field, group, cell_block, species, stride):
    offset = cell_block * 2 + species
    if group > 0:
        return ref[pl.ds((group * STEPS - 1) * stride + offset, STEPS, stride=stride), :]
    now = steps_at(ref, 0, cell_block, species, stride)
    row = field * stride + offset
    first = jnp.broadcast_to(prev_ref[row : row + 1, :], now.shape)
    index = lax.broadcasted_iota(jnp.int32, now.shape, 0)
    return jnp.where(index == 0, first, pltpu.roll(now, 1, 0))


def split(values):
    high = values.astype(BF16)
    return high, (values - high.astype(F32)).astype(BF16)


def summed_parts(groups, cell_blocks, fields, prev, parts_ref, high_row, low_row):
    stride = 2 * cell_blocks
    for place, group in enumerate(groups):
        for field in range(FIELDS):
            row = (place * FIELDS + field) * 2 * STEPS
            for block in range(cell_blocks):
                both = []
                for species, scale in enumerate((-0.5 * spread_u, -0.5 * spread_v)):
                    now = steps_at(fields[field], group, block, species, stride)
                    before = steps_before(fields[field], prev, field, group, block, species, stride)
                    both.append((now + before) * scale)
                high, low = split(jnp.concatenate(both, axis=0))
                parts_ref[block, high_row + row : high_row + row + 2 * STEPS, :] = high
                parts_ref[block, low_row + row : low_row + row + 2 * STEPS, :] = low


def choose_rows(slots, listed_ref, choose):
    cells = choose.shape[0]
    slot_rows = listed_ref.shape[1]
    cell = lax.broadcasted_iota(jnp.int32, (LANES, slot_rows), 0)
    for place, slot in enumerate(slots):
        listed = listed_ref[slot : slot + 1, :]
        for start in range(0, cells, LANES):
            hit = cell == listed - start
            choose[start : start + LANES, place * slot_rows : (place + 1) * slot_rows] = jnp.where(
                hit, 1.0, 0.0
            ).astype(BF16)


def take_rows(parts, choose, sends):
    size = parts.shape[0] // 2
    start = 0
    for send in sends:
        width = send.shape[1]
        taken = jnp.dot(parts, choose[:, start : start + width], preferred_element_type=F32)
        send[...] = taken[:size] + taken[size:]
        start += width


def side_by_side(parts_ref, rows):
    blocks = [
        jnp.concatenate([parts_ref[b, start : start + count, :] for start, count in rows], axis=0)
        for b in range(parts_ref.shape[0])
    ]
    return jnp.concatenate(blocks, axis=1)


def first_kernel(lead, slots, cell_blocks, *refs):
    refs = list(refs)
    sources = [refs.pop(0) for _ in range(FIELDS)]
    rows_hbm, count_hbm, send, parts_ref, held, listed, last, choose, rows_ref, count_ref, sems = refs
    stride = 2 * cell_blocks
    early = (lead[0] * STEPS - 1) * stride
    late = held.shape[1] - early
    small = [
        pltpu.make_async_copy(rows_hbm, rows_ref, sems.at[2 * FIELDS]),
        pltpu.make_async_copy(count_hbm, count_ref, sems.at[2 * FIELDS + 1]),
    ]
    needed = [
        pltpu.make_async_copy(sources[f].at[pl.ds(early, late), :], held.at[f, pl.ds(early, late), :], sems.at[f])
        for f in range(FIELDS)
    ]
    others = [
        pltpu.make_async_copy(sources[f].at[pl.ds(0, early), :], held.at[f, pl.ds(0, early), :], sems.at[FIELDS + f])
        for f in range(FIELDS)
    ]
    for copy in small + needed + others:
        copy.start()
    for copy in small:
        copy.wait()
    lane = lax.broadcasted_iota(jnp.int32, rows_ref.shape, 1)
    for slot in range(rows_ref.shape[0]):
        listed[slot : slot + 1, :] = jnp.where(
            lane[slot : slot + 1] < count_ref[:, slot : slot + 1], rows_ref[slot : slot + 1, :], -1
        )
    choose_rows(slots, listed, choose)
    for copy in needed:
        copy.wait()
    size = parts_ref.shape[1] // 2
    summed_parts(lead, cell_blocks, [held.at[f] for f in range(FIELDS)], None, parts_ref, 0, size)
    take_rows(side_by_side(parts_ref, [(0, 2 * size)]), choose, [send])
    for field in range(FIELDS):
        last[field * stride : (field + 1) * stride, :] = held[field, -stride:, :]
    for copy in others:
        copy.wait()


def second_kernel(middle, wide, others, cell_blocks, held, listed, lead_parts, send, *refs):
    *sends, parts_ref, choose = refs
    size = parts_ref.shape[1] // 2
    lead_size = lead_parts.shape[1] // 2
    middle_size = size - lead_size
    choose_rows(wide + others, listed, choose)
    parts_ref[:, middle_size:size, :] = lead_parts[:, :lead_size, :]
    parts_ref[:, size + middle_size :, :] = lead_parts[:, lead_size:, :]
    summed_parts(middle, cell_blocks, [held.at[f] for f in range(FIELDS)], None, parts_ref, 0, size)
    width = send.shape[1]
    take_rows(side_by_side(parts_ref, [(0, middle_size), (size, middle_size)]), choose, [send])
    take_rows(side_by_side(parts_ref, [(0, 2 * size)]), choose.at[:, width:], sends)


def third_kernel(late, wide, others, cell_blocks, held, prev, listed, *refs):
    *sends, parts_ref, choose = refs
    size = parts_ref.shape[1] // 2
    choose_rows(wide + others, listed, choose)
    summed_parts(late, cell_blocks, [held.at[f] for f in range(FIELDS)], prev, parts_ref, 0, size)
    take_rows(side_by_side(parts_ref, [(0, 2 * size)]), choose, sends)


def pointwise(u, v, du, dv, ddu, ddv, feed, total):
    square = v * v
    product = u * square
    twice = 2.0 * u * v
    outs = [feed * (1.0 - u) - product, product - total * v]
    for first, second in ((du, dv), (ddu, ddv)):
        react = square * first + twice * second
        outs += [-react - feed * first, react - total * second]
    return outs


def local_kernel(
    chunks, cell_blocks, held, prev, feed_hbm, kill_hbm, tiles_hbm, base_one, base_two, split_tiles, feed_ref, kill_ref, tiles, sems
):
    copies = [
        pltpu.make_async_copy(feed_hbm, feed_ref, sems.at[0]),
        pltpu.make_async_copy(kill_hbm, kill_ref, sems.at[1]),
        pltpu.make_async_copy(tiles_hbm, tiles, sems.at[2]),
    ]
    for copy in copies:
        copy.start()
    for copy in copies[:2]:
        copy.wait()
    fields = [held.at[f] for f in range(FIELDS)]
    stride = 2 * cell_blocks
    pairs = [(f, s) for f in range(FIELDS) for s in range(2)]
    for base, groups in zip((base_one, base_two), chunks):
        for place, group in enumerate(groups):
            for block in range(cell_blocks):
                feed = feed_ref[block : block + 1, :]
                total = feed + kill_ref[block : block + 1, :]
                now = [steps_at(fields[f], group, block, s, stride) for f, s in pairs]
                before = [steps_before(fields[f], prev, f, group, block, s, stride) for f, s in pairs]
                rate_now = pointwise(*now, feed, total)
                rate_before = pointwise(*before, feed, total)
                for index in range(2 * FIELDS):
                    row = (place * FIELDS * 2 + index) * STEPS
                    base[block, row : row + STEPS, :] = (now[index] - before[index]) * (1.0 / time_step) - 0.5 * (
                        rate_now[index] + rate_before[index]
                    )
    copies[2].wait()
    blocks, per_row = tiles.shape[:2]
    for block in range(blocks):
        for k in range(per_row):
            high, low = split(jnp.transpose(tiles[block, k]))
            split_tiles[block, k * LANES : (k + 1) * LANES, :LANES] = high
            split_tiles[block, k * LANES : (k + 1) * LANES, LANES:] = low


def apply_kernel(groups, received, cell_blocks, blocks, per_row, held_back, *refs):
    refs = list(refs)
    cols_ref, split_tiles, base, parts_ref = [refs.pop(0) for _ in range(4)]
    arrived = [refs.pop(0) for _ in received]
    refs = refs[held_back:]
    outs = [refs.pop(0) for _ in range(FIELDS)]
    extended, made, sems = refs
    stride = 2 * cell_blocks
    size = base.shape[1]
    cols = cols_ref[...]
    extended[:cell_blocks] = parts_ref[...]
    for ref, (slots, row) in zip(arrived, received):
        count, width = ref.shape
        per_slot = width // len(slots) // LANES
        for place, slot in enumerate(slots):
            for b in range(per_slot):
                lane = (place * per_slot + b) * LANES
                high, low = split(ref[:, lane : lane + LANES])
                extended[cell_blocks + slot * per_slot + b, row : row + count, :] = high
                extended[cell_blocks + slot * per_slot + b, size + row : size + row + count, :] = low
    for block in range(blocks):
        chosen = jnp.concatenate([extended[cols[k, block]] for k in range(per_row)], axis=1)
        product = jnp.dot(chosen, split_tiles[block], preferred_element_type=F32)
        product = product[:, :LANES] + product[:, LANES:]
        result = base[block] + (product[:size] + product[size:])
        for index in range(size // STEPS):
            group, field, species = index // (2 * FIELDS), index // 2 % FIELDS, index % 2
            at = group * STEPS * stride + block * 2 + species
            made[field, pl.ds(at, STEPS, stride=stride), :] = result[index * STEPS : (index + 1) * STEPS, :]
    span = pl.ds(groups[0] * STEPS * stride, len(groups) * STEPS * stride)
    copies = [pltpu.make_async_copy(made.at[f], outs[f].at[span, :], sems.at[f]) for f in range(FIELDS)]
    for copy in copies:
        copy.start()
    for copy in copies:
        copy.wait()


def per_device(state, dir_one, dir_two, feed, kill, tiles, tile_cols, send_rows, send_count):
    steps, _, cells = state.shape
    cell_blocks = cells // LANES
    stride = 2 * cell_blocks
    blocks, per_row = tiles.shape[:2]
    slot_rows = send_rows.shape[2]
    size_dom = lax.axis_size("dom")

    by_route = {}
    for slot, offset in enumerate(OFFSETS):
        by_route.setdefault(offset % size_dom, []).append(slot)
    slot_groups = sorted(by_route.values(), key=lambda slots: -len(slots))

    def view(array):
        array = array.reshape(steps, 2, cell_blocks, LANES).transpose(0, 2, 1, 3)
        return array.reshape(steps * stride, LANES)

    def unview(array):
        array = array.reshape(steps, cell_blocks, 2, LANES).transpose(0, 2, 1, 3)
        return array.reshape(steps, 2, cells)

    fields = [view(state), view(dir_one), view(dir_two)]
    rows = send_rows.reshape(send_rows.shape[1:])
    counts = send_count
    cols = tile_cols.T
    feed = feed.reshape(cell_blocks, LANES)
    kill = kill.reshape(cell_blocks, LANES)

    vmem = pl.BlockSpec(memory_space=VMEM)
    smem = pl.BlockSpec(memory_space=SMEM)
    anywhere = pl.BlockSpec(memory_space=pl.ANY)
    params = pltpu.CompilerParams(vmem_limit_bytes=16 * 1024 * 1024)

    groups = tuple(range(steps // STEPS))
    late, middle, lead = groups[:1], groups[1:-1], groups[-1:]
    most = middle + lead
    wide, *narrow = slot_groups
    others = [slot for slots in narrow for slot in slots]

    def rows_of(part):
        return len(part) * FIELDS * 2 * STEPS

    def f32(*shape):
        return jax.ShapeDtypeStruct(shape, F32)

    def parts_of(part):
        return jax.ShapeDtypeStruct((cell_blocks, 2 * rows_of(part), LANES), BF16)

    def sends_of(part, chosen):
        return [f32(rows_of(part), len(slots) * slot_rows) for slots in chosen]

    def cost(flops, moved):
        return pl.CostEstimate(flops=flops, bytes_accessed=moved, transcendentals=0)

    def in_hbm(*arrays):
        return [pltpu.with_memory_space_constraint(array, pltpu.HBM) for array in arrays]

    def send_to(send, slots):
        return shift_along(send, "dom", OFFSETS[slots[0]])

    hbm = pl.BlockSpec(memory_space=pltpu.HBM)
    size = rows_of(groups)
    every = len(OFFSETS) * slot_rows
    wide_width = len(wide) * slot_rows
    send, lead_parts, held, listed, last = pl.pallas_call(
        functools.partial(first_kernel, lead, wide, cell_blocks),
        out_shape=[
            f32(rows_of(lead), wide_width),
            parts_of(lead),
            f32(FIELDS, steps * stride, LANES),
            jax.ShapeDtypeStruct(rows.shape, jnp.int32),
            f32(FIELDS * stride, LANES),
        ],
        in_specs=[hbm] * (FIELDS + 2),
        out_specs=[vmem] * 5,
        scratch_shapes=[
            VMEM((cells, wide_width), BF16),
            VMEM(rows.shape, jnp.int32),
            VMEM(counts.shape, jnp.int32),
            pltpu.SemaphoreType.DMA((2 * FIELDS + 2,)),
        ],
        compiler_params=params,
        cost_estimate=cost(4 * rows_of(lead) * cells * wide_width, 8 * size * cells),
        name="gather_first",
    )(*in_hbm(*fields, rows, counts))
    wide_lead = send_to(send, wide)
    send, *sends, most_parts = pl.pallas_call(
        functools.partial(second_kernel, middle, wide, others, cell_blocks),
        out_shape=sends_of(middle, [wide]) + sends_of(most, narrow) + [parts_of(most)],
        in_specs=[vmem] * 3,
        out_specs=[vmem] * (len(narrow) + 2),
        scratch_shapes=[VMEM((cells, every), BF16)],
        compiler_params=params,
        cost_estimate=cost(4 * rows_of(most) * cells * every, 8 * size * cells),
        name="gather_second",
    )(held, listed, lead_parts)
    wide_middle = send_to(send, wide)
    prev = shift_along(last, "tm", 1)
    narrow_most = [send_to(part, slots) for part, slots in zip(sends, narrow)]
    *sends, late_parts = pl.pallas_call(
        functools.partial(third_kernel, late, wide, others, cell_blocks),
        out_shape=sends_of(late, slot_groups) + [parts_of(late)],
        in_specs=[vmem] * 3,
        out_specs=[vmem] * (len(slot_groups) + 1),
        scratch_shapes=[VMEM((cells, every), BF16)],
        compiler_params=params,
        cost_estimate=cost(4 * rows_of(late) * cells * every, 8 * size * cells),
        name="gather_third",
    )(held, prev, listed)
    arrived_late = [send_to(sends[0], wide)]
    sends[1], wide_lead = lax.optimization_barrier((sends[1], wide_lead))
    arrived_late.append(send_to(sends[1], slot_groups[1]))
    for number in range(2, len(sends)):
        sends[number], wide_middle = lax.optimization_barrier((sends[number], wide_middle))
        arrived_late.append(send_to(sends[number], slot_groups[number]))

    base_most, base_late, split_tiles = pl.pallas_call(
        functools.partial(local_kernel, (most, late), cell_blocks),
        out_shape=[
            f32(cell_blocks, rows_of(most), LANES),
            f32(cell_blocks, rows_of(late), LANES),
            jax.ShapeDtypeStruct((blocks, per_row * LANES, 2 * LANES), BF16),
        ],
        in_specs=[vmem] * 2 + [hbm] * 3,
        out_specs=[vmem] * 3,
        scratch_shapes=[
            VMEM(feed.shape, F32),
            VMEM(kill.shape, F32),
            VMEM(tiles.shape, F32),
            pltpu.SemaphoreType.DMA((3,)),
        ],
        compiler_params=params,
        cost_estimate=cost(60 * size * cells, 8 * tiles.size),
        name="local_terms",
    )(held, prev, *in_hbm(feed, kill, tiles))

    def apply(part, base, parts, transfers, outs):
        inputs = [cols, split_tiles, base, parts, *[array for array, _, _ in transfers]]
        received = [(slots, row) for _, slots, row in transfers]
        return pl.pallas_call(
            functools.partial(apply_kernel, part, received, cell_blocks, blocks, per_row, len(outs)),
            out_shape=[f32(steps * stride, LANES)] * FIELDS,
            in_specs=[vmem] * len(inputs) + [anywhere] * len(outs),
            out_specs=[anywhere] * FIELDS,
            input_output_aliases={len(inputs) + f: f for f in range(len(outs))},
            scratch_shapes=[
                VMEM((cell_blocks + every // LANES, 2 * rows_of(part), LANES), BF16),
                VMEM((FIELDS, len(part) * STEPS * stride, LANES), F32),
                pltpu.SemaphoreType.DMA((FIELDS,)),
            ],
            compiler_params=params,
            cost_estimate=cost(8 * rows_of(part) * blocks * per_row * LANES * LANES, 16 * rows_of(part) * cells),
            name="apply_tiles",
        )(*inputs, *outs)

    transfers = [(wide_middle, wide, 0), (wide_lead, wide, rows_of(middle))]
    transfers += [(array, slots, 0) for array, slots in zip(narrow_most, narrow)]
    outs = apply(most, base_most, most_parts, transfers, [])
    transfers = [(array, slots, 0) for array, slots in zip(arrived_late, slot_groups)]
    outs = apply(late, base_late, late_parts, transfers, outs)
    return tuple(unview(out) for out in outs)


def solution(mesh):
    fields = P(("group", "tm"), None, "dom")
    in_specs = (
        fields,
        fields,
        fields,
        P("dom"),
        P("dom"),
        P("dom", None, None, None),
        P("dom", None),
        P("dom", None, None),
        P("dom", None),
    )
    return jax.shard_map(
        per_device, mesh=mesh, in_specs=in_specs, out_specs=(fields, fields, fields), check_vma=False
    )
```

```python
import functools

import jax
import jax.numpy as jnp
from jax import lax
from jax.experimental import pallas as pl
from jax.experimental.pallas import tpu as pltpu
from jax.sharding import PartitionSpec as P

OFFSETS = (1, -1, 2, -2)
time_step = 0.5
spread_u = 1.0
spread_v = 0.5
LANES = 128
STEPS = 8
FIELDS = 3
VMEM = pltpu.VMEM
SMEM = pltpu.SMEM
F32 = jnp.float32
BF16 = jnp.bfloat16


def shift_along(block, axis, distance):
    size = lax.axis_size(axis)
    return lax.ppermute(block, axis, [((i - distance) % size, i) for i in range(size)])


def steps_at(ref, group, cell_block, species, stride):
    return ref[pl.ds(group * STEPS * stride + cell_block * 2 + species, STEPS, stride=stride), :]


def steps_before(ref, prev_ref, field, group, cell_block, species, stride):
    offset = cell_block * 2 + species
    if group > 0:
        return ref[pl.ds((group * STEPS - 1) * stride + offset, STEPS, stride=stride), :]
    now = steps_at(ref, 0, cell_block, species, stride)
    row = field * stride + offset
    first = jnp.broadcast_to(prev_ref[row : row + 1, :], now.shape)
    index = lax.broadcasted_iota(jnp.int32, now.shape, 0)
    return jnp.where(index == 0, first, pltpu.roll(now, 1, 0))


def split(values):
    high = values.astype(BF16)
    return high, (values - high.astype(F32)).astype(BF16)


def summed_parts(groups, cell_blocks, fields, prev, parts_ref, high_row, low_row):
    stride = 2 * cell_blocks
    for place, group in enumerate(groups):
        for field in range(FIELDS):
            row = (place * FIELDS + field) * 2 * STEPS
            for block in range(cell_blocks):
                both = []
                for species, scale in enumerate((-0.5 * spread_u, -0.5 * spread_v)):
                    now = steps_at(fields[field], group, block, species, stride)
                    before = steps_before(fields[field], prev, field, group, block, species, stride)
                    both.append((now + before) * scale)
                high, low = split(jnp.concatenate(both, axis=0))
                parts_ref[block, high_row + row : high_row + row + 2 * STEPS, :] = high
                parts_ref[block, low_row + row : low_row + row + 2 * STEPS, :] = low


def choose_rows(slots, listed_ref, choose):
    cells = choose.shape[0]
    slot_rows = listed_ref.shape[1]
    cell = lax.broadcasted_iota(jnp.int32, (LANES, slot_rows), 0)
    for place, slot in enumerate(slots):
        listed = listed_ref[slot : slot + 1, :]
        for start in range(0, cells, LANES):
            hit = cell == listed - start
            choose[start : start + LANES, place * slot_rows : (place + 1) * slot_rows] = jnp.where(
                hit, 1.0, 0.0
            ).astype(BF16)


def take_rows(parts, choose, sends):
    size = parts.shape[0] // 2
    start = 0
    for send in sends:
        width = send.shape[1]
        taken = jnp.dot(parts, choose[:, start : start + width], preferred_element_type=F32)
        send[...] = taken[:size] + taken[size:]
        start += width


def side_by_side(parts_ref, rows):
    blocks = [
        jnp.concatenate([parts_ref[b, start : start + count, :] for start, count in rows], axis=0)
        for b in range(parts_ref.shape[0])
    ]
    return jnp.concatenate(blocks, axis=1)


def first_kernel(lead, slots, cell_blocks, *refs):
    refs = list(refs)
    sources = [refs.pop(0) for _ in range(FIELDS)]
    rows_hbm, count_hbm, send, parts_ref, held, listed, last, choose, rows_ref, count_ref, sems = refs
    stride = 2 * cell_blocks
    early = (lead[0] * STEPS - 1) * stride
    late = held.shape[1] - early
    small = [
        pltpu.make_async_copy(rows_hbm, rows_ref, sems.at[2 * FIELDS]),
        pltpu.make_async_copy(count_hbm, count_ref, sems.at[2 * FIELDS + 1]),
    ]
    needed = [
        pltpu.make_async_copy(sources[f].at[pl.ds(early, late), :], held.at[f, pl.ds(early, late), :], sems.at[f])
        for f in range(FIELDS)
    ]
    others = [
        pltpu.make_async_copy(sources[f].at[pl.ds(0, early), :], held.at[f, pl.ds(0, early), :], sems.at[FIELDS + f])
        for f in range(FIELDS)
    ]
    for copy in small + needed + others:
        copy.start()
    for copy in small:
        copy.wait()
    lane = lax.broadcasted_iota(jnp.int32, rows_ref.shape, 1)
    for slot in range(rows_ref.shape[0]):
        listed[slot : slot + 1, :] = jnp.where(
            lane[slot : slot + 1] < count_ref[:, slot : slot + 1], rows_ref[slot : slot + 1, :], -1
        )
    choose_rows(slots, listed, choose)
    for copy in needed:
        copy.wait()
    size = parts_ref.shape[1] // 2
    summed_parts(lead, cell_blocks, [held.at[f] for f in range(FIELDS)], None, parts_ref, 0, size)
    take_rows(side_by_side(parts_ref, [(0, 2 * size)]), choose, [send])
    for field in range(FIELDS):
        last[field * stride : (field + 1) * stride, :] = held[field, -stride:, :]
    for copy in others:
        copy.wait()


def second_kernel(middle, wide, others, cell_blocks, held, listed, lead_parts, send, *refs):
    *sends, parts_ref, choose = refs
    size = parts_ref.shape[1] // 2
    lead_size = lead_parts.shape[1] // 2
    middle_size = size - lead_size
    choose_rows(wide + others, listed, choose)
    parts_ref[:, middle_size:size, :] = lead_parts[:, :lead_size, :]
    parts_ref[:, size + middle_size :, :] = lead_parts[:, lead_size:, :]
    summed_parts(middle, cell_blocks, [held.at[f] for f in range(FIELDS)], None, parts_ref, 0, size)
    width = send.shape[1]
    take_rows(side_by_side(parts_ref, [(0, middle_size), (size, middle_size)]), choose, [send])
    take_rows(side_by_side(parts_ref, [(0, 2 * size)]), choose.at[:, width:], sends)


def third_kernel(late, wide, others, cell_blocks, held, prev, listed, *refs):
    *sends, parts_ref, choose = refs
    size = parts_ref.shape[1] // 2
    choose_rows(wide + others, listed, choose)
    summed_parts(late, cell_blocks, [held.at[f] for f in range(FIELDS)], prev, parts_ref, 0, size)
    take_rows(side_by_side(parts_ref, [(0, 2 * size)]), choose, sends)


def pointwise(u, v, du, dv, ddu, ddv, feed, total):
    square = v * v
    product = u * square
    twice = 2.0 * u * v
    outs = [feed * (1.0 - u) - product, product - total * v]
    for first, second in ((du, dv), (ddu, ddv)):
        react = square * first + twice * second
        outs += [-react - feed * first, react - total * second]
    return outs


def local_kernel(
    chunks, cell_blocks, held, prev, feed_hbm, kill_hbm, tiles_hbm, base_one, base_two, split_tiles, feed_ref, kill_ref, tiles, sems
):
    copies = [
        pltpu.make_async_copy(feed_hbm, feed_ref, sems.at[0]),
        pltpu.make_async_copy(kill_hbm, kill_ref, sems.at[1]),
        pltpu.make_async_copy(tiles_hbm, tiles, sems.at[2]),
    ]
    for copy in copies:
        copy.start()
    for copy in copies[:2]:
        copy.wait()
    fields = [held.at[f] for f in range(FIELDS)]
    stride = 2 * cell_blocks
    pairs = [(f, s) for f in range(FIELDS) for s in range(2)]
    for base, groups in zip((base_one, base_two), chunks):
        for place, group in enumerate(groups):
            for block in range(cell_blocks):
                feed = feed_ref[block : block + 1, :]
                total = feed + kill_ref[block : block + 1, :]
                now = [steps_at(fields[f], group, block, s, stride) for f, s in pairs]
                before = [steps_before(fields[f], prev, f, group, block, s, stride) for f, s in pairs]
                rate_now = pointwise(*now, feed, total)
                rate_before = pointwise(*before, feed, total)
                for index in range(2 * FIELDS):
                    row = (place * FIELDS * 2 + index) * STEPS
                    base[block, row : row + STEPS, :] = (now[index] - before[index]) * (1.0 / time_step) - 0.5 * (
                        rate_now[index] + rate_before[index]
                    )
    copies[2].wait()
    blocks, per_row = tiles.shape[:2]
    for block in range(blocks):
        for k in range(per_row):
            high, low = split(jnp.transpose(tiles[block, k]))
            split_tiles[block, k * LANES : (k + 1) * LANES, :LANES] = high
            split_tiles[block, k * LANES : (k + 1) * LANES, LANES:] = low


def apply_kernel(groups, received, cell_blocks, blocks, per_row, held_back, *refs):
    refs = list(refs)
    cols_ref, split_tiles, base, parts_ref = [refs.pop(0) for _ in range(4)]
    arrived = [refs.pop(0) for _ in received]
    refs = refs[held_back:]
    outs = [refs.pop(0) for _ in range(FIELDS)]
    extended, made, sems = refs
    stride = 2 * cell_blocks
    size = base.shape[1]
    cols = cols_ref[...]
    extended[:cell_blocks] = parts_ref[...]
    for ref, (slots, row) in zip(arrived, received):
        count, width = ref.shape
        per_slot = width // len(slots) // LANES
        for place, slot in enumerate(slots):
            for b in range(per_slot):
                lane = (place * per_slot + b) * LANES
                high, low = split(ref[:, lane : lane + LANES])
                extended[cell_blocks + slot * per_slot + b, row : row + count, :] = high
                extended[cell_blocks + slot * per_slot + b, size + row : size + row + count, :] = low
    for block in range(blocks):
        chosen = jnp.concatenate([extended[cols[k, block]] for k in range(per_row)], axis=1)
        product = jnp.dot(chosen, split_tiles[block], preferred_element_type=F32)
        product = product[:, :LANES] + product[:, LANES:]
        result = base[block] + (product[:size] + product[size:])
        for index in range(size // STEPS):
            group, field, species = index // (2 * FIELDS), index // 2 % FIELDS, index % 2
            at = group * STEPS * stride + block * 2 + species
            made[field, pl.ds(at, STEPS, stride=stride), :] = result[index * STEPS : (index + 1) * STEPS, :]
    span = pl.ds(groups[0] * STEPS * stride, len(groups) * STEPS * stride)
    copies = [pltpu.make_async_copy(made.at[f], outs[f].at[span, :], sems.at[f]) for f in range(FIELDS)]
    for copy in copies:
        copy.start()
    for copy in copies:
        copy.wait()


def per_device(state, dir_one, dir_two, feed, kill, tiles, tile_cols, send_rows, send_count):
    steps, _, cells = state.shape
    cell_blocks = cells // LANES
    stride = 2 * cell_blocks
    blocks, per_row = tiles.shape[:2]
    slot_rows = send_rows.shape[2]
    size_dom = lax.axis_size("dom")

    by_route = {}
    for slot, offset in enumerate(OFFSETS):
        by_route.setdefault(offset % size_dom, []).append(slot)
    slot_groups = sorted(by_route.values(), key=lambda slots: -len(slots))

    def view(array):
        array = array.reshape(steps, 2, cell_blocks, LANES).transpose(0, 2, 1, 3)
        return array.reshape(steps * stride, LANES)

    def unview(array):
        array = array.reshape(steps, cell_blocks, 2, LANES).transpose(0, 2, 1, 3)
        return array.reshape(steps, 2, cells)

    fields = [view(state), view(dir_one), view(dir_two)]
    rows = send_rows.reshape(send_rows.shape[1:])
    counts = send_count
    cols = tile_cols.T
    feed = feed.reshape(cell_blocks, LANES)
    kill = kill.reshape(cell_blocks, LANES)

    vmem = pl.BlockSpec(memory_space=VMEM)
    smem = pl.BlockSpec(memory_space=SMEM)
    anywhere = pl.BlockSpec(memory_space=pl.ANY)
    params = pltpu.CompilerParams(vmem_limit_bytes=16 * 1024 * 1024)

    groups = tuple(range(steps // STEPS))
    late, middle, lead = groups[:1], groups[1:-1], groups[-1:]
    most = middle + lead
    wide, *narrow = slot_groups
    others = [slot for slots in narrow for slot in slots]

    def rows_of(part):
        return len(part) * FIELDS * 2 * STEPS

    def f32(*shape):
        return jax.ShapeDtypeStruct(shape, F32)

    def parts_of(part):
        return jax.ShapeDtypeStruct((cell_blocks, 2 * rows_of(part), LANES), BF16)

    def sends_of(part, chosen):
        return [f32(rows_of(part), len(slots) * slot_rows) for slots in chosen]

    def cost(flops, moved):
        return pl.CostEstimate(flops=flops, bytes_accessed=moved, transcendentals=0)

    def in_hbm(*arrays):
        return [pltpu.with_memory_space_constraint(array, pltpu.HBM) for array in arrays]

    def send_to(send, slots):
        return shift_along(send, "dom", OFFSETS[slots[0]])

    hbm = pl.BlockSpec(memory_space=pltpu.HBM)
    size = rows_of(groups)
    every = len(OFFSETS) * slot_rows
    wide_width = len(wide) * slot_rows
    send, lead_parts, held, listed, last = pl.pallas_call(
        functools.partial(first_kernel, lead, wide, cell_blocks),
        out_shape=[
            f32(rows_of(lead), wide_width),
            parts_of(lead),
            f32(FIELDS, steps * stride, LANES),
            jax.ShapeDtypeStruct(rows.shape, jnp.int32),
            f32(FIELDS * stride, LANES),
        ],
        in_specs=[hbm] * (FIELDS + 2),
        out_specs=[vmem] * 5,
        scratch_shapes=[
            VMEM((cells, wide_width), BF16),
            VMEM(rows.shape, jnp.int32),
            VMEM(counts.shape, jnp.int32),
            pltpu.SemaphoreType.DMA((2 * FIELDS + 2,)),
        ],
        compiler_params=params,
        cost_estimate=cost(4 * rows_of(lead) * cells * wide_width, 8 * size * cells),
        name="gather_first",
    )(*in_hbm(*fields, rows, counts))
    wide_lead = send_to(send, wide)
    send, *sends, most_parts = pl.pallas_call(
        functools.partial(second_kernel, middle, wide, others, cell_blocks),
        out_shape=sends_of(middle, [wide]) + sends_of(most, narrow) + [parts_of(most)],
        in_specs=[vmem] * 3,
        out_specs=[vmem] * (len(narrow) + 2),
        scratch_shapes=[VMEM((cells, every), BF16)],
        compiler_params=params,
        cost_estimate=cost(4 * rows_of(most) * cells * every, 8 * size * cells),
        name="gather_second",
    )(held, listed, lead_parts)
    wide_middle = send_to(send, wide)
    prev = shift_along(last, "tm", 1)
    narrow_most = [send_to(part, slots) for part, slots in zip(sends, narrow)]
    *sends, late_parts = pl.pallas_call(
        functools.partial(third_kernel, late, wide, others, cell_blocks),
        out_shape=sends_of(late, slot_groups) + [parts_of(late)],
        in_specs=[vmem] * 3,
        out_specs=[vmem] * (len(slot_groups) + 1),
        scratch_shapes=[VMEM((cells, every), BF16)],
        compiler_params=params,
        cost_estimate=cost(4 * rows_of(late) * cells * every, 8 * size * cells),
        name="gather_third",
    )(held, prev, listed)
    base_most, base_late, split_tiles = pl.pallas_call(
        functools.partial(local_kernel, (most, late), cell_blocks),
        out_shape=[
            f32(cell_blocks, rows_of(most), LANES),
            f32(cell_blocks, rows_of(late), LANES),
            jax.ShapeDtypeStruct((blocks, per_row * LANES, 2 * LANES), BF16),
        ],
        in_specs=[vmem] * 2 + [hbm] * 3,
        out_specs=[vmem] * 3,
        scratch_shapes=[
            VMEM(feed.shape, F32),
            VMEM(kill.shape, F32),
            VMEM(tiles.shape, F32),
            pltpu.SemaphoreType.DMA((3,)),
        ],
        compiler_params=params,
        cost_estimate=cost(60 * size * cells, 8 * tiles.size),
        name="local_terms",
    )(held, prev, *in_hbm(feed, kill, tiles))

    arrived_late = [send_to(sends[0], wide)]
    sends[1], wide_lead = lax.optimization_barrier((sends[1], wide_lead))
    arrived_late.append(send_to(sends[1], slot_groups[1]))
    for number in range(2, len(sends)):
        sends[number], wide_middle, split_tiles = lax.optimization_barrier((sends[number], wide_middle, split_tiles))
        arrived_late.append(send_to(sends[number], slot_groups[number]))

    def apply(part, base, parts, transfers, outs):
        inputs = [cols, split_tiles, base, parts, *[array for array, _, _ in transfers]]
        received = [(slots, row) for _, slots, row in transfers]
        return pl.pallas_call(
            functools.partial(apply_kernel, part, received, cell_blocks, blocks, per_row, len(outs)),
            out_shape=[f32(steps * stride, LANES)] * FIELDS,
            in_specs=[vmem] * len(inputs) + [anywhere] * len(outs),
            out_specs=[anywhere] * FIELDS,
            input_output_aliases={len(inputs) + f: f for f in range(len(outs))},
            scratch_shapes=[
                VMEM((cell_blocks + every // LANES, 2 * rows_of(part), LANES), BF16),
                VMEM((FIELDS, len(part) * STEPS * stride, LANES), F32),
                pltpu.SemaphoreType.DMA((FIELDS,)),
            ],
            compiler_params=params,
            cost_estimate=cost(8 * rows_of(part) * blocks * per_row * LANES * LANES, 16 * rows_of(part) * cells),
            name="apply_tiles",
        )(*inputs, *outs)

    transfers = [(wide_middle, wide, 0), (wide_lead, wide, rows_of(middle))]
    transfers += [(array, slots, 0) for array, slots in zip(narrow_most, narrow)]
    outs = apply(most, base_most, most_parts, transfers, [])
    transfers = [(array, slots, 0) for array, slots in zip(arrived_late, slot_groups)]
    outs = apply(late, base_late, late_parts, transfers, outs)
    return tuple(unview(out) for out in outs)


def solution(mesh):
    fields = P(("group", "tm"), None, "dom")
    in_specs = (
        fields,
        fields,
        fields,
        P("dom"),
        P("dom"),
        P("dom", None, None, None),
        P("dom", None),
        P("dom", None, None),
        P("dom", None),
    )
    return jax.shard_map(
        per_device, mesh=mesh, in_specs=in_specs, out_specs=(fields, fields, fields), check_vma=False
    )
```

```python
import functools

import jax
import jax.numpy as jnp
from jax import lax
from jax.experimental import pallas as pl
from jax.experimental.pallas import tpu as pltpu
from jax.sharding import PartitionSpec as P

OFFSETS = (1, -1, 2, -2)
time_step = 0.5
spread_u = 1.0
spread_v = 0.5
LANES = 128
STEPS = 8
FIELDS = 3
VMEM = pltpu.VMEM
SMEM = pltpu.SMEM
F32 = jnp.float32
BF16 = jnp.bfloat16


def shift_along(block, axis, distance):
    size = lax.axis_size(axis)
    return lax.ppermute(block, axis, [((i - distance) % size, i) for i in range(size)])


def steps_at(ref, group, cell_block, species, stride):
    return ref[pl.ds(group * STEPS * stride + cell_block * 2 + species, STEPS, stride=stride), :]


def steps_before(ref, prev_ref, field, group, cell_block, species, stride):
    offset = cell_block * 2 + species
    if group > 0:
        return ref[pl.ds((group * STEPS - 1) * stride + offset, STEPS, stride=stride), :]
    now = steps_at(ref, 0, cell_block, species, stride)
    row = field * stride + offset
    first = jnp.broadcast_to(prev_ref[row : row + 1, :], now.shape)
    index = lax.broadcasted_iota(jnp.int32, now.shape, 0)
    return jnp.where(index == 0, first, pltpu.roll(now, 1, 0))


def split(values):
    high = values.astype(BF16)
    return high, (values - high.astype(F32)).astype(BF16)


def scaled_sum(ref, prev_ref, field, group, cell_block, species, stride):
    now = steps_at(ref, group, cell_block, species, stride)
    before = steps_before(ref, prev_ref, field, group, cell_block, species, stride)
    return (now + before) * (-0.5 * (spread_u, spread_v)[species])


def summed_parts(groups, cell_blocks, fields, prev, parts_ref, high_row, low_row):
    stride = 2 * cell_blocks
    for place, group in enumerate(groups):
        for field in range(FIELDS):
            row = (place * FIELDS + field) * 2 * STEPS
            for block in range(cell_blocks):
                both = [scaled_sum(fields[field], prev, field, group, block, species, stride) for species in range(2)]
                high, low = split(jnp.concatenate(both, axis=0))
                parts_ref[block, high_row + row : high_row + row + 2 * STEPS, :] = high
                parts_ref[block, low_row + row : low_row + row + 2 * STEPS, :] = low


def choose_rows(slots, listed_ref, choose):
    cells = choose.shape[0]
    slot_rows = listed_ref.shape[1]
    cell = lax.broadcasted_iota(jnp.int32, (LANES, slot_rows), 0)
    for place, slot in enumerate(slots):
        listed = listed_ref[slot : slot + 1, :]
        for start in range(0, cells, LANES):
            hit = cell == listed - start
            choose[start : start + LANES, place * slot_rows : (place + 1) * slot_rows] = jnp.where(
                hit, 1.0, 0.0
            ).astype(BF16)


def take_rows(parts, choose, sends):
    size = parts.shape[0] // 2
    start = 0
    for send in sends:
        width = send.shape[1]
        taken = jnp.dot(parts, choose[:, start : start + width], preferred_element_type=F32)
        send[...] = taken[:size] + taken[size:]
        start += width


def side_by_side(parts_ref, rows):
    blocks = [
        jnp.concatenate([parts_ref[b, start : start + count, :] for start, count in rows], axis=0)
        for b in range(parts_ref.shape[0])
    ]
    return jnp.concatenate(blocks, axis=1)


def first_kernel(lead, slots, cell_blocks, *refs):
    refs = list(refs)
    sources = [refs.pop(0) for _ in range(FIELDS)]
    rows_hbm, count_hbm, send, held, listed, last, rows_ref, count_ref, sems = refs
    stride = 2 * cell_blocks
    early = (lead[0] * STEPS - 1) * stride
    late = held.shape[1] - early
    small = [
        pltpu.make_async_copy(rows_hbm, rows_ref, sems.at[2 * FIELDS]),
        pltpu.make_async_copy(count_hbm, count_ref, sems.at[2 * FIELDS + 1]),
    ]
    needed = [
        pltpu.make_async_copy(sources[f].at[pl.ds(early, late), :], held.at[f, pl.ds(early, late), :], sems.at[f])
        for f in range(FIELDS)
    ]
    others = [
        pltpu.make_async_copy(sources[f].at[pl.ds(0, early), :], held.at[f, pl.ds(0, early), :], sems.at[FIELDS + f])
        for f in range(FIELDS)
    ]
    for copy in small + needed + others:
        copy.start()
    for copy in small:
        copy.wait()
    lane = lax.broadcasted_iota(jnp.int32, rows_ref.shape, 1)
    for slot in range(rows_ref.shape[0]):
        listed[slot : slot + 1, :] = jnp.where(
            lane[slot : slot + 1] < count_ref[:, slot : slot + 1], rows_ref[slot : slot + 1, :], -1
        )
    for copy in needed:
        copy.wait()
    columns = [
        listed[slot : slot + 1, start : start + LANES]
        for slot in slots
        for start in range(0, listed.shape[1], LANES)
    ]
    columns = [jnp.broadcast_to(column, (STEPS, LANES)) for column in columns]
    for place, group in enumerate(lead):
        for field in range(FIELDS):
            for species in range(2):
                row = ((place * FIELDS + field) * 2 + species) * STEPS
                sums = [
                    scaled_sum(held.at[field], None, field, group, block, species, stride) for block in range(cell_blocks)
                ]
                for number, column in enumerate(columns):
                    lanes = column & (LANES - 1)
                    found = jnp.zeros((STEPS, LANES), F32)
                    for block in range(cell_blocks):
                        taken = jnp.take_along_axis(sums[block], lanes, axis=1, mode="promise_in_bounds")
                        found = jnp.where(column >> 7 == block, taken, found)
                    send[row : row + STEPS, number * LANES : (number + 1) * LANES] = found
    for field in range(FIELDS):
        last[field * stride : (field + 1) * stride, :] = held[field, -stride:, :]
    for copy in others:
        copy.wait()


def second_kernel(most, middle, wide, others, cell_blocks, held, listed, send, *refs):
    *sends, parts_ref, choose = refs
    size = parts_ref.shape[1] // 2
    middle_size = size * len(middle) // len(most)
    choose_rows(wide + others, listed, choose)
    summed_parts(most, cell_blocks, [held.at[f] for f in range(FIELDS)], None, parts_ref, 0, size)
    width = send.shape[1]
    take_rows(side_by_side(parts_ref, [(0, middle_size), (size, middle_size)]), choose, [send])
    take_rows(side_by_side(parts_ref, [(0, 2 * size)]), choose.at[:, width:], sends)


def third_kernel(late, wide, others, cell_blocks, held, prev, listed, *refs):
    *sends, parts_ref, choose = refs
    size = parts_ref.shape[1] // 2
    choose_rows(wide + others, listed, choose)
    summed_parts(late, cell_blocks, [held.at[f] for f in range(FIELDS)], prev, parts_ref, 0, size)
    take_rows(side_by_side(parts_ref, [(0, 2 * size)]), choose, sends)


def pointwise(u, v, du, dv, ddu, ddv, feed, total):
    square = v * v
    product = u * square
    twice = 2.0 * u * v
    outs = [feed * (1.0 - u) - product, product - total * v]
    for first, second in ((du, dv), (ddu, ddv)):
        react = square * first + twice * second
        outs += [-react - feed * first, react - total * second]
    return outs


def local_kernel(
    chunks, cell_blocks, held, prev, feed_hbm, kill_hbm, tiles_hbm, base_one, base_two, split_tiles, feed_ref, kill_ref, tiles, sems
):
    copies = [
        pltpu.make_async_copy(feed_hbm, feed_ref, sems.at[0]),
        pltpu.make_async_copy(kill_hbm, kill_ref, sems.at[1]),
        pltpu.make_async_copy(tiles_hbm, tiles, sems.at[2]),
    ]
    for copy in copies:
        copy.start()
    for copy in copies[:2]:
        copy.wait()
    fields = [held.at[f] for f in range(FIELDS)]
    stride = 2 * cell_blocks
    pairs = [(f, s) for f in range(FIELDS) for s in range(2)]
    for base, groups in zip((base_one, base_two), chunks):
        for place, group in enumerate(groups):
            for block in range(cell_blocks):
                feed = feed_ref[block : block + 1, :]
                total = feed + kill_ref[block : block + 1, :]
                now = [steps_at(fields[f], group, block, s, stride) for f, s in pairs]
                before = [steps_before(fields[f], prev, f, group, block, s, stride) for f, s in pairs]
                rate_now = pointwise(*now, feed, total)
                rate_before = pointwise(*before, feed, total)
                for index in range(2 * FIELDS):
                    row = (place * FIELDS * 2 + index) * STEPS
                    base[block, row : row + STEPS, :] = (now[index] - before[index]) * (1.0 / time_step) - 0.5 * (
                        rate_now[index] + rate_before[index]
                    )
    copies[2].wait()
    blocks, per_row = tiles.shape[:2]
    for block in range(blocks):
        for k in range(per_row):
            high, low = split(jnp.transpose(tiles[block, k]))
            split_tiles[block, k * LANES : (k + 1) * LANES, :LANES] = high
            split_tiles[block, k * LANES : (k + 1) * LANES, LANES:] = low


def apply_kernel(groups, received, cell_blocks, blocks, per_row, held_back, *refs):
    refs = list(refs)
    cols_ref, split_tiles, base, parts_ref = [refs.pop(0) for _ in range(4)]
    arrived = [refs.pop(0) for _ in received]
    refs = refs[held_back:]
    outs = [refs.pop(0) for _ in range(FIELDS)]
    extended, made, sems = refs
    stride = 2 * cell_blocks
    size = base.shape[1]
    cols = cols_ref[...]
    extended[:cell_blocks] = parts_ref[...]
    for ref, (slots, row) in zip(arrived, received):
        count, width = ref.shape
        per_slot = width // len(slots) // LANES
        for place, slot in enumerate(slots):
            for b in range(per_slot):
                lane = (place * per_slot + b) * LANES
                high, low = split(ref[:, lane : lane + LANES])
                extended[cell_blocks + slot * per_slot + b, row : row + count, :] = high
                extended[cell_blocks + slot * per_slot + b, size + row : size + row + count, :] = low
    for block in range(blocks):
        chosen = jnp.concatenate([extended[cols[k, block]] for k in range(per_row)], axis=1)
        product = jnp.dot(chosen, split_tiles[block], preferred_element_type=F32)
        product = product[:, :LANES] + product[:, LANES:]
        result = base[block] + (product[:size] + product[size:])
        for index in range(size // STEPS):
            group, field, species = index // (2 * FIELDS), index // 2 % FIELDS, index % 2
            at = group * STEPS * stride + block * 2 + species
            made[field, pl.ds(at, STEPS, stride=stride), :] = result[index * STEPS : (index + 1) * STEPS, :]
    span = pl.ds(groups[0] * STEPS * stride, len(groups) * STEPS * stride)
    copies = [pltpu.make_async_copy(made.at[f], outs[f].at[span, :], sems.at[f]) for f in range(FIELDS)]
    for copy in copies:
        copy.start()
    for copy in copies:
        copy.wait()


def per_device(state, dir_one, dir_two, feed, kill, tiles, tile_cols, send_rows, send_count):
    steps, _, cells = state.shape
    cell_blocks = cells // LANES
    stride = 2 * cell_blocks
    blocks, per_row = tiles.shape[:2]
    slot_rows = send_rows.shape[2]
    size_dom = lax.axis_size("dom")

    by_route = {}
    for slot, offset in enumerate(OFFSETS):
        by_route.setdefault(offset % size_dom, []).append(slot)
    slot_groups = sorted(by_route.values(), key=lambda slots: -len(slots))

    def view(array):
        array = array.reshape(steps, 2, cell_blocks, LANES).transpose(0, 2, 1, 3)
        return array.reshape(steps * stride, LANES)

    def unview(array):
        array = array.reshape(steps, cell_blocks, 2, LANES).transpose(0, 2, 1, 3)
        return array.reshape(steps, 2, cells)

    fields = [view(state), view(dir_one), view(dir_two)]
    rows = send_rows.reshape(send_rows.shape[1:])
    counts = send_count
    cols = tile_cols.T
    feed = feed.reshape(cell_blocks, LANES)
    kill = kill.reshape(cell_blocks, LANES)

    vmem = pl.BlockSpec(memory_space=VMEM)
    smem = pl.BlockSpec(memory_space=SMEM)
    anywhere = pl.BlockSpec(memory_space=pl.ANY)
    params = pltpu.CompilerParams(vmem_limit_bytes=16 * 1024 * 1024)

    groups = tuple(range(steps // STEPS))
    late, middle, lead = groups[:1], groups[1:-1], groups[-1:]
    most = middle + lead
    wide, *narrow = slot_groups
    others = [slot for slots in narrow for slot in slots]

    def rows_of(part):
        return len(part) * FIELDS * 2 * STEPS

    def f32(*shape):
        return jax.ShapeDtypeStruct(shape, F32)

    def parts_of(part):
        return jax.ShapeDtypeStruct((cell_blocks, 2 * rows_of(part), LANES), BF16)

    def sends_of(part, chosen):
        return [f32(rows_of(part), len(slots) * slot_rows) for slots in chosen]

    def cost(flops, moved):
        return pl.CostEstimate(flops=flops, bytes_accessed=moved, transcendentals=0)

    def in_hbm(*arrays):
        return [pltpu.with_memory_space_constraint(array, pltpu.HBM) for array in arrays]

    def send_to(send, slots):
        return shift_along(send, "dom", OFFSETS[slots[0]])

    hbm = pl.BlockSpec(memory_space=pltpu.HBM)
    size = rows_of(groups)
    every = len(OFFSETS) * slot_rows
    wide_width = len(wide) * slot_rows
    send, held, listed, last = pl.pallas_call(
        functools.partial(first_kernel, lead, wide, cell_blocks),
        out_shape=[
            f32(rows_of(lead), wide_width),
            f32(FIELDS, steps * stride, LANES),
            jax.ShapeDtypeStruct(rows.shape, jnp.int32),
            f32(FIELDS * stride, LANES),
        ],
        in_specs=[hbm] * (FIELDS + 2),
        out_specs=[vmem] * 4,
        scratch_shapes=[
            VMEM(rows.shape, jnp.int32),
            VMEM(counts.shape, jnp.int32),
            pltpu.SemaphoreType.DMA((2 * FIELDS + 2,)),
        ],
        compiler_params=params,
        cost_estimate=cost(4 * rows_of(lead) * cells * wide_width, 8 * size * cells),
        name="gather_first",
    )(*in_hbm(*fields, rows, counts))
    wide_lead = send_to(send, wide)
    send, *sends, most_parts = pl.pallas_call(
        functools.partial(second_kernel, most, middle, wide, others, cell_blocks),
        out_shape=sends_of(middle, [wide]) + sends_of(most, narrow) + [parts_of(most)],
        in_specs=[vmem] * 2,
        out_specs=[vmem] * (len(narrow) + 2),
        scratch_shapes=[VMEM((cells, every), BF16)],
        compiler_params=params,
        cost_estimate=cost(4 * rows_of(most) * cells * every, 8 * size * cells),
        name="gather_second",
    )(held, listed)
    wide_middle = send_to(send, wide)
    prev = shift_along(last, "tm", 1)
    narrow_most = [send_to(part, slots) for part, slots in zip(sends, narrow)]
    *sends, late_parts = pl.pallas_call(
        functools.partial(third_kernel, late, wide, others, cell_blocks),
        out_shape=sends_of(late, slot_groups) + [parts_of(late)],
        in_specs=[vmem] * 3,
        out_specs=[vmem] * (len(slot_groups) + 1),
        scratch_shapes=[VMEM((cells, every), BF16)],
        compiler_params=params,
        cost_estimate=cost(4 * rows_of(late) * cells * every, 8 * size * cells),
        name="gather_third",
    )(held, prev, listed)
    base_most, base_late, split_tiles = pl.pallas_call(
        functools.partial(local_kernel, (most, late), cell_blocks),
        out_shape=[
            f32(cell_blocks, rows_of(most), LANES),
            f32(cell_blocks, rows_of(late), LANES),
            jax.ShapeDtypeStruct((blocks, per_row * LANES, 2 * LANES), BF16),
        ],
        in_specs=[vmem] * 2 + [hbm] * 3,
        out_specs=[vmem] * 3,
        scratch_shapes=[
            VMEM(feed.shape, F32),
            VMEM(kill.shape, F32),
            VMEM(tiles.shape, F32),
            pltpu.SemaphoreType.DMA((3,)),
        ],
        compiler_params=params,
        cost_estimate=cost(60 * size * cells, 8 * tiles.size),
        name="local_terms",
    )(held, prev, *in_hbm(feed, kill, tiles))

    arrived_late = [send_to(sends[0], wide)]
    sends[1], wide_lead = lax.optimization_barrier((sends[1], wide_lead))
    arrived_late.append(send_to(sends[1], slot_groups[1]))
    for number in range(2, len(sends)):
        sends[number], wide_middle, split_tiles = lax.optimization_barrier((sends[number], wide_middle, split_tiles))
        arrived_late.append(send_to(sends[number], slot_groups[number]))

    def apply(part, base, parts, transfers, outs):
        inputs = [cols, split_tiles, base, parts, *[array for array, _, _ in transfers]]
        received = [(slots, row) for _, slots, row in transfers]
        return pl.pallas_call(
            functools.partial(apply_kernel, part, received, cell_blocks, blocks, per_row, len(outs)),
            out_shape=[f32(steps * stride, LANES)] * FIELDS,
            in_specs=[vmem] * len(inputs) + [anywhere] * len(outs),
            out_specs=[anywhere] * FIELDS,
            input_output_aliases={len(inputs) + f: f for f in range(len(outs))},
            scratch_shapes=[
                VMEM((cell_blocks + every // LANES, 2 * rows_of(part), LANES), BF16),
                VMEM((FIELDS, len(part) * STEPS * stride, LANES), F32),
                pltpu.SemaphoreType.DMA((FIELDS,)),
            ],
            compiler_params=params,
            cost_estimate=cost(8 * rows_of(part) * blocks * per_row * LANES * LANES, 16 * rows_of(part) * cells),
            name="apply_tiles",
        )(*inputs, *outs)

    transfers = [(wide_middle, wide, 0), (wide_lead, wide, rows_of(middle))]
    transfers += [(array, slots, 0) for array, slots in zip(narrow_most, narrow)]
    outs = apply(most, base_most, most_parts, transfers, [])
    transfers = [(array, slots, 0) for array, slots in zip(arrived_late, slot_groups)]
    outs = apply(late, base_late, late_parts, transfers, outs)
    return tuple(unview(out) for out in outs)


def solution(mesh):
    fields = P(("group", "tm"), None, "dom")
    in_specs = (
        fields,
        fields,
        fields,
        P("dom"),
        P("dom"),
        P("dom", None, None, None),
        P("dom", None),
        P("dom", None, None),
        P("dom", None),
    )
    return jax.shard_map(
        per_device, mesh=mesh, in_specs=in_specs, out_specs=(fields, fields, fields), check_vma=False
    )
```

```python
import functools

import jax
import jax.numpy as jnp
from jax import lax
from jax.experimental import pallas as pl
from jax.experimental.pallas import tpu as pltpu
from jax.sharding import PartitionSpec as P

OFFSETS = (1, -1, 2, -2)
time_step = 0.5
spread_u = 1.0
spread_v = 0.5
LANES = 128
STEPS = 8
HALF = 4
FIELDS = 3
VMEM = pltpu.VMEM
SMEM = pltpu.SMEM
F32 = jnp.float32
BF16 = jnp.bfloat16


def shift_along(block, axis, distance):
    size = lax.axis_size(axis)
    return lax.ppermute(block, axis, [((i - distance) % size, i) for i in range(size)])


def steps_at(ref, group, cell_block, species, stride):
    return ref[pl.ds(group * STEPS * stride + cell_block * 2 + species, STEPS, stride=stride), :]


def steps_before(ref, prev_ref, field, group, cell_block, species, stride):
    offset = cell_block * 2 + species
    if group > 0:
        return ref[pl.ds((group * STEPS - 1) * stride + offset, STEPS, stride=stride), :]
    now = steps_at(ref, 0, cell_block, species, stride)
    row = field * stride + offset
    first = jnp.broadcast_to(prev_ref[row : row + 1, :], now.shape)
    index = lax.broadcasted_iota(jnp.int32, now.shape, 0)
    return jnp.where(index == 0, first, pltpu.roll(now, 1, 0))


def split(values):
    high = values.astype(BF16)
    return high, (values - high.astype(F32)).astype(BF16)


def scaled_sum(ref, prev_ref, field, group, cell_block, species, stride):
    now = steps_at(ref, group, cell_block, species, stride)
    before = steps_before(ref, prev_ref, field, group, cell_block, species, stride)
    return (now + before) * (-0.5 * (spread_u, spread_v)[species])


def summed_parts(groups, cell_blocks, fields, prev, parts_ref, high_row, low_row):
    stride = 2 * cell_blocks
    for place, group in enumerate(groups):
        for field in range(FIELDS):
            row = (place * FIELDS + field) * 2 * STEPS
            for block in range(cell_blocks):
                both = [scaled_sum(fields[field], prev, field, group, block, species, stride) for species in range(2)]
                high, low = split(jnp.concatenate(both, axis=0))
                parts_ref[block, high_row + row : high_row + row + 2 * STEPS, :] = high
                parts_ref[block, low_row + row : low_row + row + 2 * STEPS, :] = low


def choose_rows(slots, listed_ref, choose):
    cells = choose.shape[0]
    slot_rows = listed_ref.shape[1]
    cell = lax.broadcasted_iota(jnp.int32, (LANES, slot_rows), 0)
    for place, slot in enumerate(slots):
        listed = listed_ref[slot : slot + 1, :]
        for start in range(0, cells, LANES):
            hit = cell == listed - start
            choose[start : start + LANES, place * slot_rows : (place + 1) * slot_rows] = jnp.where(
                hit, 1.0, 0.0
            ).astype(BF16)


def take_rows(parts, choose, sends):
    size = parts.shape[0] // 2
    start = 0
    for send in sends:
        width = send.shape[1]
        taken = jnp.dot(parts, choose[:, start : start + width], preferred_element_type=F32)
        send[...] = taken[:size] + taken[size:]
        start += width


def side_by_side(parts_ref, rows):
    blocks = [
        jnp.concatenate([parts_ref[b, start : start + count, :] for start, count in rows], axis=0)
        for b in range(parts_ref.shape[0])
    ]
    return jnp.concatenate(blocks, axis=1)


def first_kernel(lead, slots, cell_blocks, *refs):
    refs = list(refs)
    sources = [refs.pop(0) for _ in range(FIELDS)]
    rows_hbm, count_hbm, send, listed, near, rows_ref, count_ref, sems = refs
    stride = 2 * cell_blocks
    first = (lead[0] * STEPS - 1) * stride
    small = [
        pltpu.make_async_copy(rows_hbm, rows_ref, sems.at[FIELDS]),
        pltpu.make_async_copy(count_hbm, count_ref, sems.at[FIELDS + 1]),
    ]
    needed = [
        pltpu.make_async_copy(sources[f].at[pl.ds(first, near.shape[1]), :], near.at[f], sems.at[f])
        for f in range(FIELDS)
    ]
    for copy in small + needed:
        copy.start()
    for copy in small:
        copy.wait()
    lane = lax.broadcasted_iota(jnp.int32, rows_ref.shape, 1)
    columns = {}
    for slot in range(rows_ref.shape[0]):
        live = lane[slot : slot + 1] < count_ref[:, slot : slot + 1]
        row = jnp.where(live, rows_ref[slot : slot + 1, :], -1)
        listed[slot : slot + 1, :] = row
        columns[slot] = [row[:, start : start + LANES] for start in range(0, row.shape[1], LANES)]
    columns = [jnp.broadcast_to(column, (STEPS, LANES)) for slot in slots for column in columns[slot]]
    lanes = [column & (LANES - 1) for column in columns]
    blocks = [column >> 7 for column in columns]
    for copy in needed:
        copy.wait()
    for place in range(len(lead)):
        for field in range(FIELDS):
            for species, spread in enumerate((spread_u, spread_v)):
                row = ((place * FIELDS + field) * 2 + species) * STEPS
                sums = []
                for block in range(cell_blocks):
                    at = place * STEPS * stride + block * 2 + species
                    before = near[field, pl.ds(at, STEPS, stride=stride), :]
                    now = near[field, pl.ds(at + stride, STEPS, stride=stride), :]
                    sums.append((now + before) * (-0.5 * spread))
                for number in range(len(columns)):
                    found = jnp.zeros((STEPS, LANES), F32)
                    for block in range(cell_blocks):
                        taken = jnp.take_along_axis(sums[block], lanes[number], axis=1, mode="promise_in_bounds")
                        found = jnp.where(blocks[number] == block, taken, found)
                    send[row : row + STEPS, number * LANES : (number + 1) * LANES] = found


def second_kernel(most, middle, wide, others, cell_blocks, *refs):
    refs = list(refs)
    sources = [refs.pop(0) for _ in range(FIELDS)]
    listed, send, *sends, parts_ref, held, last, choose, sems = refs
    copies = [pltpu.make_async_copy(sources[f], held.at[f], sems.at[f]) for f in range(FIELDS)]
    for copy in copies:
        copy.start()
    choose_rows(wide + others, listed, choose)
    for copy in copies:
        copy.wait()
    stride = 2 * cell_blocks
    size = parts_ref.shape[1] // 2
    middle_size = size * len(middle) // len(most)
    summed_parts(most, cell_blocks, [held.at[f] for f in range(FIELDS)], None, parts_ref, 0, size)
    width = send.shape[1]
    take_rows(side_by_side(parts_ref, [(0, middle_size), (size, middle_size)]), choose, [send])
    take_rows(side_by_side(parts_ref, [(0, 2 * size)]), choose.at[:, width:], sends)
    for field in range(FIELDS):
        last[field * stride : (field + 1) * stride, :] = held[field, -stride:, :]


def third_kernel(late, wide, others, cell_blocks, held, prev, listed, *refs):
    *sends, parts_ref, choose = refs
    size = parts_ref.shape[1] // 2
    choose_rows(wide + others, listed, choose)
    summed_parts(late, cell_blocks, [held.at[f] for f in range(FIELDS)], prev, parts_ref, 0, size)
    take_rows(side_by_side(parts_ref, [(0, 2 * size)]), choose, sends)


def pointwise(u, v, du, dv, ddu, ddv, feed, total):
    square = v * v
    product = u * square
    twice = 2.0 * u * v
    outs = [feed * (1.0 - u) - product, product - total * v]
    for first, second in ((du, dv), (ddu, ddv)):
        react = square * first + twice * second
        outs += [-react - feed * first, react - total * second]
    return outs


def local_kernel(
    chunks, cell_blocks, held, prev, feed_hbm, kill_hbm, tiles_hbm, base_one, base_two, split_tiles, feed_ref, kill_ref, tiles, sems
):
    copies = [
        pltpu.make_async_copy(feed_hbm, feed_ref, sems.at[0]),
        pltpu.make_async_copy(kill_hbm, kill_ref, sems.at[1]),
        pltpu.make_async_copy(tiles_hbm, tiles, sems.at[2]),
    ]
    for copy in copies:
        copy.start()
    for copy in copies[:2]:
        copy.wait()
    fields = [held.at[f] for f in range(FIELDS)]
    stride = 2 * cell_blocks
    pairs = [(f, s) for f in range(FIELDS) for s in range(2)]
    for base, groups in zip((base_one, base_two), chunks):
        for place, group in enumerate(groups):
            for block in range(cell_blocks):
                feed = feed_ref[block : block + 1, :]
                total = feed + kill_ref[block : block + 1, :]
                now = [steps_at(fields[f], group, block, s, stride) for f, s in pairs]
                before = [steps_before(fields[f], prev, f, group, block, s, stride) for f, s in pairs]
                rate_now = pointwise(*now, feed, total)
                rate_before = pointwise(*before, feed, total)
                for index in range(2 * FIELDS):
                    row = (place * FIELDS * 2 + index) * STEPS
                    base[block, row : row + STEPS, :] = (now[index] - before[index]) * (1.0 / time_step) - 0.5 * (
                        rate_now[index] + rate_before[index]
                    )
    copies[2].wait()
    blocks, per_row = tiles.shape[:2]
    for block in range(blocks):
        for k in range(per_row):
            high, low = split(jnp.transpose(tiles[block, k]))
            split_tiles[block, k * LANES : (k + 1) * LANES, :LANES] = high
            split_tiles[block, k * LANES : (k + 1) * LANES, LANES:] = low


def apply_kernel(groups, received, cell_blocks, blocks, per_row, held_back, *refs):
    refs = list(refs)
    cols_ref, split_tiles, base, parts_ref = [refs.pop(0) for _ in range(4)]
    arrived = [refs.pop(0) for _ in received]
    refs = refs[held_back:]
    outs = [refs.pop(0) for _ in range(FIELDS)]
    extended, made, sems = refs
    stride = 2 * cell_blocks
    size = base.shape[1]
    cols = cols_ref[...]
    extended[:cell_blocks] = parts_ref[...]
    for ref, (slots, row) in zip(arrived, received):
        count, width = ref.shape
        per_slot = width // len(slots) // LANES
        for place, slot in enumerate(slots):
            for b in range(per_slot):
                lane = (place * per_slot + b) * LANES
                high, low = split(ref[:, lane : lane + LANES])
                extended[cell_blocks + slot * per_slot + b, row : row + count, :] = high
                extended[cell_blocks + slot * per_slot + b, size + row : size + row + count, :] = low
    steps = len(groups) * STEPS
    copies = []
    for block in range(blocks):
        chosen = jnp.concatenate([extended[cols[k, block]] for k in range(per_row)], axis=1)
        product = jnp.dot(chosen, split_tiles[block], preferred_element_type=F32)
        product = product[:, :LANES] + product[:, LANES:]
        result = base[block] + (product[:size] + product[size:])
        for index in range(size // STEPS):
            group, field, species = index // (2 * FIELDS), index // 2 % FIELDS, index % 2
            at = group * STEPS * stride + block * 2 + species
            made[field, pl.ds(at, STEPS, stride=stride), :] = result[index * STEPS : (index + 1) * STEPS, :]
        if (block + 1) % HALF == 0:
            span = pl.ds((block + 1 - HALF) * 2, 2 * HALF)
            for field in range(FIELDS):
                copy = pltpu.make_async_copy(
                    made.at[field].reshape(steps, stride, LANES).at[:, span, :],
                    outs[field].at[pl.ds(groups[0] * STEPS, steps), span, :],
                    sems.at[field, block // HALF],
                )
                copy.start()
                copies.append(copy)
    for copy in copies:
        copy.wait()


def per_device(state, dir_one, dir_two, feed, kill, tiles, tile_cols, send_rows, send_count):
    steps, _, cells = state.shape
    cell_blocks = cells // LANES
    stride = 2 * cell_blocks
    blocks, per_row = tiles.shape[:2]
    slot_rows = send_rows.shape[2]
    size_dom = lax.axis_size("dom")

    by_route = {}
    for slot, offset in enumerate(OFFSETS):
        by_route.setdefault(offset % size_dom, []).append(slot)
    slot_groups = sorted(by_route.values(), key=lambda slots: -len(slots))

    def view(array):
        array = array.reshape(steps, 2, cell_blocks, LANES).transpose(0, 2, 1, 3)
        return array.reshape(steps * stride, LANES)

    def unview(array):
        array = array.reshape(steps, cell_blocks, 2, LANES).transpose(0, 2, 1, 3)
        return array.reshape(steps, 2, cells)

    fields = [view(state), view(dir_one), view(dir_two)]
    rows = send_rows.reshape(send_rows.shape[1:])
    counts = send_count
    cols = tile_cols.T
    feed = feed.reshape(cell_blocks, LANES)
    kill = kill.reshape(cell_blocks, LANES)

    vmem = pl.BlockSpec(memory_space=VMEM)
    smem = pl.BlockSpec(memory_space=SMEM)
    anywhere = pl.BlockSpec(memory_space=pl.ANY)
    params = pltpu.CompilerParams(vmem_limit_bytes=16 * 1024 * 1024)

    groups = tuple(range(steps // STEPS))
    late, middle, lead = groups[:1], groups[1:-1], groups[-1:]
    most = middle + lead
    wide, *narrow = slot_groups
    others = [slot for slots in narrow for slot in slots]

    def rows_of(part):
        return len(part) * FIELDS * 2 * STEPS

    def f32(*shape):
        return jax.ShapeDtypeStruct(shape, F32)

    def parts_of(part):
        return jax.ShapeDtypeStruct((cell_blocks, 2 * rows_of(part), LANES), BF16)

    def sends_of(part, chosen):
        return [f32(rows_of(part), len(slots) * slot_rows) for slots in chosen]

    def cost(flops, moved):
        return pl.CostEstimate(flops=flops, bytes_accessed=moved, transcendentals=0)

    def in_hbm(*arrays):
        return [pltpu.with_memory_space_constraint(array, pltpu.HBM) for array in arrays]

    def send_to(send, slots):
        return shift_along(send, "dom", OFFSETS[slots[0]])

    hbm = pl.BlockSpec(memory_space=pltpu.HBM)
    size = rows_of(groups)
    every = len(OFFSETS) * slot_rows
    wide_width = len(wide) * slot_rows
    first_fields = in_hbm(*fields)
    send, listed = pl.pallas_call(
        functools.partial(first_kernel, lead, wide, cell_blocks),
        out_shape=[f32(rows_of(lead), wide_width), jax.ShapeDtypeStruct(rows.shape, jnp.int32)],
        in_specs=[hbm] * (FIELDS + 2),
        out_specs=[vmem] * 2,
        scratch_shapes=[
            VMEM((FIELDS, (len(lead) * STEPS + 1) * stride, LANES), F32),
            VMEM(rows.shape, jnp.int32),
            VMEM(counts.shape, jnp.int32),
            pltpu.SemaphoreType.DMA((FIELDS + 2,)),
        ],
        compiler_params=params,
        cost_estimate=cost(4 * rows_of(lead) * cells * wide_width, 8 * size * cells),
        name="gather_first",
    )(*first_fields, *in_hbm(rows, counts))
    wide_lead = send_to(send, wide)
    send, *sends, most_parts, held, last = pl.pallas_call(
        functools.partial(second_kernel, most, middle, wide, others, cell_blocks),
        out_shape=sends_of(middle, [wide])
        + sends_of(most, narrow)
        + [parts_of(most), f32(FIELDS, steps * stride, LANES), f32(FIELDS * stride, LANES)],
        in_specs=[hbm] * FIELDS + [vmem],
        out_specs=[vmem] * (len(narrow) + 4),
        scratch_shapes=[VMEM((cells, every), BF16), pltpu.SemaphoreType.DMA((FIELDS,))],
        compiler_params=params,
        cost_estimate=cost(4 * rows_of(most) * cells * every, 8 * size * cells),
        name="gather_second",
    )(*first_fields, listed)
    wide_middle = send_to(send, wide)
    prev = shift_along(last, "tm", 1)
    narrow_most = [send_to(part, slots) for part, slots in zip(sends, narrow)]
    *sends, late_parts = pl.pallas_call(
        functools.partial(third_kernel, late, wide, others, cell_blocks),
        out_shape=sends_of(late, slot_groups) + [parts_of(late)],
        in_specs=[vmem] * 3,
        out_specs=[vmem] * (len(slot_groups) + 1),
        scratch_shapes=[VMEM((cells, every), BF16)],
        compiler_params=params,
        cost_estimate=cost(4 * rows_of(late) * cells * every, 8 * size * cells),
        name="gather_third",
    )(held, prev, listed)
    base_most, base_late, split_tiles = pl.pallas_call(
        functools.partial(local_kernel, (most, late), cell_blocks),
        out_shape=[
            f32(cell_blocks, rows_of(most), LANES),
            f32(cell_blocks, rows_of(late), LANES),
            jax.ShapeDtypeStruct((blocks, per_row * LANES, 2 * LANES), BF16),
        ],
        in_specs=[vmem] * 2 + [hbm] * 3,
        out_specs=[vmem] * 3,
        scratch_shapes=[
            VMEM(feed.shape, F32),
            VMEM(kill.shape, F32),
            VMEM(tiles.shape, F32),
            pltpu.SemaphoreType.DMA((3,)),
        ],
        compiler_params=params,
        cost_estimate=cost(60 * size * cells, 8 * tiles.size),
        name="local_terms",
    )(held, prev, *in_hbm(feed, kill, tiles))

    arrived_late = [send_to(sends[0], wide)]
    sends[1], wide_lead = lax.optimization_barrier((sends[1], wide_lead))
    arrived_late.append(send_to(sends[1], slot_groups[1]))
    for number in range(2, len(sends)):
        sends[number], wide_middle, split_tiles = lax.optimization_barrier((sends[number], wide_middle, split_tiles))
        arrived_late.append(send_to(sends[number], slot_groups[number]))

    def apply(part, base, parts, transfers, outs):
        inputs = [cols, split_tiles, base, parts, *[array for array, _, _ in transfers]]
        received = [(slots, row) for _, slots, row in transfers]
        return pl.pallas_call(
            functools.partial(apply_kernel, part, received, cell_blocks, blocks, per_row, len(outs)),
            out_shape=[f32(steps, stride, LANES)] * FIELDS,
            in_specs=[vmem] * len(inputs) + [anywhere] * len(outs),
            out_specs=[anywhere] * FIELDS,
            input_output_aliases={len(inputs) + f: f for f in range(len(outs))},
            scratch_shapes=[
                VMEM((cell_blocks + every // LANES, 2 * rows_of(part), LANES), BF16),
                VMEM((FIELDS, len(part) * STEPS * stride, LANES), F32),
                pltpu.SemaphoreType.DMA((FIELDS, blocks // HALF)),
            ],
            compiler_params=params,
            cost_estimate=cost(8 * rows_of(part) * blocks * per_row * LANES * LANES, 16 * rows_of(part) * cells),
            name="apply_tiles",
        )(*inputs, *outs)

    transfers = [(wide_middle, wide, 0), (wide_lead, wide, rows_of(middle))]
    transfers += [(array, slots, 0) for array, slots in zip(narrow_most, narrow)]
    outs = apply(most, base_most, most_parts, transfers, [])
    transfers = [(array, slots, 0) for array, slots in zip(arrived_late, slot_groups)]
    outs = apply(late, base_late, late_parts, transfers, outs)
    return tuple(unview(out) for out in outs)


def solution(mesh):
    fields = P(("group", "tm"), None, "dom")
    in_specs = (
        fields,
        fields,
        fields,
        P("dom"),
        P("dom"),
        P("dom", None, None, None),
        P("dom", None),
        P("dom", None, None),
        P("dom", None),
    )
    return jax.shard_map(
        per_device, mesh=mesh, in_specs=in_specs, out_specs=(fields, fields, fields), check_vma=False
    )
```

```python
import functools

import jax
import jax.numpy as jnp
from jax import lax
from jax.experimental import pallas as pl
from jax.experimental.pallas import tpu as pltpu
from jax.sharding import PartitionSpec as P

OFFSETS = (1, -1, 2, -2)
time_step = 0.5
spread_u = 1.0
spread_v = 0.5
LANES = 128
STEPS = 8
FIELDS = 3
VMEM = pltpu.VMEM
SMEM = pltpu.SMEM
F32 = jnp.float32
BF16 = jnp.bfloat16


def shift_along(block, axis, distance):
    size = lax.axis_size(axis)
    return lax.ppermute(block, axis, [((i - distance) % size, i) for i in range(size)])


def steps_at(ref, group, cell_block, species, stride):
    return ref[pl.ds(group * STEPS * stride + cell_block * 2 + species, STEPS, stride=stride), :]


def steps_before(ref, prev_ref, field, group, cell_block, species, stride):
    offset = cell_block * 2 + species
    if group > 0:
        return ref[pl.ds((group * STEPS - 1) * stride + offset, STEPS, stride=stride), :]
    now = steps_at(ref, 0, cell_block, species, stride)
    row = field * stride + offset
    first = jnp.broadcast_to(prev_ref[row : row + 1, :], now.shape)
    index = lax.broadcasted_iota(jnp.int32, now.shape, 0)
    return jnp.where(index == 0, first, pltpu.roll(now, 1, 0))


def split(values):
    high = values.astype(BF16)
    return high, (values - high.astype(F32)).astype(BF16)


def scaled_sum(ref, prev_ref, field, group, cell_block, species, stride):
    now = steps_at(ref, group, cell_block, species, stride)
    before = steps_before(ref, prev_ref, field, group, cell_block, species, stride)
    return (now + before) * (-0.5 * (spread_u, spread_v)[species])


def summed_parts(groups, cell_blocks, fields, prev, parts_ref, high_row, low_row):
    stride = 2 * cell_blocks
    for place, group in enumerate(groups):
        for field in range(FIELDS):
            row = (place * FIELDS + field) * 2 * STEPS
            for block in range(cell_blocks):
                both = [scaled_sum(fields[field], prev, field, group, block, species, stride) for species in range(2)]
                high, low = split(jnp.concatenate(both, axis=0))
                parts_ref[block, high_row + row : high_row + row + 2 * STEPS, :] = high
                parts_ref[block, low_row + row : low_row + row + 2 * STEPS, :] = low


def choose_rows(slots, listed_ref, choose):
    cells = choose.shape[0]
    slot_rows = listed_ref.shape[1]
    cell = lax.broadcasted_iota(jnp.int32, (LANES, slot_rows), 0)
    for place, slot in enumerate(slots):
        listed = listed_ref[slot : slot + 1, :]
        for start in range(0, cells, LANES):
            hit = cell == listed - start
            choose[start : start + LANES, place * slot_rows : (place + 1) * slot_rows] = jnp.where(
                hit, 1.0, 0.0
            ).astype(BF16)


def take_rows(parts, choose, sends):
    size = parts.shape[0] // 2
    start = 0
    for send in sends:
        width = send.shape[1]
        taken = jnp.dot(parts, choose[:, start : start + width], preferred_element_type=F32)
        send[...] = taken[:size] + taken[size:]
        start += width


def side_by_side(parts_ref, rows):
    blocks = [
        jnp.concatenate([parts_ref[b, start : start + count, :] for start, count in rows], axis=0)
        for b in range(parts_ref.shape[0])
    ]
    return jnp.concatenate(blocks, axis=1)


def first_kernel(lead, slots, cell_blocks, *refs):
    refs = list(refs)
    sources = [refs.pop(0) for _ in range(FIELDS)]
    rows_hbm, count_hbm, send, held, listed, last, rows_ref, count_ref, sems = refs
    stride = 2 * cell_blocks
    early = (lead[0] * STEPS - 1) * stride
    late = held.shape[1] - early
    small = [
        pltpu.make_async_copy(rows_hbm, rows_ref, sems.at[2 * FIELDS]),
        pltpu.make_async_copy(count_hbm, count_ref, sems.at[2 * FIELDS + 1]),
    ]
    needed = [
        pltpu.make_async_copy(sources[f].at[pl.ds(early, late), :], held.at[f, pl.ds(early, late), :], sems.at[f])
        for f in range(FIELDS)
    ]
    others = [
        pltpu.make_async_copy(sources[f].at[pl.ds(0, early), :], held.at[f, pl.ds(0, early), :], sems.at[FIELDS + f])
        for f in range(FIELDS)
    ]
    for copy in small + needed + others:
        copy.start()
    for copy in small:
        copy.wait()
    lane = lax.broadcasted_iota(jnp.int32, rows_ref.shape, 1)
    for slot in range(rows_ref.shape[0]):
        listed[slot : slot + 1, :] = jnp.where(
            lane[slot : slot + 1] < count_ref[:, slot : slot + 1], rows_ref[slot : slot + 1, :], -1
        )
    for copy in needed:
        copy.wait()
    columns = [
        listed[slot : slot + 1, start : start + LANES]
        for slot in slots
        for start in range(0, listed.shape[1], LANES)
    ]
    columns = [jnp.broadcast_to(column, (STEPS, LANES)) for column in columns]
    for place, group in enumerate(lead):
        for field in range(FIELDS):
            for species in range(2):
                row = ((place * FIELDS + field) * 2 + species) * STEPS
                sums = [
                    scaled_sum(held.at[field], None, field, group, block, species, stride) for block in range(cell_blocks)
                ]
                for number, column in enumerate(columns):
                    lanes = column & (LANES - 1)
                    found = jnp.zeros((STEPS, LANES), F32)
                    for block in range(cell_blocks):
                        taken = jnp.take_along_axis(sums[block], lanes, axis=1, mode="promise_in_bounds")
                        found = jnp.where(column >> 7 == block, taken, found)
                    send[row : row + STEPS, number * LANES : (number + 1) * LANES] = found
    for field in range(FIELDS):
        last[field * stride : (field + 1) * stride, :] = held[field, -stride:, :]
    for copy in others:
        copy.wait()


def second_kernel(most, middle, wide, others, cell_blocks, held, listed, send, *refs):
    *sends, parts_ref, choose = refs
    size = parts_ref.shape[1] // 2
    middle_size = size * len(middle) // len(most)
    choose_rows(wide + others, listed, choose)
    summed_parts(most, cell_blocks, [held.at[f] for f in range(FIELDS)], None, parts_ref, 0, size)
    width = send.shape[1]
    take_rows(side_by_side(parts_ref, [(0, middle_size), (size, middle_size)]), choose, [send])
    take_rows(side_by_side(parts_ref, [(0, 2 * size)]), choose.at[:, width:], sends)


def third_kernel(late, wide, others, cell_blocks, held, prev, listed, *refs):
    *sends, parts_ref, choose = refs
    size = parts_ref.shape[1] // 2
    choose_rows(wide + others, listed, choose)
    summed_parts(late, cell_blocks, [held.at[f] for f in range(FIELDS)], prev, parts_ref, 0, size)
    take_rows(side_by_side(parts_ref, [(0, 2 * size)]), choose, sends)


def pointwise(u, v, du, dv, ddu, ddv, feed, total):
    square = v * v
    product = u * square
    twice = 2.0 * u * v
    outs = [feed * (1.0 - u) - product, product - total * v]
    for first, second in ((du, dv), (ddu, ddv)):
        react = square * first + twice * second
        outs += [-react - feed * first, react - total * second]
    return outs


def local_kernel(
    chunks, cell_blocks, held, prev, feed_hbm, kill_hbm, tiles_hbm, base_one, base_two, split_tiles, feed_ref, kill_ref, tiles, sems
):
    copies = [
        pltpu.make_async_copy(feed_hbm, feed_ref, sems.at[0]),
        pltpu.make_async_copy(kill_hbm, kill_ref, sems.at[1]),
        pltpu.make_async_copy(tiles_hbm, tiles, sems.at[2]),
    ]
    for copy in copies:
        copy.start()
    for copy in copies[:2]:
        copy.wait()
    fields = [held.at[f] for f in range(FIELDS)]
    stride = 2 * cell_blocks
    pairs = [(f, s) for f in range(FIELDS) for s in range(2)]
    for base, groups in zip((base_one, base_two), chunks):
        for place, group in enumerate(groups):
            for block in range(cell_blocks):
                feed = feed_ref[block : block + 1, :]
                total = feed + kill_ref[block : block + 1, :]
                now = [steps_at(fields[f], group, block, s, stride) for f, s in pairs]
                before = [steps_before(fields[f], prev, f, group, block, s, stride) for f, s in pairs]
                rate_now = pointwise(*now, feed, total)
                rate_before = pointwise(*before, feed, total)
                for index in range(2 * FIELDS):
                    row = (place * FIELDS * 2 + index) * STEPS
                    base[block, row : row + STEPS, :] = (now[index] - before[index]) * (1.0 / time_step) - 0.5 * (
                        rate_now[index] + rate_before[index]
                    )
    copies[2].wait()
    blocks, per_row = tiles.shape[:2]
    for block in range(blocks):
        for k in range(per_row):
            high, low = split(jnp.transpose(tiles[block, k]))
            split_tiles[block, k * LANES : (k + 1) * LANES, :LANES] = high
            split_tiles[block, k * LANES : (k + 1) * LANES, LANES:] = low


def apply_kernel(groups, received, cell_blocks, blocks, per_row, held_back, *refs):
    refs = list(refs)
    cols_ref, split_tiles, base, parts_ref = [refs.pop(0) for _ in range(4)]
    arrived = [refs.pop(0) for _ in received]
    refs = refs[held_back:]
    outs = [refs.pop(0) for _ in range(FIELDS)]
    extended, made, sems = refs
    stride = 2 * cell_blocks
    size = base.shape[1]
    cols = cols_ref[...]
    extended[:cell_blocks] = parts_ref[...]
    for ref, (slots, row) in zip(arrived, received):
        count, width = ref.shape
        per_slot = width // len(slots) // LANES
        for place, slot in enumerate(slots):
            for b in range(per_slot):
                lane = (place * per_slot + b) * LANES
                high, low = split(ref[:, lane : lane + LANES])
                extended[cell_blocks + slot * per_slot + b, row : row + count, :] = high
                extended[cell_blocks + slot * per_slot + b, size + row : size + row + count, :] = low
    for block in range(blocks):
        chosen = jnp.concatenate([extended[cols[k, block]] for k in range(per_row)], axis=1)
        product = jnp.dot(chosen, split_tiles[block], preferred_element_type=F32)
        product = product[:, :LANES] + product[:, LANES:]
        result = base[block] + (product[:size] + product[size:])
        for index in range(size // STEPS):
            group, field, species = index // (2 * FIELDS), index // 2 % FIELDS, index % 2
            at = group * STEPS * stride + block * 2 + species
            made[field, pl.ds(at, STEPS, stride=stride), :] = result[index * STEPS : (index + 1) * STEPS, :]
    span = pl.ds(groups[0] * STEPS * stride, len(groups) * STEPS * stride)
    copies = [pltpu.make_async_copy(made.at[f], outs[f].at[span, :], sems.at[f]) for f in range(FIELDS)]
    for copy in copies:
        copy.start()
    for copy in copies:
        copy.wait()


def per_device(state, dir_one, dir_two, feed, kill, tiles, tile_cols, send_rows, send_count):
    steps, _, cells = state.shape
    cell_blocks = cells // LANES
    stride = 2 * cell_blocks
    blocks, per_row = tiles.shape[:2]
    slot_rows = send_rows.shape[2]
    size_dom = lax.axis_size("dom")

    by_route = {}
    for slot, offset in enumerate(OFFSETS):
        by_route.setdefault(offset % size_dom, []).append(slot)
    slot_groups = sorted(by_route.values(), key=lambda slots: -len(slots))

    def view(array):
        array = array.reshape(steps, 2, cell_blocks, LANES).transpose(0, 2, 1, 3)
        return array.reshape(steps * stride, LANES)

    def unview(array):
        array = array.reshape(steps, cell_blocks, 2, LANES).transpose(0, 2, 1, 3)
        return array.reshape(steps, 2, cells)

    fields = [view(state), view(dir_one), view(dir_two)]
    rows = send_rows.reshape(send_rows.shape[1:])
    counts = send_count
    cols = tile_cols.T
    feed = feed.reshape(cell_blocks, LANES)
    kill = kill.reshape(cell_blocks, LANES)

    vmem = pl.BlockSpec(memory_space=VMEM)
    smem = pl.BlockSpec(memory_space=SMEM)
    anywhere = pl.BlockSpec(memory_space=pl.ANY)
    params = pltpu.CompilerParams(vmem_limit_bytes=16 * 1024 * 1024)

    groups = tuple(range(steps // STEPS))
    late, middle, lead = groups[:1], groups[1:-1], groups[-1:]
    most = middle + lead
    wide, *narrow = slot_groups
    others = [slot for slots in narrow for slot in slots]

    def rows_of(part):
        return len(part) * FIELDS * 2 * STEPS

    def f32(*shape):
        return jax.ShapeDtypeStruct(shape, F32)

    def parts_of(part):
        return jax.ShapeDtypeStruct((cell_blocks, 2 * rows_of(part), LANES), BF16)

    def sends_of(part, chosen):
        return [f32(rows_of(part), len(slots) * slot_rows) for slots in chosen]

    def cost(flops, moved):
        return pl.CostEstimate(flops=flops, bytes_accessed=moved, transcendentals=0)

    def in_hbm(*arrays):
        return [pltpu.with_memory_space_constraint(array, pltpu.HBM) for array in arrays]

    def send_to(send, slots):
        return shift_along(send, "dom", OFFSETS[slots[0]])

    hbm = pl.BlockSpec(memory_space=pltpu.HBM)
    size = rows_of(groups)
    every = len(OFFSETS) * slot_rows
    wide_width = len(wide) * slot_rows
    send, held, listed, last = pl.pallas_call(
        functools.partial(first_kernel, lead, wide, cell_blocks),
        out_shape=[
            f32(rows_of(lead), wide_width),
            f32(FIELDS, steps * stride, LANES),
            jax.ShapeDtypeStruct(rows.shape, jnp.int32),
            f32(FIELDS * stride, LANES),
        ],
        in_specs=[hbm] * (FIELDS + 2),
        out_specs=[vmem] * 4,
        scratch_shapes=[
            VMEM(rows.shape, jnp.int32),
            VMEM(counts.shape, jnp.int32),
            pltpu.SemaphoreType.DMA((2 * FIELDS + 2,)),
        ],
        compiler_params=params,
        cost_estimate=cost(4 * rows_of(lead) * cells * wide_width, 8 * size * cells),
        name="gather_first",
    )(*in_hbm(*fields, rows, counts))
    wide_lead = send_to(send, wide)
    send, *sends, most_parts = pl.pallas_call(
        functools.partial(second_kernel, most, middle, wide, others, cell_blocks),
        out_shape=sends_of(middle, [wide]) + sends_of(most, narrow) + [parts_of(most)],
        in_specs=[vmem] * 2,
        out_specs=[vmem] * (len(narrow) + 2),
        scratch_shapes=[VMEM((cells, every), BF16)],
        compiler_params=params,
        cost_estimate=cost(4 * rows_of(most) * cells * every, 8 * size * cells),
        name="gather_second",
    )(held, listed)
    wide_middle = send_to(send, wide)
    prev = shift_along(last, "tm", 1)
    narrow_most = [send_to(part, slots) for part, slots in zip(sends, narrow)]
    *sends, late_parts = pl.pallas_call(
        functools.partial(third_kernel, late, wide, others, cell_blocks),
        out_shape=sends_of(late, slot_groups) + [parts_of(late)],
        in_specs=[vmem] * 3,
        out_specs=[vmem] * (len(slot_groups) + 1),
        scratch_shapes=[VMEM((cells, every), BF16)],
        compiler_params=params,
        cost_estimate=cost(4 * rows_of(late) * cells * every, 8 * size * cells),
        name="gather_third",
    )(held, prev, listed)
    base_most, base_late, split_tiles = pl.pallas_call(
        functools.partial(local_kernel, (most, late), cell_blocks),
        out_shape=[
            f32(cell_blocks, rows_of(most), LANES),
            f32(cell_blocks, rows_of(late), LANES),
            jax.ShapeDtypeStruct((blocks, per_row * LANES, 2 * LANES), BF16),
        ],
        in_specs=[vmem] * 2 + [hbm] * 3,
        out_specs=[vmem] * 3,
        scratch_shapes=[
            VMEM(feed.shape, F32),
            VMEM(kill.shape, F32),
            VMEM(tiles.shape, F32),
            pltpu.SemaphoreType.DMA((3,)),
        ],
        compiler_params=params,
        cost_estimate=cost(60 * size * cells, 8 * tiles.size),
        name="local_terms",
    )(held, prev, *in_hbm(feed, kill, tiles))

    arrived_late = [send_to(sends[0], wide)]
    sends[1], wide_lead = lax.optimization_barrier((sends[1], wide_lead))
    arrived_late.append(send_to(sends[1], slot_groups[1]))
    for number in range(2, len(sends)):
        sends[number], narrow_most[0], split_tiles = lax.optimization_barrier((sends[number], narrow_most[0], split_tiles))
        arrived_late.append(send_to(sends[number], slot_groups[number]))

    def apply(part, base, parts, transfers, outs):
        inputs = [cols, split_tiles, base, parts, *[array for array, _, _ in transfers]]
        received = [(slots, row) for _, slots, row in transfers]
        return pl.pallas_call(
            functools.partial(apply_kernel, part, received, cell_blocks, blocks, per_row, len(outs)),
            out_shape=[f32(steps * stride, LANES)] * FIELDS,
            in_specs=[vmem] * len(inputs) + [anywhere] * len(outs),
            out_specs=[anywhere] * FIELDS,
            input_output_aliases={len(inputs) + f: f for f in range(len(outs))},
            scratch_shapes=[
                VMEM((cell_blocks + every // LANES, 2 * rows_of(part), LANES), BF16),
                VMEM((FIELDS, len(part) * STEPS * stride, LANES), F32),
                pltpu.SemaphoreType.DMA((FIELDS,)),
            ],
            compiler_params=params,
            cost_estimate=cost(8 * rows_of(part) * blocks * per_row * LANES * LANES, 16 * rows_of(part) * cells),
            name="apply_tiles",
        )(*inputs, *outs)

    transfers = [(wide_middle, wide, 0), (wide_lead, wide, rows_of(middle))]
    transfers += [(array, slots, 0) for array, slots in zip(narrow_most, narrow)]
    outs = apply(most, base_most, most_parts, transfers, [])
    transfers = [(array, slots, 0) for array, slots in zip(arrived_late, slot_groups)]
    outs = apply(late, base_late, late_parts, transfers, outs)
    return tuple(unview(out) for out in outs)


def solution(mesh):
    fields = P(("group", "tm"), None, "dom")
    in_specs = (
        fields,
        fields,
        fields,
        P("dom"),
        P("dom"),
        P("dom", None, None, None),
        P("dom", None),
        P("dom", None, None),
        P("dom", None),
    )
    return jax.shard_map(
        per_device, mesh=mesh, in_specs=in_specs, out_specs=(fields, fields, fields), check_vma=False
    )
```

```python
import functools

import jax
import jax.numpy as jnp
from jax import lax
from jax.experimental import pallas as pl
from jax.experimental.pallas import tpu as pltpu
from jax.sharding import PartitionSpec as P

OFFSETS = (1, -1, 2, -2)
time_step = 0.5
spread_u = 1.0
spread_v = 0.5
LANES = 128
STEPS = 8
FIELDS = 3
VMEM = pltpu.VMEM
SMEM = pltpu.SMEM
F32 = jnp.float32
BF16 = jnp.bfloat16


def shift_along(block, axis, distance):
    size = lax.axis_size(axis)
    return lax.ppermute(block, axis, [((i - distance) % size, i) for i in range(size)])


def steps_at(ref, group, cell_block, species, stride):
    return ref[pl.ds(group * STEPS * stride + cell_block * 2 + species, STEPS, stride=stride), :]


def steps_before(ref, prev_ref, field, group, cell_block, species, stride):
    offset = cell_block * 2 + species
    if group > 0:
        return ref[pl.ds((group * STEPS - 1) * stride + offset, STEPS, stride=stride), :]
    now = steps_at(ref, 0, cell_block, species, stride)
    row = field * stride + offset
    first = jnp.broadcast_to(prev_ref[row : row + 1, :], now.shape)
    index = lax.broadcasted_iota(jnp.int32, now.shape, 0)
    return jnp.where(index == 0, first, pltpu.roll(now, 1, 0))


def split(values):
    high = values.astype(BF16)
    return high, (values - high.astype(F32)).astype(BF16)


def scaled_sum(ref, prev_ref, field, group, cell_block, species, stride):
    now = steps_at(ref, group, cell_block, species, stride)
    before = steps_before(ref, prev_ref, field, group, cell_block, species, stride)
    return (now + before) * (-0.5 * (spread_u, spread_v)[species])


def summed_parts(groups, cell_blocks, fields, prev, parts_ref, high_row, low_row):
    stride = 2 * cell_blocks
    for place, group in enumerate(groups):
        for field in range(FIELDS):
            row = (place * FIELDS + field) * 2 * STEPS
            for block in range(cell_blocks):
                both = [scaled_sum(fields[field], prev, field, group, block, species, stride) for species in range(2)]
                high, low = split(jnp.concatenate(both, axis=0))
                parts_ref[block, high_row + row : high_row + row + 2 * STEPS, :] = high
                parts_ref[block, low_row + row : low_row + row + 2 * STEPS, :] = low


def choose_rows(slots, listed_ref, choose):
    cells = choose.shape[0]
    slot_rows = listed_ref.shape[1]
    cell = lax.broadcasted_iota(jnp.int32, (LANES, slot_rows), 0)
    for place, slot in enumerate(slots):
        listed = listed_ref[slot : slot + 1, :]
        for start in range(0, cells, LANES):
            hit = cell == listed - start
            choose[start : start + LANES, place * slot_rows : (place + 1) * slot_rows] = jnp.where(
                hit, 1.0, 0.0
            ).astype(BF16)


def take_rows(parts, choose, sends):
    size = parts.shape[0] // 2
    start = 0
    for send in sends:
        width = send.shape[1]
        taken = jnp.dot(parts, choose[:, start : start + width], preferred_element_type=F32)
        send[...] = taken[:size] + taken[size:]
        start += width


def side_by_side(parts_ref, rows):
    blocks = [
        jnp.concatenate([parts_ref[b, start : start + count, :] for start, count in rows], axis=0)
        for b in range(parts_ref.shape[0])
    ]
    return jnp.concatenate(blocks, axis=1)


def first_kernel(lead, slots, cell_blocks, *refs):
    refs = list(refs)
    sources = [refs.pop(0) for _ in range(FIELDS)]
    rows_hbm, count_hbm, send, held, listed, last, rows_ref, count_ref, sems = refs
    stride = 2 * cell_blocks
    early = (lead[0] * STEPS - 1) * stride
    late = held.shape[1] - early
    small = [
        pltpu.make_async_copy(rows_hbm, rows_ref, sems.at[2 * FIELDS]),
        pltpu.make_async_copy(count_hbm, count_ref, sems.at[2 * FIELDS + 1]),
    ]
    needed = [
        pltpu.make_async_copy(sources[f].at[pl.ds(early, late), :], held.at[f, pl.ds(early, late), :], sems.at[f])
        for f in range(FIELDS)
    ]
    others = [
        pltpu.make_async_copy(sources[f].at[pl.ds(0, early), :], held.at[f, pl.ds(0, early), :], sems.at[FIELDS + f])
        for f in range(FIELDS)
    ]
    for copy in small + needed + others:
        copy.start()
    for copy in small:
        copy.wait()
    lane = lax.broadcasted_iota(jnp.int32, rows_ref.shape, 1)
    for slot in range(rows_ref.shape[0]):
        listed[slot : slot + 1, :] = jnp.where(
            lane[slot : slot + 1] < count_ref[:, slot : slot + 1], rows_ref[slot : slot + 1, :], -1
        )
    for copy in needed:
        copy.wait()
    columns = [
        listed[slot : slot + 1, start : start + LANES]
        for slot in slots
        for start in range(0, listed.shape[1], LANES)
    ]
    columns = [jnp.broadcast_to(column, (STEPS, LANES)) for column in columns]
    for place, group in enumerate(lead):
        for field in range(FIELDS):
            for species in range(2):
                row = ((place * FIELDS + field) * 2 + species) * STEPS
                sums = [
                    scaled_sum(held.at[field], None, field, group, block, species, stride) for block in range(cell_blocks)
                ]
                for number, column in enumerate(columns):
                    lanes = column & (LANES - 1)
                    found = jnp.zeros((STEPS, LANES), F32)
                    for block in range(cell_blocks):
                        taken = jnp.take_along_axis(sums[block], lanes, axis=1, mode="promise_in_bounds")
                        found = jnp.where(column >> 7 == block, taken, found)
                    send[row : row + STEPS, number * LANES : (number + 1) * LANES] = found
    for field in range(FIELDS):
        last[field * stride : (field + 1) * stride, :] = held[field, -stride:, :]
    for copy in others:
        copy.wait()


def second_kernel(most, middle, wide, others, cell_blocks, held, listed, send, *refs):
    *sends, parts_ref, choose = refs
    size = parts_ref.shape[1] // 2
    middle_size = size * len(middle) // len(most)
    choose_rows(wide + others, listed, choose)
    summed_parts(most, cell_blocks, [held.at[f] for f in range(FIELDS)], None, parts_ref, 0, size)
    width = send.shape[1]
    take_rows(side_by_side(parts_ref, [(0, middle_size), (size, middle_size)]), choose, [send])
    take_rows(side_by_side(parts_ref, [(0, 2 * size)]), choose.at[:, width:], sends)


def third_kernel(late, wide, others, cell_blocks, held, prev, listed, *refs):
    *sends, parts_ref, choose = refs
    size = parts_ref.shape[1] // 2
    choose_rows(wide + others, listed, choose)
    summed_parts(late, cell_blocks, [held.at[f] for f in range(FIELDS)], prev, parts_ref, 0, size)
    take_rows(side_by_side(parts_ref, [(0, 2 * size)]), choose, sends)


def pointwise(u, v, du, dv, ddu, ddv, feed, total):
    square = v * v
    product = u * square
    twice = 2.0 * u * v
    outs = [feed * (1.0 - u) - product, product - total * v]
    for first, second in ((du, dv), (ddu, ddv)):
        react = square * first + twice * second
        outs += [-react - feed * first, react - total * second]
    return outs


def local_kernel(
    chunks, cell_blocks, held, prev, feed_hbm, kill_hbm, tiles_hbm, base_one, base_two, split_tiles, feed_ref, kill_ref, tiles, sems
):
    copies = [
        pltpu.make_async_copy(feed_hbm, feed_ref, sems.at[0]),
        pltpu.make_async_copy(kill_hbm, kill_ref, sems.at[1]),
        pltpu.make_async_copy(tiles_hbm, tiles, sems.at[2]),
    ]
    for copy in copies:
        copy.start()
    for copy in copies[:2]:
        copy.wait()
    fields = [held.at[f] for f in range(FIELDS)]
    stride = 2 * cell_blocks
    pairs = [(f, s) for f in range(FIELDS) for s in range(2)]
    for base, groups in zip((base_one, base_two), chunks):
        for place, group in enumerate(groups):
            for block in range(cell_blocks):
                feed = feed_ref[block : block + 1, :]
                total = feed + kill_ref[block : block + 1, :]
                now = [steps_at(fields[f], group, block, s, stride) for f, s in pairs]
                before = [steps_before(fields[f], prev, f, group, block, s, stride) for f, s in pairs]
                rate_now = pointwise(*now, feed, total)
                rate_before = pointwise(*before, feed, total)
                for index in range(2 * FIELDS):
                    row = (place * FIELDS * 2 + index) * STEPS
                    base[block, row : row + STEPS, :] = (now[index] - before[index]) * (1.0 / time_step) - 0.5 * (
                        rate_now[index] + rate_before[index]
                    )
    copies[2].wait()
    blocks, per_row = tiles.shape[:2]
    for block in range(blocks):
        for k in range(per_row):
            high, low = split(jnp.transpose(tiles[block, k]))
            split_tiles[block, k * LANES : (k + 1) * LANES, :LANES] = high
            split_tiles[block, k * LANES : (k + 1) * LANES, LANES:] = low


def apply_kernel(groups, received, cell_blocks, blocks, per_row, held_back, *refs):
    refs = list(refs)
    cols_ref, split_tiles, base, parts_ref = [refs.pop(0) for _ in range(4)]
    arrived = [refs.pop(0) for _ in received]
    refs = refs[held_back:]
    outs = [refs.pop(0) for _ in range(FIELDS)]
    extended, made, sems = refs
    stride = 2 * cell_blocks
    size = base.shape[1]
    cols = cols_ref[...]
    extended[:cell_blocks] = parts_ref[...]
    for ref, (slots, row) in zip(arrived, received):
        count, width = ref.shape
        per_slot = width // len(slots) // LANES
        for place, slot in enumerate(slots):
            for b in range(per_slot):
                lane = (place * per_slot + b) * LANES
                high, low = split(ref[:, lane : lane + LANES])
                extended[cell_blocks + slot * per_slot + b, row : row + count, :] = high
                extended[cell_blocks + slot * per_slot + b, size + row : size + row + count, :] = low
    for block in range(blocks):
        chosen = jnp.concatenate([extended[cols[k, block]] for k in range(per_row)], axis=1)
        product = jnp.dot(chosen, split_tiles[block], preferred_element_type=F32)
        product = product[:, :LANES] + product[:, LANES:]
        result = base[block] + (product[:size] + product[size:])
        for index in range(size // STEPS):
            group, field, species = index // (2 * FIELDS), index // 2 % FIELDS, index % 2
            at = group * STEPS * stride + block * 2 + species
            made[field, pl.ds(at, STEPS, stride=stride), :] = result[index * STEPS : (index + 1) * STEPS, :]
    span = pl.ds(groups[0] * STEPS * stride, len(groups) * STEPS * stride)
    copies = [pltpu.make_async_copy(made.at[f], outs[f].at[span, :], sems.at[f]) for f in range(FIELDS)]
    for copy in copies:
        copy.start()
    for copy in copies:
        copy.wait()


def per_device(state, dir_one, dir_two, feed, kill, tiles, tile_cols, send_rows, send_count):
    steps, _, cells = state.shape
    cell_blocks = cells // LANES
    stride = 2 * cell_blocks
    blocks, per_row = tiles.shape[:2]
    slot_rows = send_rows.shape[2]
    size_dom = lax.axis_size("dom")

    by_route = {}
    for slot, offset in enumerate(OFFSETS):
        by_route.setdefault(offset % size_dom, []).append(slot)
    slot_groups = sorted(by_route.values(), key=lambda slots: -len(slots))

    def view(array):
        array = array.reshape(steps, 2, cell_blocks, LANES).transpose(0, 2, 1, 3)
        return array.reshape(steps * stride, LANES)

    def unview(array):
        array = array.reshape(steps, cell_blocks, 2, LANES).transpose(0, 2, 1, 3)
        return array.reshape(steps, 2, cells)

    fields = [view(state), view(dir_one), view(dir_two)]
    rows = send_rows.reshape(send_rows.shape[1:])
    counts = send_count
    cols = tile_cols.T
    feed = feed.reshape(cell_blocks, LANES)
    kill = kill.reshape(cell_blocks, LANES)

    vmem = pl.BlockSpec(memory_space=VMEM)
    smem = pl.BlockSpec(memory_space=SMEM)
    anywhere = pl.BlockSpec(memory_space=pl.ANY)
    params = pltpu.CompilerParams(vmem_limit_bytes=16 * 1024 * 1024)

    groups = tuple(range(steps // STEPS))
    late, middle, lead = groups[:1], groups[1:-1], groups[-1:]
    most = middle + lead
    wide, *narrow = slot_groups
    others = [slot for slots in narrow for slot in slots]

    def rows_of(part):
        return len(part) * FIELDS * 2 * STEPS

    def f32(*shape):
        return jax.ShapeDtypeStruct(shape, F32)

    def parts_of(part):
        return jax.ShapeDtypeStruct((cell_blocks, 2 * rows_of(part), LANES), BF16)

    def sends_of(part, chosen):
        return [f32(rows_of(part), len(slots) * slot_rows) for slots in chosen]

    def cost(flops, moved):
        return pl.CostEstimate(flops=flops, bytes_accessed=moved, transcendentals=0)

    def in_hbm(*arrays):
        return [pltpu.with_memory_space_constraint(array, pltpu.HBM) for array in arrays]

    def send_to(send, slots):
        return shift_along(send, "dom", OFFSETS[slots[0]])

    hbm = pl.BlockSpec(memory_space=pltpu.HBM)
    size = rows_of(groups)
    every = len(OFFSETS) * slot_rows
    wide_width = len(wide) * slot_rows
    send, held, listed, last = pl.pallas_call(
        functools.partial(first_kernel, lead, wide, cell_blocks),
        out_shape=[
            f32(rows_of(lead), wide_width),
            f32(FIELDS, steps * stride, LANES),
            jax.ShapeDtypeStruct(rows.shape, jnp.int32),
            f32(FIELDS * stride, LANES),
        ],
        in_specs=[hbm] * (FIELDS + 2),
        out_specs=[vmem] * 4,
        scratch_shapes=[
            VMEM(rows.shape, jnp.int32),
            VMEM(counts.shape, jnp.int32),
            pltpu.SemaphoreType.DMA((2 * FIELDS + 2,)),
        ],
        compiler_params=params,
        cost_estimate=cost(4 * rows_of(lead) * cells * wide_width, 8 * size * cells),
        name="gather_first",
    )(*in_hbm(*fields, rows, counts))
    wide_lead = send_to(send, wide)
    send, *sends, most_parts = pl.pallas_call(
        functools.partial(second_kernel, most, middle, wide, others, cell_blocks),
        out_shape=sends_of(middle, [wide]) + sends_of(most, narrow) + [parts_of(most)],
        in_specs=[vmem] * 2,
        out_specs=[vmem] * (len(narrow) + 2),
        scratch_shapes=[VMEM((cells, every), BF16)],
        compiler_params=params,
        cost_estimate=cost(4 * rows_of(most) * cells * every, 8 * size * cells),
        name="gather_second",
    )(held, listed)
    wide_middle = send_to(send, wide)
    prev = shift_along(last, "tm", 1)
    narrow_most = [send_to(part, slots) for part, slots in zip(sends, narrow)]
    *sends, late_parts = pl.pallas_call(
        functools.partial(third_kernel, late, wide, others, cell_blocks),
        out_shape=sends_of(late, slot_groups) + [parts_of(late)],
        in_specs=[vmem] * 3,
        out_specs=[vmem] * (len(slot_groups) + 1),
        scratch_shapes=[VMEM((cells, every), BF16)],
        compiler_params=params,
        cost_estimate=cost(4 * rows_of(late) * cells * every, 8 * size * cells),
        name="gather_third",
    )(held, prev, listed)
    base_most, base_late, split_tiles = pl.pallas_call(
        functools.partial(local_kernel, (most, late), cell_blocks),
        out_shape=[
            f32(cell_blocks, rows_of(most), LANES),
            f32(cell_blocks, rows_of(late), LANES),
            jax.ShapeDtypeStruct((blocks, per_row * LANES, 2 * LANES), BF16),
        ],
        in_specs=[vmem] * 2 + [hbm] * 3,
        out_specs=[vmem] * 3,
        scratch_shapes=[
            VMEM(feed.shape, F32),
            VMEM(kill.shape, F32),
            VMEM(tiles.shape, F32),
            pltpu.SemaphoreType.DMA((3,)),
        ],
        compiler_params=params,
        cost_estimate=cost(60 * size * cells, 8 * tiles.size),
        name="local_terms",
    )(held, prev, *in_hbm(feed, kill, tiles))

    arrived_late = [send_to(sends[0], wide)]
    sends[1], wide_lead = lax.optimization_barrier((sends[1], wide_lead))
    arrived_late.append(send_to(sends[1], slot_groups[1]))
    for number in range(2, len(sends)):
        sends[number], narrow_most[0] = lax.optimization_barrier((sends[number], narrow_most[0]))
        arrived_late.append(send_to(sends[number], slot_groups[number]))

    def apply(part, base, parts, transfers, outs):
        inputs = [cols, split_tiles, base, parts, *[array for array, _, _ in transfers]]
        received = [(slots, row) for _, slots, row in transfers]
        return pl.pallas_call(
            functools.partial(apply_kernel, part, received, cell_blocks, blocks, per_row, len(outs)),
            out_shape=[f32(steps * stride, LANES)] * FIELDS,
            in_specs=[vmem] * len(inputs) + [anywhere] * len(outs),
            out_specs=[anywhere] * FIELDS,
            input_output_aliases={len(inputs) + f: f for f in range(len(outs))},
            scratch_shapes=[
                VMEM((cell_blocks + every // LANES, 2 * rows_of(part), LANES), BF16),
                VMEM((FIELDS, len(part) * STEPS * stride, LANES), F32),
                pltpu.SemaphoreType.DMA((FIELDS,)),
            ],
            compiler_params=params,
            cost_estimate=cost(8 * rows_of(part) * blocks * per_row * LANES * LANES, 16 * rows_of(part) * cells),
            name="apply_tiles",
        )(*inputs, *outs)

    transfers = [(wide_middle, wide, 0), (wide_lead, wide, rows_of(middle))]
    transfers += [(array, slots, 0) for array, slots in zip(narrow_most, narrow)]
    outs = apply(most, base_most, most_parts, transfers, [])
    transfers = [(array, slots, 0) for array, slots in zip(arrived_late, slot_groups)]
    outs = apply(late, base_late, late_parts, transfers, outs)
    return tuple(unview(out) for out in outs)


def solution(mesh):
    fields = P(("group", "tm"), None, "dom")
    in_specs = (
        fields,
        fields,
        fields,
        P("dom"),
        P("dom"),
        P("dom", None, None, None),
        P("dom", None),
        P("dom", None, None),
        P("dom", None),
    )
    return jax.shard_map(
        per_device, mesh=mesh, in_specs=in_specs, out_specs=(fields, fields, fields), check_vma=False
    )
```

```python
import functools

import jax
import jax.numpy as jnp
from jax import lax
from jax.experimental import pallas as pl
from jax.experimental.pallas import tpu as pltpu
from jax.sharding import PartitionSpec as P

OFFSETS = (1, -1, 2, -2)
time_step = 0.5
spread_u = 1.0
spread_v = 0.5
LANES = 128
STEPS = 8
FIELDS = 3
VMEM = pltpu.VMEM
SMEM = pltpu.SMEM
F32 = jnp.float32
BF16 = jnp.bfloat16


def shift_along(block, axis, distance):
    size = lax.axis_size(axis)
    return lax.ppermute(block, axis, [((i - distance) % size, i) for i in range(size)])


def steps_at(ref, group, cell_block, species, stride):
    return ref[pl.ds(group * STEPS * stride + cell_block * 2 + species, STEPS, stride=stride), :]


def steps_before(ref, prev_ref, field, group, cell_block, species, stride):
    offset = cell_block * 2 + species
    if group > 0:
        return ref[pl.ds((group * STEPS - 1) * stride + offset, STEPS, stride=stride), :]
    now = steps_at(ref, 0, cell_block, species, stride)
    row = field * stride + offset
    first = jnp.broadcast_to(prev_ref[row : row + 1, :], now.shape)
    index = lax.broadcasted_iota(jnp.int32, now.shape, 0)
    return jnp.where(index == 0, first, pltpu.roll(now, 1, 0))


def split(values):
    high = values.astype(BF16)
    return high, (values - high.astype(F32)).astype(BF16)


def scaled_sum(ref, prev_ref, field, group, cell_block, species, stride):
    now = steps_at(ref, group, cell_block, species, stride)
    before = steps_before(ref, prev_ref, field, group, cell_block, species, stride)
    return (now + before) * (-0.5 * (spread_u, spread_v)[species])


def summed_parts(groups, cell_blocks, fields, prev, parts_ref, high_row, low_row):
    stride = 2 * cell_blocks
    for place, group in enumerate(groups):
        for field in range(FIELDS):
            row = (place * FIELDS + field) * 2 * STEPS
            for block in range(cell_blocks):
                both = [scaled_sum(fields[field], prev, field, group, block, species, stride) for species in range(2)]
                high, low = split(jnp.concatenate(both, axis=0))
                parts_ref[block, high_row + row : high_row + row + 2 * STEPS, :] = high
                parts_ref[block, low_row + row : low_row + row + 2 * STEPS, :] = low


def choose_rows(slots, listed_ref, choose):
    cells = choose.shape[0]
    slot_rows = listed_ref.shape[1]
    cell = lax.broadcasted_iota(jnp.int32, (LANES, slot_rows), 0)
    for place, slot in enumerate(slots):
        listed = listed_ref[slot : slot + 1, :]
        for start in range(0, cells, LANES):
            hit = cell == listed - start
            choose[start : start + LANES, place * slot_rows : (place + 1) * slot_rows] = jnp.where(
                hit, 1.0, 0.0
            ).astype(BF16)


def take_rows(parts, choose, sends):
    size = parts.shape[0] // 2
    start = 0
    for send in sends:
        width = send.shape[1]
        taken = jnp.dot(parts, choose[:, start : start + width], preferred_element_type=F32)
        send[...] = taken[:size] + taken[size:]
        start += width


def side_by_side(parts_ref, rows):
    blocks = [
        jnp.concatenate([parts_ref[b, start : start + count, :] for start, count in rows], axis=0)
        for b in range(parts_ref.shape[0])
    ]
    return jnp.concatenate(blocks, axis=1)


def first_kernel(lead, slots, cell_blocks, *refs):
    refs = list(refs)
    sources = [refs.pop(0) for _ in range(FIELDS)]
    rows_hbm, count_hbm, send, held, listed, last, rows_ref, count_ref, sems = refs
    stride = 2 * cell_blocks
    early = (lead[0] * STEPS - 1) * stride
    late = held.shape[1] - early
    small = [
        pltpu.make_async_copy(rows_hbm, rows_ref, sems.at[2 * FIELDS]),
        pltpu.make_async_copy(count_hbm, count_ref, sems.at[2 * FIELDS + 1]),
    ]
    needed = [
        pltpu.make_async_copy(sources[f].at[pl.ds(early, late), :], held.at[f, pl.ds(early, late), :], sems.at[f])
        for f in range(FIELDS)
    ]
    others = [
        pltpu.make_async_copy(sources[f].at[pl.ds(0, early), :], held.at[f, pl.ds(0, early), :], sems.at[FIELDS + f])
        for f in range(FIELDS)
    ]
    for copy in small + needed + others:
        copy.start()
    for copy in small:
        copy.wait()
    lane = lax.broadcasted_iota(jnp.int32, rows_ref.shape, 1)
    for slot in range(rows_ref.shape[0]):
        listed[slot : slot + 1, :] = jnp.where(
            lane[slot : slot + 1] < count_ref[:, slot : slot + 1], rows_ref[slot : slot + 1, :], -1
        )
    for copy in needed:
        copy.wait()
    columns = [
        listed[slot : slot + 1, start : start + LANES]
        for slot in slots
        for start in range(0, listed.shape[1], LANES)
    ]
    columns = [jnp.broadcast_to(column, (STEPS, LANES)) for column in columns]
    for place, group in enumerate(lead):
        for field in range(FIELDS):
            for species in range(2):
                row = ((place * FIELDS + field) * 2 + species) * STEPS
                sums = [
                    scaled_sum(held.at[field], None, field, group, block, species, stride) for block in range(cell_blocks)
                ]
                for number, column in enumerate(columns):
                    lanes = column & (LANES - 1)
                    found = jnp.zeros((STEPS, LANES), F32)
                    for block in range(cell_blocks):
                        taken = jnp.take_along_axis(sums[block], lanes, axis=1, mode="promise_in_bounds")
                        found = jnp.where(column >> 7 == block, taken, found)
                    send[row : row + STEPS, number * LANES : (number + 1) * LANES] = found
    for field in range(FIELDS):
        last[field * stride : (field + 1) * stride, :] = held[field, -stride:, :]
    for copy in others:
        copy.wait()


def second_kernel(most, middle, wide, others, cell_blocks, held, listed, send, *refs):
    *sends, parts_ref, choose = refs
    size = parts_ref.shape[1] // 2
    middle_size = size * len(middle) // len(most)
    choose_rows(wide + others, listed, choose)
    summed_parts(most, cell_blocks, [held.at[f] for f in range(FIELDS)], None, parts_ref, 0, size)
    width = send.shape[1]
    take_rows(side_by_side(parts_ref, [(0, middle_size), (size, middle_size)]), choose, [send])
    take_rows(side_by_side(parts_ref, [(0, 2 * size)]), choose.at[:, width:], sends)


def third_kernel(late, wide, others, cell_blocks, held, prev, listed, *refs):
    *sends, parts_ref, choose = refs
    size = parts_ref.shape[1] // 2
    choose_rows(wide + others, listed, choose)
    summed_parts(late, cell_blocks, [held.at[f] for f in range(FIELDS)], prev, parts_ref, 0, size)
    take_rows(side_by_side(parts_ref, [(0, 2 * size)]), choose, sends)


def pointwise(u, v, du, dv, ddu, ddv, feed, total):
    square = v * v
    product = u * square
    twice = 2.0 * u * v
    outs = [feed * (1.0 - u) - product, product - total * v]
    for first, second in ((du, dv), (ddu, ddv)):
        react = square * first + twice * second
        outs += [-react - feed * first, react - total * second]
    return outs


def local_kernel(
    chunks, cell_blocks, held, prev, feed_hbm, kill_hbm, tiles_hbm, base_one, base_two, split_tiles, feed_ref, kill_ref, tiles, sems
):
    copies = [
        pltpu.make_async_copy(feed_hbm, feed_ref, sems.at[0]),
        pltpu.make_async_copy(kill_hbm, kill_ref, sems.at[1]),
        pltpu.make_async_copy(tiles_hbm, tiles, sems.at[2]),
    ]
    for copy in copies:
        copy.start()
    for copy in copies[:2]:
        copy.wait()
    fields = [held.at[f] for f in range(FIELDS)]
    stride = 2 * cell_blocks
    pairs = [(f, s) for f in range(FIELDS) for s in range(2)]
    for base, groups in zip((base_one, base_two), chunks):
        for place, group in enumerate(groups):
            for block in range(cell_blocks):
                feed = feed_ref[block : block + 1, :]
                total = feed + kill_ref[block : block + 1, :]
                now = [steps_at(fields[f], group, block, s, stride) for f, s in pairs]
                before = [steps_before(fields[f], prev, f, group, block, s, stride) for f, s in pairs]
                rate_now = pointwise(*now, feed, total)
                rate_before = pointwise(*before, feed, total)
                for index in range(2 * FIELDS):
                    row = (place * FIELDS * 2 + index) * STEPS
                    base[block, row : row + STEPS, :] = (now[index] - before[index]) * (1.0 / time_step) - 0.5 * (
                        rate_now[index] + rate_before[index]
                    )
    copies[2].wait()
    blocks, per_row = tiles.shape[:2]
    for block in range(blocks):
        for k in range(per_row):
            high, low = split(jnp.transpose(tiles[block, k]))
            split_tiles[block, k * LANES : (k + 1) * LANES, :LANES] = high
            split_tiles[block, k * LANES : (k + 1) * LANES, LANES:] = low


def apply_kernel(groups, received, cell_blocks, blocks, per_row, held_back, *refs):
    refs = list(refs)
    cols_ref, split_tiles, base, parts_ref = [refs.pop(0) for _ in range(4)]
    arrived = [refs.pop(0) for _ in received]
    refs = refs[held_back:]
    outs = [refs.pop(0) for _ in range(FIELDS)]
    extended, made, sems = refs
    stride = 2 * cell_blocks
    size = base.shape[1]
    cols = cols_ref[...]
    extended[:cell_blocks] = parts_ref[...]
    for ref, (slots, row) in zip(arrived, received):
        count, width = ref.shape
        per_slot = width // len(slots) // LANES
        for place, slot in enumerate(slots):
            for b in range(per_slot):
                lane = (place * per_slot + b) * LANES
                high, low = split(ref[:, lane : lane + LANES])
                extended[cell_blocks + slot * per_slot + b, row : row + count, :] = high
                extended[cell_blocks + slot * per_slot + b, size + row : size + row + count, :] = low
    for block in range(blocks):
        chosen = jnp.concatenate([extended[cols[k, block]] for k in range(per_row)], axis=1)
        product = jnp.dot(chosen, split_tiles[block], preferred_element_type=F32)
        product = product[:, :LANES] + product[:, LANES:]
        result = base[block] + (product[:size] + product[size:])
        for index in range(size // STEPS):
            group, field, species = index // (2 * FIELDS), index // 2 % FIELDS, index % 2
            at = group * STEPS * stride + block * 2 + species
            made[field, pl.ds(at, STEPS, stride=stride), :] = result[index * STEPS : (index + 1) * STEPS, :]
    span = pl.ds(groups[0] * STEPS * stride, len(groups) * STEPS * stride)
    copies = [pltpu.make_async_copy(made.at[f], outs[f].at[span, :], sems.at[f]) for f in range(FIELDS)]
    for copy in copies:
        copy.start()
    for copy in copies:
        copy.wait()


def per_device(state, dir_one, dir_two, feed, kill, tiles, tile_cols, send_rows, send_count):
    steps, _, cells = state.shape
    cell_blocks = cells // LANES
    stride = 2 * cell_blocks
    blocks, per_row = tiles.shape[:2]
    slot_rows = send_rows.shape[2]
    size_dom = lax.axis_size("dom")

    by_route = {}
    for slot, offset in enumerate(OFFSETS):
        by_route.setdefault(offset % size_dom, []).append(slot)
    slot_groups = sorted(by_route.values(), key=lambda slots: -len(slots))

    def view(array):
        array = array.reshape(steps, 2, cell_blocks, LANES).transpose(0, 2, 1, 3)
        return array.reshape(steps * stride, LANES)

    def unview(array):
        array = array.reshape(steps, cell_blocks, 2, LANES).transpose(0, 2, 1, 3)
        return array.reshape(steps, 2, cells)

    fields = [view(state), view(dir_one), view(dir_two)]
    rows = send_rows.reshape(send_rows.shape[1:])
    counts = send_count
    cols = tile_cols.T
    feed = feed.reshape(cell_blocks, LANES)
    kill = kill.reshape(cell_blocks, LANES)

    vmem = pl.BlockSpec(memory_space=VMEM)
    smem = pl.BlockSpec(memory_space=SMEM)
    anywhere = pl.BlockSpec(memory_space=pl.ANY)
    params = pltpu.CompilerParams(vmem_limit_bytes=16 * 1024 * 1024)

    groups = tuple(range(steps // STEPS))
    late, middle, lead = groups[:1], groups[1:-1], groups[-1:]
    most = middle + lead
    wide, *narrow = slot_groups
    others = [slot for slots in narrow for slot in slots]

    def rows_of(part):
        return len(part) * FIELDS * 2 * STEPS

    def f32(*shape):
        return jax.ShapeDtypeStruct(shape, F32)

    def parts_of(part):
        return jax.ShapeDtypeStruct((cell_blocks, 2 * rows_of(part), LANES), BF16)

    def sends_of(part, chosen):
        return [f32(rows_of(part), len(slots) * slot_rows) for slots in chosen]

    def cost(flops, moved):
        return pl.CostEstimate(flops=flops, bytes_accessed=moved, transcendentals=0)

    def in_hbm(*arrays):
        return [pltpu.with_memory_space_constraint(array, pltpu.HBM) for array in arrays]

    def send_to(send, slots):
        return shift_along(send, "dom", OFFSETS[slots[0]])

    hbm = pl.BlockSpec(memory_space=pltpu.HBM)
    size = rows_of(groups)
    every = len(OFFSETS) * slot_rows
    wide_width = len(wide) * slot_rows
    send, held, listed, last = pl.pallas_call(
        functools.partial(first_kernel, lead, wide, cell_blocks),
        out_shape=[
            f32(rows_of(lead), wide_width),
            f32(FIELDS, steps * stride, LANES),
            jax.ShapeDtypeStruct(rows.shape, jnp.int32),
            f32(FIELDS * stride, LANES),
        ],
        in_specs=[hbm] * (FIELDS + 2),
        out_specs=[vmem] * 4,
        scratch_shapes=[
            VMEM(rows.shape, jnp.int32),
            VMEM(counts.shape, jnp.int32),
            pltpu.SemaphoreType.DMA((2 * FIELDS + 2,)),
        ],
        compiler_params=params,
        cost_estimate=cost(4 * rows_of(lead) * cells * wide_width, 8 * size * cells),
        name="gather_first",
    )(*in_hbm(*fields, rows, counts))
    wide_lead = send_to(send, wide)
    send, *sends, most_parts = pl.pallas_call(
        functools.partial(second_kernel, most, middle, wide, others, cell_blocks),
        out_shape=sends_of(middle, [wide]) + sends_of(most, narrow) + [parts_of(most)],
        in_specs=[vmem] * 2,
        out_specs=[vmem] * (len(narrow) + 2),
        scratch_shapes=[VMEM((cells, every), BF16)],
        compiler_params=params,
        cost_estimate=cost(4 * rows_of(most) * cells * every, 8 * size * cells),
        name="gather_second",
    )(held, listed)
    wide_middle = send_to(send, wide)
    prev = shift_along(last, "tm", 1)
    narrow_sends = sends
    narrow_most = [send_to(narrow_sends[0], narrow[0])]
    *sends, late_parts = pl.pallas_call(
        functools.partial(third_kernel, late, wide, others, cell_blocks),
        out_shape=sends_of(late, slot_groups) + [parts_of(late)],
        in_specs=[vmem] * 3,
        out_specs=[vmem] * (len(slot_groups) + 1),
        scratch_shapes=[VMEM((cells, every), BF16)],
        compiler_params=params,
        cost_estimate=cost(4 * rows_of(late) * cells * every, 8 * size * cells),
        name="gather_third",
    )(held, prev, listed)
    base_most, base_late, split_tiles = pl.pallas_call(
        functools.partial(local_kernel, (most, late), cell_blocks),
        out_shape=[
            f32(cell_blocks, rows_of(most), LANES),
            f32(cell_blocks, rows_of(late), LANES),
            jax.ShapeDtypeStruct((blocks, per_row * LANES, 2 * LANES), BF16),
        ],
        in_specs=[vmem] * 2 + [hbm] * 3,
        out_specs=[vmem] * 3,
        scratch_shapes=[
            VMEM(feed.shape, F32),
            VMEM(kill.shape, F32),
            VMEM(tiles.shape, F32),
            pltpu.SemaphoreType.DMA((3,)),
        ],
        compiler_params=params,
        cost_estimate=cost(60 * size * cells, 8 * tiles.size),
        name="local_terms",
    )(held, prev, *in_hbm(feed, kill, tiles))

    arrived_late = [send_to(sends[0], wide)]
    for part, slots in zip(narrow_sends[1:], narrow[1:]):
        part, wide_lead = lax.optimization_barrier((part, wide_lead))
        narrow_most.append(send_to(part, slots))
    sends[1], split_tiles = lax.optimization_barrier((sends[1], split_tiles))
    arrived_late.append(send_to(sends[1], slot_groups[1]))
    for number in range(2, len(sends)):
        sends[number], narrow_most[0] = lax.optimization_barrier((sends[number], narrow_most[0]))
        arrived_late.append(send_to(sends[number], slot_groups[number]))

    def apply(part, base, parts, transfers, outs):
        inputs = [cols, split_tiles, base, parts, *[array for array, _, _ in transfers]]
        received = [(slots, row) for _, slots, row in transfers]
        return pl.pallas_call(
            functools.partial(apply_kernel, part, received, cell_blocks, blocks, per_row, len(outs)),
            out_shape=[f32(steps * stride, LANES)] * FIELDS,
            in_specs=[vmem] * len(inputs) + [anywhere] * len(outs),
            out_specs=[anywhere] * FIELDS,
            input_output_aliases={len(inputs) + f: f for f in range(len(outs))},
            scratch_shapes=[
                VMEM((cell_blocks + every // LANES, 2 * rows_of(part), LANES), BF16),
                VMEM((FIELDS, len(part) * STEPS * stride, LANES), F32),
                pltpu.SemaphoreType.DMA((FIELDS,)),
            ],
            compiler_params=params,
            cost_estimate=cost(8 * rows_of(part) * blocks * per_row * LANES * LANES, 16 * rows_of(part) * cells),
            name="apply_tiles",
        )(*inputs, *outs)

    transfers = [(wide_middle, wide, 0), (wide_lead, wide, rows_of(middle))]
    transfers += [(array, slots, 0) for array, slots in zip(narrow_most, narrow)]
    outs = apply(most, base_most, most_parts, transfers, [])
    transfers = [(array, slots, 0) for array, slots in zip(arrived_late, slot_groups)]
    outs = apply(late, base_late, late_parts, transfers, outs)
    return tuple(unview(out) for out in outs)


def solution(mesh):
    fields = P(("group", "tm"), None, "dom")
    in_specs = (
        fields,
        fields,
        fields,
        P("dom"),
        P("dom"),
        P("dom", None, None, None),
        P("dom", None),
        P("dom", None, None),
        P("dom", None),
    )
    return jax.shard_map(
        per_device, mesh=mesh, in_specs=in_specs, out_specs=(fields, fields, fields), check_vma=False
    )
```

```python
import functools

import jax
import jax.numpy as jnp
from jax import lax
from jax.experimental import pallas as pl
from jax.experimental.pallas import tpu as pltpu
from jax.sharding import PartitionSpec as P

OFFSETS = (1, -1, 2, -2)
time_step = 0.5
spread_u = 1.0
spread_v = 0.5
LANES = 128
STEPS = 8
FIELDS = 3
VMEM = pltpu.VMEM
SMEM = pltpu.SMEM
F32 = jnp.float32
BF16 = jnp.bfloat16


def shift_along(block, axis, distance):
    size = lax.axis_size(axis)
    return lax.ppermute(block, axis, [((i - distance) % size, i) for i in range(size)])


def steps_at(ref, group, cell_block, species, stride):
    return ref[pl.ds(group * STEPS * stride + cell_block * 2 + species, STEPS, stride=stride), :]


def steps_before(ref, prev_ref, field, group, cell_block, species, stride):
    offset = cell_block * 2 + species
    if group > 0:
        return ref[pl.ds((group * STEPS - 1) * stride + offset, STEPS, stride=stride), :]
    now = steps_at(ref, 0, cell_block, species, stride)
    row = field * stride + offset
    first = jnp.broadcast_to(prev_ref[row : row + 1, :], now.shape)
    index = lax.broadcasted_iota(jnp.int32, now.shape, 0)
    return jnp.where(index == 0, first, pltpu.roll(now, 1, 0))


def split(values):
    high = values.astype(BF16)
    return high, (values - high.astype(F32)).astype(BF16)


def scaled_sum(ref, prev_ref, field, group, cell_block, species, stride):
    now = steps_at(ref, group, cell_block, species, stride)
    before = steps_before(ref, prev_ref, field, group, cell_block, species, stride)
    return (now + before) * (-0.5 * (spread_u, spread_v)[species])


def summed_parts(groups, cell_blocks, fields, prev, parts_ref, high_row, low_row):
    stride = 2 * cell_blocks
    for place, group in enumerate(groups):
        for field in range(FIELDS):
            row = (place * FIELDS + field) * 2 * STEPS
            for block in range(cell_blocks):
                both = [scaled_sum(fields[field], prev, field, group, block, species, stride) for species in range(2)]
                high, low = split(jnp.concatenate(both, axis=0))
                parts_ref[block, high_row + row : high_row + row + 2 * STEPS, :] = high
                parts_ref[block, low_row + row : low_row + row + 2 * STEPS, :] = low


def choose_rows(slots, listed_ref, choose):
    cells = choose.shape[0]
    slot_rows = listed_ref.shape[1]
    cell = lax.broadcasted_iota(jnp.int32, (LANES, slot_rows), 0)
    for place, slot in enumerate(slots):
        listed = listed_ref[slot : slot + 1, :]
        for start in range(0, cells, LANES):
            hit = cell == listed - start
            choose[start : start + LANES, place * slot_rows : (place + 1) * slot_rows] = jnp.where(
                hit, 1.0, 0.0
            ).astype(BF16)


def take_rows(parts, choose, sends):
    size = parts.shape[0] // 2
    start = 0
    for send in sends:
        width = send.shape[1]
        taken = jnp.dot(parts, choose[:, start : start + width], preferred_element_type=F32)
        send[...] = taken[:size] + taken[size:]
        start += width


def side_by_side(parts_ref, rows):
    blocks = [
        jnp.concatenate([parts_ref[b, start : start + count, :] for start, count in rows], axis=0)
        for b in range(parts_ref.shape[0])
    ]
    return jnp.concatenate(blocks, axis=1)


def first_kernel(lead, slots, cell_blocks, *refs):
    refs = list(refs)
    sources = [refs.pop(0) for _ in range(FIELDS)]
    rows_hbm, count_hbm, send, held, listed, last, rows_ref, count_ref, sems = refs
    stride = 2 * cell_blocks
    early = (lead[0] * STEPS - 1) * stride
    late = held.shape[1] - early
    small = [
        pltpu.make_async_copy(rows_hbm, rows_ref, sems.at[2 * FIELDS]),
        pltpu.make_async_copy(count_hbm, count_ref, sems.at[2 * FIELDS + 1]),
    ]
    needed = [
        pltpu.make_async_copy(sources[f].at[pl.ds(early, late), :], held.at[f, pl.ds(early, late), :], sems.at[f])
        for f in range(FIELDS)
    ]
    others = [
        pltpu.make_async_copy(sources[f].at[pl.ds(0, early), :], held.at[f, pl.ds(0, early), :], sems.at[FIELDS + f])
        for f in range(FIELDS)
    ]
    for copy in small + needed + others:
        copy.start()
    for copy in small:
        copy.wait()
    lane = lax.broadcasted_iota(jnp.int32, rows_ref.shape, 1)
    columns = {}
    for slot in range(rows_ref.shape[0]):
        live = lane[slot : slot + 1] < count_ref[:, slot : slot + 1]
        row = jnp.where(live, rows_ref[slot : slot + 1, :], -1)
        listed[slot : slot + 1, :] = row
        columns[slot] = [row[:, start : start + LANES] for start in range(0, row.shape[1], LANES)]
    columns = [jnp.broadcast_to(column, (STEPS, LANES)) for slot in slots for column in columns[slot]]
    lanes = [column & (LANES - 1) for column in columns]
    blocks = [column >> 7 for column in columns]
    for field in range(FIELDS):
        needed[field].wait()
        for place, group in enumerate(lead):
            for species in range(2):
                row = ((place * FIELDS + field) * 2 + species) * STEPS
                sums = [
                    scaled_sum(held.at[field], None, field, group, block, species, stride) for block in range(cell_blocks)
                ]
                for number in range(len(columns)):
                    found = jnp.zeros((STEPS, LANES), F32)
                    for block in range(cell_blocks):
                        taken = jnp.take_along_axis(sums[block], lanes[number], axis=1, mode="promise_in_bounds")
                        found = jnp.where(blocks[number] == block, taken, found)
                    send[row : row + STEPS, number * LANES : (number + 1) * LANES] = found
    for field in range(FIELDS):
        last[field * stride : (field + 1) * stride, :] = held[field, -stride:, :]
    for copy in others:
        copy.wait()


def second_kernel(most, middle, wide, others, cell_blocks, held, listed, send, *refs):
    *sends, parts_ref, choose = refs
    size = parts_ref.shape[1] // 2
    middle_size = size * len(middle) // len(most)
    choose_rows(wide + others, listed, choose)
    summed_parts(most, cell_blocks, [held.at[f] for f in range(FIELDS)], None, parts_ref, 0, size)
    width = send.shape[1]
    take_rows(side_by_side(parts_ref, [(0, middle_size), (size, middle_size)]), choose, [send])
    take_rows(side_by_side(parts_ref, [(0, 2 * size)]), choose.at[:, width:], sends)


def third_kernel(late, wide, others, cell_blocks, held, prev, listed, *refs):
    *sends, parts_ref, choose = refs
    size = parts_ref.shape[1] // 2
    choose_rows(wide + others, listed, choose)
    summed_parts(late, cell_blocks, [held.at[f] for f in range(FIELDS)], prev, parts_ref, 0, size)
    take_rows(side_by_side(parts_ref, [(0, 2 * size)]), choose, sends)


def pointwise(u, v, du, dv, ddu, ddv, feed, total):
    square = v * v
    product = u * square
    twice = 2.0 * u * v
    outs = [feed * (1.0 - u) - product, product - total * v]
    for first, second in ((du, dv), (ddu, ddv)):
        react = square * first + twice * second
        outs += [-react - feed * first, react - total * second]
    return outs


def local_kernel(
    chunks, cell_blocks, held, prev, feed_hbm, kill_hbm, tiles_hbm, base_one, base_two, split_tiles, feed_ref, kill_ref, tiles, sems
):
    copies = [
        pltpu.make_async_copy(feed_hbm, feed_ref, sems.at[0]),
        pltpu.make_async_copy(kill_hbm, kill_ref, sems.at[1]),
        pltpu.make_async_copy(tiles_hbm, tiles, sems.at[2]),
    ]
    for copy in copies:
        copy.start()
    for copy in copies[:2]:
        copy.wait()
    fields = [held.at[f] for f in range(FIELDS)]
    stride = 2 * cell_blocks
    pairs = [(f, s) for f in range(FIELDS) for s in range(2)]
    for base, groups in zip((base_one, base_two), chunks):
        for place, group in enumerate(groups):
            for block in range(cell_blocks):
                feed = feed_ref[block : block + 1, :]
                total = feed + kill_ref[block : block + 1, :]
                now = [steps_at(fields[f], group, block, s, stride) for f, s in pairs]
                before = [steps_before(fields[f], prev, f, group, block, s, stride) for f, s in pairs]
                rate_now = pointwise(*now, feed, total)
                rate_before = pointwise(*before, feed, total)
                for index in range(2 * FIELDS):
                    row = (place * FIELDS * 2 + index) * STEPS
                    base[block, row : row + STEPS, :] = (now[index] - before[index]) * (1.0 / time_step) - 0.5 * (
                        rate_now[index] + rate_before[index]
                    )
    copies[2].wait()
    blocks, per_row = tiles.shape[:2]
    for block in range(blocks):
        for k in range(per_row):
            high, low = split(jnp.transpose(tiles[block, k]))
            split_tiles[block, k * LANES : (k + 1) * LANES, :LANES] = high
            split_tiles[block, k * LANES : (k + 1) * LANES, LANES:] = low


def apply_kernel(groups, received, cell_blocks, blocks, per_row, held_back, *refs):
    refs = list(refs)
    cols_ref, split_tiles, base, parts_ref = [refs.pop(0) for _ in range(4)]
    arrived = [refs.pop(0) for _ in received]
    refs = refs[held_back:]
    outs = [refs.pop(0) for _ in range(FIELDS)]
    extended, made, sems = refs
    stride = 2 * cell_blocks
    size = base.shape[1]
    cols = cols_ref[...]
    extended[:cell_blocks] = parts_ref[...]
    for ref, (slots, row) in zip(arrived, received):
        count, width = ref.shape
        per_slot = width // len(slots) // LANES
        for place, slot in enumerate(slots):
            for b in range(per_slot):
                lane = (place * per_slot + b) * LANES
                high, low = split(ref[:, lane : lane + LANES])
                extended[cell_blocks + slot * per_slot + b, row : row + count, :] = high
                extended[cell_blocks + slot * per_slot + b, size + row : size + row + count, :] = low
    for block in range(blocks):
        chosen = jnp.concatenate([extended[cols[k, block]] for k in range(per_row)], axis=1)
        product = jnp.dot(chosen, split_tiles[block], preferred_element_type=F32)
        product = product[:, :LANES] + product[:, LANES:]
        result = base[block] + (product[:size] + product[size:])
        for index in range(size // STEPS):
            group, field, species = index // (2 * FIELDS), index // 2 % FIELDS, index % 2
            at = group * STEPS * stride + block * 2 + species
            made[field, pl.ds(at, STEPS, stride=stride), :] = result[index * STEPS : (index + 1) * STEPS, :]
    span = pl.ds(groups[0] * STEPS * stride, len(groups) * STEPS * stride)
    copies = [pltpu.make_async_copy(made.at[f], outs[f].at[span, :], sems.at[f]) for f in range(FIELDS)]
    for copy in copies:
        copy.start()
    for copy in copies:
        copy.wait()


def per_device(state, dir_one, dir_two, feed, kill, tiles, tile_cols, send_rows, send_count):
    steps, _, cells = state.shape
    cell_blocks = cells // LANES
    stride = 2 * cell_blocks
    blocks, per_row = tiles.shape[:2]
    slot_rows = send_rows.shape[2]
    size_dom = lax.axis_size("dom")

    by_route = {}
    for slot, offset in enumerate(OFFSETS):
        by_route.setdefault(offset % size_dom, []).append(slot)
    slot_groups = sorted(by_route.values(), key=lambda slots: -len(slots))

    def view(array):
        array = array.reshape(steps, 2, cell_blocks, LANES).transpose(0, 2, 1, 3)
        return array.reshape(steps * stride, LANES)

    def unview(array):
        array = array.reshape(steps, cell_blocks, 2, LANES).transpose(0, 2, 1, 3)
        return array.reshape(steps, 2, cells)

    fields = [view(state), view(dir_one), view(dir_two)]
    rows = send_rows.reshape(send_rows.shape[1:])
    counts = send_count
    cols = tile_cols.T
    feed = feed.reshape(cell_blocks, LANES)
    kill = kill.reshape(cell_blocks, LANES)

    vmem = pl.BlockSpec(memory_space=VMEM)
    smem = pl.BlockSpec(memory_space=SMEM)
    anywhere = pl.BlockSpec(memory_space=pl.ANY)
    params = pltpu.CompilerParams(vmem_limit_bytes=16 * 1024 * 1024)

    groups = tuple(range(steps // STEPS))
    late, middle, lead = groups[:1], groups[1:-1], groups[-1:]
    most = middle + lead
    wide, *narrow = slot_groups
    others = [slot for slots in narrow for slot in slots]

    def rows_of(part):
        return len(part) * FIELDS * 2 * STEPS

    def f32(*shape):
        return jax.ShapeDtypeStruct(shape, F32)

    def parts_of(part):
        return jax.ShapeDtypeStruct((cell_blocks, 2 * rows_of(part), LANES), BF16)

    def sends_of(part, chosen):
        return [f32(rows_of(part), len(slots) * slot_rows) for slots in chosen]

    def cost(flops, moved):
        return pl.CostEstimate(flops=flops, bytes_accessed=moved, transcendentals=0)

    def in_hbm(*arrays):
        return [pltpu.with_memory_space_constraint(array, pltpu.HBM) for array in arrays]

    def send_to(send, slots):
        return shift_along(send, "dom", OFFSETS[slots[0]])

    hbm = pl.BlockSpec(memory_space=pltpu.HBM)
    size = rows_of(groups)
    every = len(OFFSETS) * slot_rows
    wide_width = len(wide) * slot_rows
    send, held, listed, last = pl.pallas_call(
        functools.partial(first_kernel, lead, wide, cell_blocks),
        out_shape=[
            f32(rows_of(lead), wide_width),
            f32(FIELDS, steps * stride, LANES),
            jax.ShapeDtypeStruct(rows.shape, jnp.int32),
            f32(FIELDS * stride, LANES),
        ],
        in_specs=[hbm] * (FIELDS + 2),
        out_specs=[vmem] * 4,
        scratch_shapes=[
            VMEM(rows.shape, jnp.int32),
            VMEM(counts.shape, jnp.int32),
            pltpu.SemaphoreType.DMA((2 * FIELDS + 2,)),
        ],
        compiler_params=params,
        cost_estimate=cost(4 * rows_of(lead) * cells * wide_width, 8 * size * cells),
        name="gather_first",
    )(*in_hbm(*fields, rows, counts))
    wide_lead = send_to(send, wide)
    send, *sends, most_parts = pl.pallas_call(
        functools.partial(second_kernel, most, middle, wide, others, cell_blocks),
        out_shape=sends_of(middle, [wide]) + sends_of(most, narrow) + [parts_of(most)],
        in_specs=[vmem] * 2,
        out_specs=[vmem] * (len(narrow) + 2),
        scratch_shapes=[VMEM((cells, every), BF16)],
        compiler_params=params,
        cost_estimate=cost(4 * rows_of(most) * cells * every, 8 * size * cells),
        name="gather_second",
    )(held, listed)
    wide_middle = send_to(send, wide)
    prev = shift_along(last, "tm", 1)
    narrow_most = [send_to(part, slots) for part, slots in zip(sends, narrow)]
    *sends, late_parts = pl.pallas_call(
        functools.partial(third_kernel, late, wide, others, cell_blocks),
        out_shape=sends_of(late, slot_groups) + [parts_of(late)],
        in_specs=[vmem] * 3,
        out_specs=[vmem] * (len(slot_groups) + 1),
        scratch_shapes=[VMEM((cells, every), BF16)],
        compiler_params=params,
        cost_estimate=cost(4 * rows_of(late) * cells * every, 8 * size * cells),
        name="gather_third",
    )(held, prev, listed)
    base_most, base_late, split_tiles = pl.pallas_call(
        functools.partial(local_kernel, (most, late), cell_blocks),
        out_shape=[
            f32(cell_blocks, rows_of(most), LANES),
            f32(cell_blocks, rows_of(late), LANES),
            jax.ShapeDtypeStruct((blocks, per_row * LANES, 2 * LANES), BF16),
        ],
        in_specs=[vmem] * 2 + [hbm] * 3,
        out_specs=[vmem] * 3,
        scratch_shapes=[
            VMEM(feed.shape, F32),
            VMEM(kill.shape, F32),
            VMEM(tiles.shape, F32),
            pltpu.SemaphoreType.DMA((3,)),
        ],
        compiler_params=params,
        cost_estimate=cost(60 * size * cells, 8 * tiles.size),
        name="local_terms",
    )(held, prev, *in_hbm(feed, kill, tiles))

    arrived_late = [send_to(sends[0], wide)]
    sends[1], wide_lead = lax.optimization_barrier((sends[1], wide_lead))
    arrived_late.append(send_to(sends[1], slot_groups[1]))
    for number in range(2, len(sends)):
        sends[number], narrow_most[0], split_tiles = lax.optimization_barrier((sends[number], narrow_most[0], split_tiles))
        arrived_late.append(send_to(sends[number], slot_groups[number]))

    def apply(part, base, parts, transfers, outs):
        inputs = [cols, split_tiles, base, parts, *[array for array, _, _ in transfers]]
        received = [(slots, row) for _, slots, row in transfers]
        return pl.pallas_call(
            functools.partial(apply_kernel, part, received, cell_blocks, blocks, per_row, len(outs)),
            out_shape=[f32(steps * stride, LANES)] * FIELDS,
            in_specs=[vmem] * len(inputs) + [anywhere] * len(outs),
            out_specs=[anywhere] * FIELDS,
            input_output_aliases={len(inputs) + f: f for f in range(len(outs))},
            scratch_shapes=[
                VMEM((cell_blocks + every // LANES, 2 * rows_of(part), LANES), BF16),
                VMEM((FIELDS, len(part) * STEPS * stride, LANES), F32),
                pltpu.SemaphoreType.DMA((FIELDS,)),
            ],
            compiler_params=params,
            cost_estimate=cost(8 * rows_of(part) * blocks * per_row * LANES * LANES, 16 * rows_of(part) * cells),
            name="apply_tiles",
        )(*inputs, *outs)

    transfers = [(wide_middle, wide, 0), (wide_lead, wide, rows_of(middle))]
    transfers += [(array, slots, 0) for array, slots in zip(narrow_most, narrow)]
    outs = apply(most, base_most, most_parts, transfers, [])
    transfers = [(array, slots, 0) for array, slots in zip(arrived_late, slot_groups)]
    outs = apply(late, base_late, late_parts, transfers, outs)
    return tuple(unview(out) for out in outs)


def solution(mesh):
    fields = P(("group", "tm"), None, "dom")
    in_specs = (
        fields,
        fields,
        fields,
        P("dom"),
        P("dom"),
        P("dom", None, None, None),
        P("dom", None),
        P("dom", None, None),
        P("dom", None),
    )
    return jax.shard_map(
        per_device, mesh=mesh, in_specs=in_specs, out_specs=(fields, fields, fields), check_vma=False
    )
```

```python
import functools

import jax
import jax.numpy as jnp
from jax import lax
from jax.experimental import pallas as pl
from jax.experimental.pallas import tpu as pltpu
from jax.sharding import PartitionSpec as P

OFFSETS = (1, -1, 2, -2)
time_step = 0.5
spread_u = 1.0
spread_v = 0.5
LANES = 128
STEPS = 8
FIELDS = 3
VMEM = pltpu.VMEM
SMEM = pltpu.SMEM
F32 = jnp.float32
BF16 = jnp.bfloat16


def shift_along(block, axis, distance):
    size = lax.axis_size(axis)
    return lax.ppermute(block, axis, [((i - distance) % size, i) for i in range(size)])


def steps_at(ref, group, cell_block, species, stride):
    return ref[pl.ds(group * STEPS * stride + cell_block * 2 + species, STEPS, stride=stride), :]


def steps_before(ref, prev_ref, field, group, cell_block, species, stride):
    offset = cell_block * 2 + species
    if group > 0:
        return ref[pl.ds((group * STEPS - 1) * stride + offset, STEPS, stride=stride), :]
    now = steps_at(ref, 0, cell_block, species, stride)
    row = field * stride + offset
    first = jnp.broadcast_to(prev_ref[row : row + 1, :], now.shape)
    index = lax.broadcasted_iota(jnp.int32, now.shape, 0)
    return jnp.where(index == 0, first, pltpu.roll(now, 1, 0))


def split(values):
    high = values.astype(BF16)
    return high, (values - high.astype(F32)).astype(BF16)


def scaled_sum(ref, prev_ref, field, group, cell_block, species, stride):
    now = steps_at(ref, group, cell_block, species, stride)
    before = steps_before(ref, prev_ref, field, group, cell_block, species, stride)
    return (now + before) * (-0.5 * (spread_u, spread_v)[species])


def summed_parts(groups, cell_blocks, fields, prev, parts_ref, high_row, low_row):
    stride = 2 * cell_blocks
    for place, group in enumerate(groups):
        for field in range(FIELDS):
            row = (place * FIELDS + field) * 2 * STEPS
            for block in range(cell_blocks):
                both = [scaled_sum(fields[field], prev, field, group, block, species, stride) for species in range(2)]
                high, low = split(jnp.concatenate(both, axis=0))
                parts_ref[block, high_row + row : high_row + row + 2 * STEPS, :] = high
                parts_ref[block, low_row + row : low_row + row + 2 * STEPS, :] = low


def choose_rows(slots, listed_ref, choose):
    cells = choose.shape[0]
    slot_rows = listed_ref.shape[1]
    cell = lax.broadcasted_iota(jnp.int32, (LANES, slot_rows), 0)
    for place, slot in enumerate(slots):
        listed = listed_ref[slot : slot + 1, :]
        for start in range(0, cells, LANES):
            hit = cell == listed - start
            choose[start : start + LANES, place * slot_rows : (place + 1) * slot_rows] = jnp.where(
                hit, 1.0, 0.0
            ).astype(BF16)


def take_rows(parts, choose, sends):
    size = parts.shape[0] // 2
    start = 0
    for send in sends:
        width = send.shape[1]
        taken = jnp.dot(parts, choose[:, start : start + width], preferred_element_type=F32)
        send[...] = taken[:size] + taken[size:]
        start += width


def side_by_side(parts_ref, rows):
    blocks = [
        jnp.concatenate([parts_ref[b, start : start + count, :] for start, count in rows], axis=0)
        for b in range(parts_ref.shape[0])
    ]
    return jnp.concatenate(blocks, axis=1)


def first_kernel(lead, slots, cell_blocks, *refs):
    refs = list(refs)
    sources = [refs.pop(0) for _ in range(FIELDS)]
    rows_hbm, count_hbm, send, held, listed, last, rows_ref, count_ref, sems = refs
    stride = 2 * cell_blocks
    early = (lead[0] * STEPS - 1) * stride
    late = held.shape[1] - early
    small = [
        pltpu.make_async_copy(rows_hbm, rows_ref, sems.at[2 * FIELDS]),
        pltpu.make_async_copy(count_hbm, count_ref, sems.at[2 * FIELDS + 1]),
    ]
    needed = [
        pltpu.make_async_copy(sources[f].at[pl.ds(early, late), :], held.at[f, pl.ds(early, late), :], sems.at[f])
        for f in range(FIELDS)
    ]
    others = [
        pltpu.make_async_copy(sources[f].at[pl.ds(0, early), :], held.at[f, pl.ds(0, early), :], sems.at[FIELDS + f])
        for f in range(FIELDS)
    ]
    for copy in small + needed + others:
        copy.start()
    for copy in small:
        copy.wait()
    lane = lax.broadcasted_iota(jnp.int32, rows_ref.shape, 1)
    for slot in range(rows_ref.shape[0]):
        listed[slot : slot + 1, :] = jnp.where(
            lane[slot : slot + 1] < count_ref[:, slot : slot + 1], rows_ref[slot : slot + 1, :], -1
        )
    for copy in needed:
        copy.wait()
    columns = [
        listed[slot : slot + 1, start : start + LANES]
        for slot in slots
        for start in range(0, listed.shape[1], LANES)
    ]
    columns = [jnp.broadcast_to(column, (STEPS, LANES)) for column in columns]
    for place, group in enumerate(lead):
        for field in range(FIELDS):
            for species in range(2):
                row = ((place * FIELDS + field) * 2 + species) * STEPS
                sums = [
                    scaled_sum(held.at[field], None, field, group, block, species, stride) for block in range(cell_blocks)
                ]
                for number, column in enumerate(columns):
                    lanes = column & (LANES - 1)
                    found = jnp.zeros((STEPS, LANES), F32)
                    for block in range(cell_blocks):
                        taken = jnp.take_along_axis(sums[block], lanes, axis=1, mode="promise_in_bounds")
                        found = jnp.where(column >> 7 == block, taken, found)
                    send[row : row + STEPS, number * LANES : (number + 1) * LANES] = found
    for field in range(FIELDS):
        last[field * stride : (field + 1) * stride, :] = held[field, -stride:, :]
    for copy in others:
        copy.wait()


def second_kernel(most, middle, wide, others, cell_blocks, held, listed, send, *refs):
    *sends, parts_ref, choose = refs
    size = parts_ref.shape[1] // 2
    middle_size = size * len(middle) // len(most)
    choose_rows(wide + others, listed, choose)
    summed_parts(most, cell_blocks, [held.at[f] for f in range(FIELDS)], None, parts_ref, 0, size)
    width = send.shape[1]
    take_rows(side_by_side(parts_ref, [(0, middle_size), (size, middle_size)]), choose, [send])
    take_rows(side_by_side(parts_ref, [(0, 2 * size)]), choose.at[:, width:], sends)


def third_kernel(late, wide, others, cell_blocks, held, prev, listed, *refs):
    *sends, parts_ref, choose = refs
    size = parts_ref.shape[1] // 2
    choose_rows(wide + others, listed, choose)
    summed_parts(late, cell_blocks, [held.at[f] for f in range(FIELDS)], prev, parts_ref, 0, size)
    take_rows(side_by_side(parts_ref, [(0, 2 * size)]), choose, sends)


def pointwise(u, v, du, dv, ddu, ddv, feed, total):
    square = v * v
    product = u * square
    twice = 2.0 * u * v
    outs = [feed * (1.0 - u) - product, product - total * v]
    for first, second in ((du, dv), (ddu, ddv)):
        react = square * first + twice * second
        outs += [-react - feed * first, react - total * second]
    return outs


def local_kernel(
    chunks, cell_blocks, held, prev, feed_hbm, kill_hbm, tiles_hbm, base_one, base_two, split_tiles, feed_ref, kill_ref, tiles, sems
):
    copies = [
        pltpu.make_async_copy(feed_hbm, feed_ref, sems.at[0]),
        pltpu.make_async_copy(kill_hbm, kill_ref, sems.at[1]),
        pltpu.make_async_copy(tiles_hbm, tiles, sems.at[2]),
    ]
    for copy in copies:
        copy.start()
    for copy in copies[:2]:
        copy.wait()
    fields = [held.at[f] for f in range(FIELDS)]
    stride = 2 * cell_blocks
    pairs = [(f, s) for f in range(FIELDS) for s in range(2)]
    for base, groups in zip((base_one, base_two), chunks):
        for place, group in enumerate(groups):
            for block in range(cell_blocks):
                feed = feed_ref[block : block + 1, :]
                total = feed + kill_ref[block : block + 1, :]
                now = [steps_at(fields[f], group, block, s, stride) for f, s in pairs]
                before = [steps_before(fields[f], prev, f, group, block, s, stride) for f, s in pairs]
                rate_now = pointwise(*now, feed, total)
                rate_before = pointwise(*before, feed, total)
                for index in range(2 * FIELDS):
                    row = (place * FIELDS * 2 + index) * STEPS
                    base[block, row : row + STEPS, :] = (now[index] - before[index]) * (1.0 / time_step) - 0.5 * (
                        rate_now[index] + rate_before[index]
                    )
    copies[2].wait()
    blocks, per_row = tiles.shape[:2]
    for block in range(blocks):
        for k in range(per_row):
            high, low = split(jnp.transpose(tiles[block, k]))
            split_tiles[block, k * LANES : (k + 1) * LANES, :LANES] = high
            split_tiles[block, k * LANES : (k + 1) * LANES, LANES:] = low


def apply_kernel(groups, received, cell_blocks, blocks, per_row, held_back, *refs):
    refs = list(refs)
    cols_ref, split_tiles, base, parts_ref = [refs.pop(0) for _ in range(4)]
    arrived = [refs.pop(0) for _ in received]
    refs = refs[held_back:]
    outs = [refs.pop(0) for _ in range(FIELDS)]
    extended, made, sems = refs
    stride = 2 * cell_blocks
    size = base.shape[1]
    cols = cols_ref[...]
    extended[:cell_blocks] = parts_ref[...]
    for ref, (slots, row) in zip(arrived, received):
        count, width = ref.shape
        per_slot = width // len(slots) // LANES
        for place, slot in enumerate(slots):
            for b in range(per_slot):
                lane = (place * per_slot + b) * LANES
                high, low = split(ref[:, lane : lane + LANES])
                extended[cell_blocks + slot * per_slot + b, row : row + count, :] = high
                extended[cell_blocks + slot * per_slot + b, size + row : size + row + count, :] = low
    for block in range(blocks):
        chosen = jnp.concatenate([extended[cols[k, block]] for k in range(per_row)], axis=1)
        product = jnp.dot(chosen, split_tiles[block], preferred_element_type=F32)
        product = product[:, :LANES] + product[:, LANES:]
        result = base[block] + (product[:size] + product[size:])
        for index in range(size // STEPS):
            group, field, species = index // (2 * FIELDS), index // 2 % FIELDS, index % 2
            at = group * STEPS * stride + block * 2 + species
            made[field, pl.ds(at, STEPS, stride=stride), :] = result[index * STEPS : (index + 1) * STEPS, :]
    span = pl.ds(groups[0] * STEPS * stride, len(groups) * STEPS * stride)
    copies = [pltpu.make_async_copy(made.at[f], outs[f].at[span, :], sems.at[f]) for f in range(FIELDS)]
    for copy in copies:
        copy.start()
    for copy in copies:
        copy.wait()


def per_device(state, dir_one, dir_two, feed, kill, tiles, tile_cols, send_rows, send_count):
    steps, _, cells = state.shape
    cell_blocks = cells // LANES
    stride = 2 * cell_blocks
    blocks, per_row = tiles.shape[:2]
    slot_rows = send_rows.shape[2]
    size_dom = lax.axis_size("dom")

    by_route = {}
    for slot, offset in enumerate(OFFSETS):
        by_route.setdefault(offset % size_dom, []).append(slot)
    slot_groups = sorted(by_route.values(), key=lambda slots: -len(slots))

    def view(array):
        array = array.reshape(steps, 2, cell_blocks, LANES).transpose(0, 2, 1, 3)
        return array.reshape(steps * stride, LANES)

    def unview(array):
        array = array.reshape(steps, cell_blocks, 2, LANES).transpose(0, 2, 1, 3)
        return array.reshape(steps, 2, cells)

    fields = [view(state), view(dir_one), view(dir_two)]
    rows = send_rows.reshape(send_rows.shape[1:])
    counts = send_count
    cols = tile_cols.T
    feed = feed.reshape(cell_blocks, LANES)
    kill = kill.reshape(cell_blocks, LANES)

    vmem = pl.BlockSpec(memory_space=VMEM)
    smem = pl.BlockSpec(memory_space=SMEM)
    anywhere = pl.BlockSpec(memory_space=pl.ANY)
    params = pltpu.CompilerParams(vmem_limit_bytes=16 * 1024 * 1024)

    groups = tuple(range(steps // STEPS))
    late, middle, lead = groups[:1], groups[1:-1], groups[-1:]
    most = middle + lead
    wide, *narrow = slot_groups
    others = [slot for slots in narrow for slot in slots]

    def rows_of(part):
        return len(part) * FIELDS * 2 * STEPS

    def f32(*shape):
        return jax.ShapeDtypeStruct(shape, F32)

    def parts_of(part):
        return jax.ShapeDtypeStruct((cell_blocks, 2 * rows_of(part), LANES), BF16)

    def sends_of(part, chosen):
        return [f32(rows_of(part), len(slots) * slot_rows) for slots in chosen]

    def cost(flops, moved):
        return pl.CostEstimate(flops=flops, bytes_accessed=moved, transcendentals=0)

    def in_hbm(*arrays):
        return [pltpu.with_memory_space_constraint(array, pltpu.HBM) for array in arrays]

    def send_to(send, slots):
        return shift_along(send, "dom", OFFSETS[slots[0]])

    hbm = pl.BlockSpec(memory_space=pltpu.HBM)
    size = rows_of(groups)
    every = len(OFFSETS) * slot_rows
    wide_width = len(wide) * slot_rows
    send, held, listed, last = pl.pallas_call(
        functools.partial(first_kernel, lead, wide, cell_blocks),
        out_shape=[
            f32(rows_of(lead), wide_width),
            f32(FIELDS, steps * stride, LANES),
            jax.ShapeDtypeStruct(rows.shape, jnp.int32),
            f32(FIELDS * stride, LANES),
        ],
        in_specs=[hbm] * (FIELDS + 2),
        out_specs=[vmem] * 4,
        scratch_shapes=[
            VMEM(rows.shape, jnp.int32),
            VMEM(counts.shape, jnp.int32),
            pltpu.SemaphoreType.DMA((2 * FIELDS + 2,)),
        ],
        compiler_params=params,
        cost_estimate=cost(4 * rows_of(lead) * cells * wide_width, 8 * size * cells),
        name="gather_first",
    )(*in_hbm(*fields, rows, counts))
    wide_lead = send_to(send, wide)
    send, *sends, most_parts = pl.pallas_call(
        functools.partial(second_kernel, most, middle, wide, others, cell_blocks),
        out_shape=sends_of(middle, [wide]) + sends_of(most, narrow) + [parts_of(most)],
        in_specs=[vmem] * 2,
        out_specs=[vmem] * (len(narrow) + 2),
        scratch_shapes=[VMEM((cells, every), BF16)],
        compiler_params=params,
        cost_estimate=cost(4 * rows_of(most) * cells * every, 8 * size * cells),
        name="gather_second",
    )(held, listed)
    wide_middle = send_to(send, wide)
    prev = shift_along(last, "tm", 1)
    narrow_most = [send_to(part, slots) for part, slots in zip(sends, narrow)]
    *sends, late_parts = pl.pallas_call(
        functools.partial(third_kernel, late, wide, others, cell_blocks),
        out_shape=sends_of(late, slot_groups) + [parts_of(late)],
        in_specs=[vmem] * 3,
        out_specs=[vmem] * (len(slot_groups) + 1),
        scratch_shapes=[VMEM((cells, every), BF16)],
        compiler_params=params,
        cost_estimate=cost(4 * rows_of(late) * cells * every, 8 * size * cells),
        name="gather_third",
    )(held, prev, listed)
    base_most, base_late, split_tiles = pl.pallas_call(
        functools.partial(local_kernel, (most, late), cell_blocks),
        out_shape=[
            f32(cell_blocks, rows_of(most), LANES),
            f32(cell_blocks, rows_of(late), LANES),
            jax.ShapeDtypeStruct((blocks, per_row * LANES, 2 * LANES), BF16),
        ],
        in_specs=[vmem] * 2 + [hbm] * 3,
        out_specs=[vmem] * 3,
        scratch_shapes=[
            VMEM(feed.shape, F32),
            VMEM(kill.shape, F32),
            VMEM(tiles.shape, F32),
            pltpu.SemaphoreType.DMA((3,)),
        ],
        compiler_params=params,
        cost_estimate=cost(60 * size * cells, 8 * tiles.size),
        name="local_terms",
    )(held, prev, *in_hbm(feed, kill, tiles))

    arrived_late = [send_to(sends[0], wide)]
    sends[1], wide_lead = lax.optimization_barrier((sends[1], wide_lead))
    arrived_late.append(send_to(sends[1], slot_groups[1]))
    for number in range(2, len(sends)):
        sends[number], narrow_most[0], wide_middle, split_tiles = lax.optimization_barrier(
            (sends[number], narrow_most[0], wide_middle, split_tiles)
        )
        arrived_late.append(send_to(sends[number], slot_groups[number]))

    def apply(part, base, parts, transfers, outs):
        inputs = [cols, split_tiles, base, parts, *[array for array, _, _ in transfers]]
        received = [(slots, row) for _, slots, row in transfers]
        return pl.pallas_call(
            functools.partial(apply_kernel, part, received, cell_blocks, blocks, per_row, len(outs)),
            out_shape=[f32(steps * stride, LANES)] * FIELDS,
            in_specs=[vmem] * len(inputs) + [anywhere] * len(outs),
            out_specs=[anywhere] * FIELDS,
            input_output_aliases={len(inputs) + f: f for f in range(len(outs))},
            scratch_shapes=[
                VMEM((cell_blocks + every // LANES, 2 * rows_of(part), LANES), BF16),
                VMEM((FIELDS, len(part) * STEPS * stride, LANES), F32),
                pltpu.SemaphoreType.DMA((FIELDS,)),
            ],
            compiler_params=params,
            cost_estimate=cost(8 * rows_of(part) * blocks * per_row * LANES * LANES, 16 * rows_of(part) * cells),
            name="apply_tiles",
        )(*inputs, *outs)

    transfers = [(wide_middle, wide, 0), (wide_lead, wide, rows_of(middle))]
    transfers += [(array, slots, 0) for array, slots in zip(narrow_most, narrow)]
    outs = apply(most, base_most, most_parts, transfers, [])
    transfers = [(array, slots, 0) for array, slots in zip(arrived_late, slot_groups)]
    outs = apply(late, base_late, late_parts, transfers, outs)
    return tuple(unview(out) for out in outs)


def solution(mesh):
    fields = P(("group", "tm"), None, "dom")
    in_specs = (
        fields,
        fields,
        fields,
        P("dom"),
        P("dom"),
        P("dom", None, None, None),
        P("dom", None),
        P("dom", None, None),
        P("dom", None),
    )
    return jax.shard_map(
        per_device, mesh=mesh, in_specs=in_specs, out_specs=(fields, fields, fields), check_vma=False
    )
```

```python
import functools

import jax
import jax.numpy as jnp
from jax import lax
from jax.experimental import pallas as pl
from jax.experimental.pallas import tpu as pltpu
from jax.sharding import PartitionSpec as P

OFFSETS = (1, -1, 2, -2)
time_step = 0.5
spread_u = 1.0
spread_v = 0.5
LANES = 128
STEPS = 8
FIELDS = 3
VMEM = pltpu.VMEM
SMEM = pltpu.SMEM
F32 = jnp.float32
BF16 = jnp.bfloat16


def shift_along(block, axis, distance):
    size = lax.axis_size(axis)
    return lax.ppermute(block, axis, [((i - distance) % size, i) for i in range(size)])


def steps_at(ref, group, cell_block, species, stride):
    return ref[pl.ds(group * STEPS * stride + cell_block * 2 + species, STEPS, stride=stride), :]


def steps_before(ref, prev_ref, field, group, cell_block, species, stride):
    offset = cell_block * 2 + species
    if group > 0:
        return ref[pl.ds((group * STEPS - 1) * stride + offset, STEPS, stride=stride), :]
    now = steps_at(ref, 0, cell_block, species, stride)
    row = field * stride + offset
    first = jnp.broadcast_to(prev_ref[row : row + 1, :], now.shape)
    index = lax.broadcasted_iota(jnp.int32, now.shape, 0)
    return jnp.where(index == 0, first, pltpu.roll(now, 1, 0))


def split(values):
    high = values.astype(BF16)
    return high, (values - high.astype(F32)).astype(BF16)


def scaled_sum(ref, prev_ref, field, group, cell_block, species, stride):
    now = steps_at(ref, group, cell_block, species, stride)
    before = steps_before(ref, prev_ref, field, group, cell_block, species, stride)
    return (now + before) * (-0.5 * (spread_u, spread_v)[species])


def summed_parts(groups, cell_blocks, fields, prev, parts_ref, high_row, low_row):
    stride = 2 * cell_blocks
    for place, group in enumerate(groups):
        for field in range(FIELDS):
            row = (place * FIELDS + field) * 2 * STEPS
            for block in range(cell_blocks):
                both = [scaled_sum(fields[field], prev, field, group, block, species, stride) for species in range(2)]
                high, low = split(jnp.concatenate(both, axis=0))
                parts_ref[block, high_row + row : high_row + row + 2 * STEPS, :] = high
                parts_ref[block, low_row + row : low_row + row + 2 * STEPS, :] = low


def choose_rows(slots, listed_ref, choose):
    cells = choose.shape[0]
    slot_rows = listed_ref.shape[1]
    cell = lax.broadcasted_iota(jnp.int32, (LANES, slot_rows), 0)
    for place, slot in enumerate(slots):
        listed = listed_ref[slot : slot + 1, :]
        for start in range(0, cells, LANES):
            hit = cell == listed - start
            choose[start : start + LANES, place * slot_rows : (place + 1) * slot_rows] = jnp.where(
                hit, 1.0, 0.0
            ).astype(BF16)


def take_rows(parts, choose, sends):
    size = parts.shape[0] // 2
    start = 0
    for send in sends:
        width = send.shape[1]
        taken = jnp.dot(parts, choose[:, start : start + width], preferred_element_type=F32)
        send[...] = taken[:size] + taken[size:]
        start += width


def side_by_side(parts_ref, rows):
    blocks = [
        jnp.concatenate([parts_ref[b, start : start + count, :] for start, count in rows], axis=0)
        for b in range(parts_ref.shape[0])
    ]
    return jnp.concatenate(blocks, axis=1)


def first_kernel(lead, slots, cell_blocks, *refs):
    refs = list(refs)
    sources = [refs.pop(0) for _ in range(FIELDS)]
    rows_hbm, count_hbm, send, held, listed, last, rows_ref, count_ref, sems = refs
    stride = 2 * cell_blocks
    early = (lead[0] * STEPS - 1) * stride
    late = held.shape[1] - early
    small = [
        pltpu.make_async_copy(rows_hbm, rows_ref, sems.at[2 * FIELDS]),
        pltpu.make_async_copy(count_hbm, count_ref, sems.at[2 * FIELDS + 1]),
    ]
    needed = [
        pltpu.make_async_copy(sources[f].at[pl.ds(early, late), :], held.at[f, pl.ds(early, late), :], sems.at[f])
        for f in range(FIELDS)
    ]
    others = [
        pltpu.make_async_copy(sources[f].at[pl.ds(0, early), :], held.at[f, pl.ds(0, early), :], sems.at[FIELDS + f])
        for f in range(FIELDS)
    ]
    for copy in small + needed + others:
        copy.start()
    for copy in small:
        copy.wait()
    lane = lax.broadcasted_iota(jnp.int32, rows_ref.shape, 1)
    columns = {}
    for slot in range(rows_ref.shape[0]):
        live = lane[slot : slot + 1] < count_ref[:, slot : slot + 1]
        row = jnp.where(live, rows_ref[slot : slot + 1, :], -1)
        listed[slot : slot + 1, :] = row
        columns[slot] = [row[:, start : start + LANES] for start in range(0, row.shape[1], LANES)]
    columns = [jnp.broadcast_to(column, (STEPS, LANES)) for slot in slots for column in columns[slot]]
    lanes = [column & (LANES - 1) for column in columns]
    blocks = [column >> 7 for column in columns]
    for copy in needed:
        copy.wait()
    for field in range(FIELDS):
        for place, group in enumerate(lead):
            for species in range(2):
                row = ((place * FIELDS + field) * 2 + species) * STEPS
                sums = [
                    scaled_sum(held.at[field], None, field, group, block, species, stride) for block in range(cell_blocks)
                ]
                for number in range(len(columns)):
                    found = jnp.zeros((STEPS, LANES), F32)
                    for block in range(cell_blocks):
                        taken = jnp.take_along_axis(sums[block], lanes[number], axis=1, mode="promise_in_bounds")
                        found = jnp.where(blocks[number] == block, taken, found)
                    send[row : row + STEPS, number * LANES : (number + 1) * LANES] = found
    for field in range(FIELDS):
        last[field * stride : (field + 1) * stride, :] = held[field, -stride:, :]
    for copy in others:
        copy.wait()


def second_kernel(most, middle, wide, others, cell_blocks, held, listed, send, *refs):
    *sends, parts_ref, choose = refs
    size = parts_ref.shape[1] // 2
    middle_size = size * len(middle) // len(most)
    choose_rows(wide + others, listed, choose)
    summed_parts(most, cell_blocks, [held.at[f] for f in range(FIELDS)], None, parts_ref, 0, size)
    width = send.shape[1]
    take_rows(side_by_side(parts_ref, [(0, middle_size), (size, middle_size)]), choose, [send])
    take_rows(side_by_side(parts_ref, [(0, 2 * size)]), choose.at[:, width:], sends)


def third_kernel(late, wide, others, cell_blocks, held, prev, listed, *refs):
    *sends, parts_ref, choose = refs
    size = parts_ref.shape[1] // 2
    choose_rows(wide + others, listed, choose)
    summed_parts(late, cell_blocks, [held.at[f] for f in range(FIELDS)], prev, parts_ref, 0, size)
    take_rows(side_by_side(parts_ref, [(0, 2 * size)]), choose, sends)


def pointwise(u, v, du, dv, ddu, ddv, feed, total):
    square = v * v
    product = u * square
    twice = 2.0 * u * v
    outs = [feed * (1.0 - u) - product, product - total * v]
    for first, second in ((du, dv), (ddu, ddv)):
        react = square * first + twice * second
        outs += [-react - feed * first, react - total * second]
    return outs


def local_kernel(
    chunks, cell_blocks, held, prev, feed_hbm, kill_hbm, tiles_hbm, base_one, base_two, split_tiles, feed_ref, kill_ref, tiles, sems
):
    copies = [
        pltpu.make_async_copy(feed_hbm, feed_ref, sems.at[0]),
        pltpu.make_async_copy(kill_hbm, kill_ref, sems.at[1]),
        pltpu.make_async_copy(tiles_hbm, tiles, sems.at[2]),
    ]
    for copy in copies:
        copy.start()
    for copy in copies[:2]:
        copy.wait()
    fields = [held.at[f] for f in range(FIELDS)]
    stride = 2 * cell_blocks
    pairs = [(f, s) for f in range(FIELDS) for s in range(2)]
    for base, groups in zip((base_one, base_two), chunks):
        for place, group in enumerate(groups):
            for block in range(cell_blocks):
                feed = feed_ref[block : block + 1, :]
                total = feed + kill_ref[block : block + 1, :]
                now = [steps_at(fields[f], group, block, s, stride) for f, s in pairs]
                before = [steps_before(fields[f], prev, f, group, block, s, stride) for f, s in pairs]
                rate_now = pointwise(*now, feed, total)
                rate_before = pointwise(*before, feed, total)
                for index in range(2 * FIELDS):
                    row = (place * FIELDS * 2 + index) * STEPS
                    base[block, row : row + STEPS, :] = (now[index] - before[index]) * (1.0 / time_step) - 0.5 * (
                        rate_now[index] + rate_before[index]
                    )
    copies[2].wait()
    blocks, per_row = tiles.shape[:2]
    for block in range(blocks):
        for k in range(per_row):
            high, low = split(jnp.transpose(tiles[block, k]))
            split_tiles[block, k * LANES : (k + 1) * LANES, :LANES] = high
            split_tiles[block, k * LANES : (k + 1) * LANES, LANES:] = low


def apply_kernel(groups, received, cell_blocks, blocks, per_row, held_back, *refs):
    refs = list(refs)
    cols_ref, split_tiles, base, parts_ref = [refs.pop(0) for _ in range(4)]
    arrived = [refs.pop(0) for _ in received]
    refs = refs[held_back:]
    outs = [refs.pop(0) for _ in range(FIELDS)]
    extended, made, sems = refs
    stride = 2 * cell_blocks
    size = base.shape[1]
    cols = cols_ref[...]
    extended[:cell_blocks] = parts_ref[...]
    for ref, (slots, row) in zip(arrived, received):
        count, width = ref.shape
        per_slot = width // len(slots) // LANES
        for place, slot in enumerate(slots):
            for b in range(per_slot):
                lane = (place * per_slot + b) * LANES
                high, low = split(ref[:, lane : lane + LANES])
                extended[cell_blocks + slot * per_slot + b, row : row + count, :] = high
                extended[cell_blocks + slot * per_slot + b, size + row : size + row + count, :] = low
    for block in range(blocks):
        chosen = jnp.concatenate([extended[cols[k, block]] for k in range(per_row)], axis=1)
        product = jnp.dot(chosen, split_tiles[block], preferred_element_type=F32)
        product = product[:, :LANES] + product[:, LANES:]
        result = base[block] + (product[:size] + product[size:])
        for index in range(size // STEPS):
            group, field, species = index // (2 * FIELDS), index // 2 % FIELDS, index % 2
            at = group * STEPS * stride + block * 2 + species
            made[field, pl.ds(at, STEPS, stride=stride), :] = result[index * STEPS : (index + 1) * STEPS, :]
    span = pl.ds(groups[0] * STEPS * stride, len(groups) * STEPS * stride)
    copies = [pltpu.make_async_copy(made.at[f], outs[f].at[span, :], sems.at[f]) for f in range(FIELDS)]
    for copy in copies:
        copy.start()
    for copy in copies:
        copy.wait()


def per_device(state, dir_one, dir_two, feed, kill, tiles, tile_cols, send_rows, send_count):
    steps, _, cells = state.shape
    cell_blocks = cells // LANES
    stride = 2 * cell_blocks
    blocks, per_row = tiles.shape[:2]
    slot_rows = send_rows.shape[2]
    size_dom = lax.axis_size("dom")

    by_route = {}
    for slot, offset in enumerate(OFFSETS):
        by_route.setdefault(offset % size_dom, []).append(slot)
    slot_groups = sorted(by_route.values(), key=lambda slots: -len(slots))

    def view(array):
        array = array.reshape(steps, 2, cell_blocks, LANES).transpose(0, 2, 1, 3)
        return array.reshape(steps * stride, LANES)

    def unview(array):
        array = array.reshape(steps, cell_blocks, 2, LANES).transpose(0, 2, 1, 3)
        return array.reshape(steps, 2, cells)

    fields = [view(state), view(dir_one), view(dir_two)]
    rows = send_rows.reshape(send_rows.shape[1:])
    counts = send_count
    cols = tile_cols.T
    feed = feed.reshape(cell_blocks, LANES)
    kill = kill.reshape(cell_blocks, LANES)

    vmem = pl.BlockSpec(memory_space=VMEM)
    smem = pl.BlockSpec(memory_space=SMEM)
    anywhere = pl.BlockSpec(memory_space=pl.ANY)
    params = pltpu.CompilerParams(vmem_limit_bytes=16 * 1024 * 1024)

    groups = tuple(range(steps // STEPS))
    late, middle, lead = groups[:1], groups[1:-1], groups[-1:]
    most = middle + lead
    wide, *narrow = slot_groups
    others = [slot for slots in narrow for slot in slots]

    def rows_of(part):
        return len(part) * FIELDS * 2 * STEPS

    def f32(*shape):
        return jax.ShapeDtypeStruct(shape, F32)

    def parts_of(part):
        return jax.ShapeDtypeStruct((cell_blocks, 2 * rows_of(part), LANES), BF16)

    def sends_of(part, chosen):
        return [f32(rows_of(part), len(slots) * slot_rows) for slots in chosen]

    def cost(flops, moved):
        return pl.CostEstimate(flops=flops, bytes_accessed=moved, transcendentals=0)

    def in_hbm(*arrays):
        return [pltpu.with_memory_space_constraint(array, pltpu.HBM) for array in arrays]

    def send_to(send, slots):
        return shift_along(send, "dom", OFFSETS[slots[0]])

    hbm = pl.BlockSpec(memory_space=pltpu.HBM)
    size = rows_of(groups)
    every = len(OFFSETS) * slot_rows
    wide_width = len(wide) * slot_rows
    send, held, listed, last = pl.pallas_call(
        functools.partial(first_kernel, lead, wide, cell_blocks),
        out_shape=[
            f32(rows_of(lead), wide_width),
            f32(FIELDS, steps * stride, LANES),
            jax.ShapeDtypeStruct(rows.shape, jnp.int32),
            f32(FIELDS * stride, LANES),
        ],
        in_specs=[hbm] * (FIELDS + 2),
        out_specs=[vmem] * 4,
        scratch_shapes=[
            VMEM(rows.shape, jnp.int32),
            VMEM(counts.shape, jnp.int32),
            pltpu.SemaphoreType.DMA((2 * FIELDS + 2,)),
        ],
        compiler_params=params,
        cost_estimate=cost(4 * rows_of(lead) * cells * wide_width, 8 * size * cells),
        name="gather_first",
    )(*in_hbm(*fields, rows, counts))
    wide_lead = send_to(send, wide)
    send, *sends, most_parts = pl.pallas_call(
        functools.partial(second_kernel, most, middle, wide, others, cell_blocks),
        out_shape=sends_of(middle, [wide]) + sends_of(most, narrow) + [parts_of(most)],
        in_specs=[vmem] * 2,
        out_specs=[vmem] * (len(narrow) + 2),
        scratch_shapes=[VMEM((cells, every), BF16)],
        compiler_params=params,
        cost_estimate=cost(4 * rows_of(most) * cells * every, 8 * size * cells),
        name="gather_second",
    )(held, listed)
    wide_middle = send_to(send, wide)
    prev = shift_along(last, "tm", 1)
    narrow_most = [send_to(part, slots) for part, slots in zip(sends, narrow)]
    *sends, late_parts = pl.pallas_call(
        functools.partial(third_kernel, late, wide, others, cell_blocks),
        out_shape=sends_of(late, slot_groups) + [parts_of(late)],
        in_specs=[vmem] * 3,
        out_specs=[vmem] * (len(slot_groups) + 1),
        scratch_shapes=[VMEM((cells, every), BF16)],
        compiler_params=params,
        cost_estimate=cost(4 * rows_of(late) * cells * every, 8 * size * cells),
        name="gather_third",
    )(held, prev, listed)
    base_most, base_late, split_tiles = pl.pallas_call(
        functools.partial(local_kernel, (most, late), cell_blocks),
        out_shape=[
            f32(cell_blocks, rows_of(most), LANES),
            f32(cell_blocks, rows_of(late), LANES),
            jax.ShapeDtypeStruct((blocks, per_row * LANES, 2 * LANES), BF16),
        ],
        in_specs=[vmem] * 2 + [hbm] * 3,
        out_specs=[vmem] * 3,
        scratch_shapes=[
            VMEM(feed.shape, F32),
            VMEM(kill.shape, F32),
            VMEM(tiles.shape, F32),
            pltpu.SemaphoreType.DMA((3,)),
        ],
        compiler_params=params,
        cost_estimate=cost(60 * size * cells, 8 * tiles.size),
        name="local_terms",
    )(held, prev, *in_hbm(feed, kill, tiles))

    arrived_late = [send_to(sends[0], wide)]
    sends[1], wide_lead = lax.optimization_barrier((sends[1], wide_lead))
    arrived_late.append(send_to(sends[1], slot_groups[1]))
    for number in range(2, len(sends)):
        sends[number], narrow_most[0], split_tiles = lax.optimization_barrier((sends[number], narrow_most[0], split_tiles))
        arrived_late.append(send_to(sends[number], slot_groups[number]))

    def apply(part, base, parts, transfers, outs):
        inputs = [cols, split_tiles, base, parts, *[array for array, _, _ in transfers]]
        received = [(slots, row) for _, slots, row in transfers]
        return pl.pallas_call(
            functools.partial(apply_kernel, part, received, cell_blocks, blocks, per_row, len(outs)),
            out_shape=[f32(steps * stride, LANES)] * FIELDS,
            in_specs=[vmem] * len(inputs) + [anywhere] * len(outs),
            out_specs=[anywhere] * FIELDS,
            input_output_aliases={len(inputs) + f: f for f in range(len(outs))},
            scratch_shapes=[
                VMEM((cell_blocks + every // LANES, 2 * rows_of(part), LANES), BF16),
                VMEM((FIELDS, len(part) * STEPS * stride, LANES), F32),
                pltpu.SemaphoreType.DMA((FIELDS,)),
            ],
            compiler_params=params,
            cost_estimate=cost(8 * rows_of(part) * blocks * per_row * LANES * LANES, 16 * rows_of(part) * cells),
            name="apply_tiles",
        )(*inputs, *outs)

    transfers = [(wide_middle, wide, 0), (wide_lead, wide, rows_of(middle))]
    transfers += [(array, slots, 0) for array, slots in zip(narrow_most, narrow)]
    outs = apply(most, base_most, most_parts, transfers, [])
    transfers = [(array, slots, 0) for array, slots in zip(arrived_late, slot_groups)]
    outs = apply(late, base_late, late_parts, transfers, outs)
    return tuple(unview(out) for out in outs)


def solution(mesh):
    fields = P(("group", "tm"), None, "dom")
    in_specs = (
        fields,
        fields,
        fields,
        P("dom"),
        P("dom"),
        P("dom", None, None, None),
        P("dom", None),
        P("dom", None, None),
        P("dom", None),
    )
    return jax.shard_map(
        per_device, mesh=mesh, in_specs=in_specs, out_specs=(fields, fields, fields), check_vma=False
    )
```

```python
import functools

import jax
import jax.numpy as jnp
from jax import lax
from jax.experimental import pallas as pl
from jax.experimental.pallas import tpu as pltpu
from jax.sharding import PartitionSpec as P

OFFSETS = (1, -1, 2, -2)
time_step = 0.5
spread_u = 1.0
spread_v = 0.5
LANES = 128
STEPS = 8
FIELDS = 3
VMEM = pltpu.VMEM
SMEM = pltpu.SMEM
F32 = jnp.float32
BF16 = jnp.bfloat16


def shift_along(block, axis, distance):
    size = lax.axis_size(axis)
    return lax.ppermute(block, axis, [((i - distance) % size, i) for i in range(size)])


def steps_at(ref, group, cell_block, species, stride):
    return ref[pl.ds(group * STEPS * stride + cell_block * 2 + species, STEPS, stride=stride), :]


def steps_before(ref, prev_ref, field, group, cell_block, species, stride):
    offset = cell_block * 2 + species
    if group > 0:
        return ref[pl.ds((group * STEPS - 1) * stride + offset, STEPS, stride=stride), :]
    now = steps_at(ref, 0, cell_block, species, stride)
    row = field * stride + offset
    first = jnp.broadcast_to(prev_ref[row : row + 1, :], now.shape)
    index = lax.broadcasted_iota(jnp.int32, now.shape, 0)
    return jnp.where(index == 0, first, pltpu.roll(now, 1, 0))


def split(values):
    high = values.astype(BF16)
    return high, (values - high.astype(F32)).astype(BF16)


def scaled_sum(ref, prev_ref, field, group, cell_block, species, stride):
    now = steps_at(ref, group, cell_block, species, stride)
    before = steps_before(ref, prev_ref, field, group, cell_block, species, stride)
    return (now + before) * (-0.5 * (spread_u, spread_v)[species])


def summed_parts(groups, cell_blocks, fields, prev, parts_ref, high_row, low_row):
    stride = 2 * cell_blocks
    for place, group in enumerate(groups):
        for field in range(FIELDS):
            row = (place * FIELDS + field) * 2 * STEPS
            for block in range(cell_blocks):
                both = [scaled_sum(fields[field], prev, field, group, block, species, stride) for species in range(2)]
                high, low = split(jnp.concatenate(both, axis=0))
                parts_ref[block, high_row + row : high_row + row + 2 * STEPS, :] = high
                parts_ref[block, low_row + row : low_row + row + 2 * STEPS, :] = low


def choose_rows(slots, listed_ref, choose):
    cells = choose.shape[0]
    slot_rows = listed_ref.shape[1]
    cell = lax.broadcasted_iota(jnp.int32, (LANES, slot_rows), 0)
    for place, slot in enumerate(slots):
        listed = listed_ref[slot : slot + 1, :]
        for start in range(0, cells, LANES):
            hit = cell == listed - start
            choose[start : start + LANES, place * slot_rows : (place + 1) * slot_rows] = jnp.where(
                hit, 1.0, 0.0
            ).astype(BF16)


def take_rows(parts, choose, sends):
    size = parts.shape[0] // 2
    start = 0
    for send in sends:
        width = send.shape[1]
        taken = jnp.dot(parts, choose[:, start : start + width], preferred_element_type=F32)
        send[...] = taken[:size] + taken[size:]
        start += width


def side_by_side(parts_ref, rows):
    blocks = [
        jnp.concatenate([parts_ref[b, start : start + count, :] for start, count in rows], axis=0)
        for b in range(parts_ref.shape[0])
    ]
    return jnp.concatenate(blocks, axis=1)


def first_kernel(lead, slots, cell_blocks, *refs):
    refs = list(refs)
    sources = [refs.pop(0) for _ in range(FIELDS)]
    rows_hbm, count_hbm, send, held, listed, last, rows_ref, count_ref, sems = refs
    stride = 2 * cell_blocks
    early = (lead[0] * STEPS - 1) * stride
    late = held.shape[1] - early
    small = [
        pltpu.make_async_copy(rows_hbm, rows_ref, sems.at[2 * FIELDS]),
        pltpu.make_async_copy(count_hbm, count_ref, sems.at[2 * FIELDS + 1]),
    ]
    needed = [
        pltpu.make_async_copy(sources[f].at[pl.ds(early, late), :], held.at[f, pl.ds(early, late), :], sems.at[f])
        for f in range(FIELDS)
    ]
    others = [
        pltpu.make_async_copy(sources[f].at[pl.ds(0, early), :], held.at[f, pl.ds(0, early), :], sems.at[FIELDS + f])
        for f in range(FIELDS)
    ]
    for copy in needed + small:
        copy.start()
    for copy in small:
        copy.wait()
    for copy in others:
        copy.start()
    lane = lax.broadcasted_iota(jnp.int32, rows_ref.shape, 1)
    columns = {}
    for slot in range(rows_ref.shape[0]):
        live = lane[slot : slot + 1] < count_ref[:, slot : slot + 1]
        row = jnp.where(live, rows_ref[slot : slot + 1, :], -1)
        listed[slot : slot + 1, :] = row
        columns[slot] = [row[:, start : start + LANES] for start in range(0, row.shape[1], LANES)]
    columns = [jnp.broadcast_to(column, (STEPS, LANES)) for slot in slots for column in columns[slot]]
    lanes = [column & (LANES - 1) for column in columns]
    blocks = [column >> 7 for column in columns]
    for copy in needed:
        copy.wait()
    for field in range(FIELDS):
        for place, group in enumerate(lead):
            for species in range(2):
                row = ((place * FIELDS + field) * 2 + species) * STEPS
                sums = [
                    scaled_sum(held.at[field], None, field, group, block, species, stride) for block in range(cell_blocks)
                ]
                for number in range(len(columns)):
                    found = jnp.zeros((STEPS, LANES), F32)
                    for block in range(cell_blocks):
                        taken = jnp.take_along_axis(sums[block], lanes[number], axis=1, mode="promise_in_bounds")
                        found = jnp.where(blocks[number] == block, taken, found)
                    send[row : row + STEPS, number * LANES : (number + 1) * LANES] = found
    for field in range(FIELDS):
        last[field * stride : (field + 1) * stride, :] = held[field, -stride:, :]
    for copy in others:
        copy.wait()


def second_kernel(most, middle, wide, others, cell_blocks, held, listed, send, *refs):
    *sends, parts_ref, choose = refs
    size = parts_ref.shape[1] // 2
    middle_size = size * len(middle) // len(most)
    choose_rows(wide + others, listed, choose)
    summed_parts(most, cell_blocks, [held.at[f] for f in range(FIELDS)], None, parts_ref, 0, size)
    width = send.shape[1]
    take_rows(side_by_side(parts_ref, [(0, middle_size), (size, middle_size)]), choose, [send])
    take_rows(side_by_side(parts_ref, [(0, 2 * size)]), choose.at[:, width:], sends)


def third_kernel(late, wide, others, cell_blocks, held, prev, listed, *refs):
    *sends, parts_ref, choose = refs
    size = parts_ref.shape[1] // 2
    choose_rows(wide + others, listed, choose)
    summed_parts(late, cell_blocks, [held.at[f] for f in range(FIELDS)], prev, parts_ref, 0, size)
    take_rows(side_by_side(parts_ref, [(0, 2 * size)]), choose, sends)


def pointwise(u, v, du, dv, ddu, ddv, feed, total):
    square = v * v
    product = u * square
    twice = 2.0 * u * v
    outs = [feed * (1.0 - u) - product, product - total * v]
    for first, second in ((du, dv), (ddu, ddv)):
        react = square * first + twice * second
        outs += [-react - feed * first, react - total * second]
    return outs


def local_kernel(
    chunks, cell_blocks, held, prev, feed_hbm, kill_hbm, tiles_hbm, base_one, base_two, split_tiles, feed_ref, kill_ref, tiles, sems
):
    copies = [
        pltpu.make_async_copy(feed_hbm, feed_ref, sems.at[0]),
        pltpu.make_async_copy(kill_hbm, kill_ref, sems.at[1]),
        pltpu.make_async_copy(tiles_hbm, tiles, sems.at[2]),
    ]
    for copy in copies:
        copy.start()
    for copy in copies[:2]:
        copy.wait()
    fields = [held.at[f] for f in range(FIELDS)]
    stride = 2 * cell_blocks
    pairs = [(f, s) for f in range(FIELDS) for s in range(2)]
    for base, groups in zip((base_one, base_two), chunks):
        for place, group in enumerate(groups):
            for block in range(cell_blocks):
                feed = feed_ref[block : block + 1, :]
                total = feed + kill_ref[block : block + 1, :]
                now = [steps_at(fields[f], group, block, s, stride) for f, s in pairs]
                before = [steps_before(fields[f], prev, f, group, block, s, stride) for f, s in pairs]
                rate_now = pointwise(*now, feed, total)
                rate_before = pointwise(*before, feed, total)
                for index in range(2 * FIELDS):
                    row = (place * FIELDS * 2 + index) * STEPS
                    base[block, row : row + STEPS, :] = (now[index] - before[index]) * (1.0 / time_step) - 0.5 * (
                        rate_now[index] + rate_before[index]
                    )
    copies[2].wait()
    blocks, per_row = tiles.shape[:2]
    for block in range(blocks):
        for k in range(per_row):
            high, low = split(jnp.transpose(tiles[block, k]))
            split_tiles[block, k * LANES : (k + 1) * LANES, :LANES] = high
            split_tiles[block, k * LANES : (k + 1) * LANES, LANES:] = low


def apply_kernel(groups, received, cell_blocks, blocks, per_row, held_back, *refs):
    refs = list(refs)
    cols_ref, split_tiles, base, parts_ref = [refs.pop(0) for _ in range(4)]
    arrived = [refs.pop(0) for _ in received]
    refs = refs[held_back:]
    outs = [refs.pop(0) for _ in range(FIELDS)]
    extended, made, sems = refs
    stride = 2 * cell_blocks
    size = base.shape[1]
    cols = cols_ref[...]
    extended[:cell_blocks] = parts_ref[...]
    for ref, (slots, row) in zip(arrived, received):
        count, width = ref.shape
        per_slot = width // len(slots) // LANES
        for place, slot in enumerate(slots):
            for b in range(per_slot):
                lane = (place * per_slot + b) * LANES
                high, low = split(ref[:, lane : lane + LANES])
                extended[cell_blocks + slot * per_slot + b, row : row + count, :] = high
                extended[cell_blocks + slot * per_slot + b, size + row : size + row + count, :] = low
    for block in range(blocks):
        chosen = jnp.concatenate([extended[cols[k, block]] for k in range(per_row)], axis=1)
        product = jnp.dot(chosen, split_tiles[block], preferred_element_type=F32)
        product = product[:, :LANES] + product[:, LANES:]
        result = base[block] + (product[:size] + product[size:])
        for index in range(size // STEPS):
            group, field, species = index // (2 * FIELDS), index // 2 % FIELDS, index % 2
            at = group * STEPS * stride + block * 2 + species
            made[field, pl.ds(at, STEPS, stride=stride), :] = result[index * STEPS : (index + 1) * STEPS, :]
    span = pl.ds(groups[0] * STEPS * stride, len(groups) * STEPS * stride)
    copies = [pltpu.make_async_copy(made.at[f], outs[f].at[span, :], sems.at[f]) for f in range(FIELDS)]
    for copy in copies:
        copy.start()
    for copy in copies:
        copy.wait()


def per_device(state, dir_one, dir_two, feed, kill, tiles, tile_cols, send_rows, send_count):
    steps, _, cells = state.shape
    cell_blocks = cells // LANES
    stride = 2 * cell_blocks
    blocks, per_row = tiles.shape[:2]
    slot_rows = send_rows.shape[2]
    size_dom = lax.axis_size("dom")

    by_route = {}
    for slot, offset in enumerate(OFFSETS):
        by_route.setdefault(offset % size_dom, []).append(slot)
    slot_groups = sorted(by_route.values(), key=lambda slots: -len(slots))

    def view(array):
        array = array.reshape(steps, 2, cell_blocks, LANES).transpose(0, 2, 1, 3)
        return array.reshape(steps * stride, LANES)

    def unview(array):
        array = array.reshape(steps, cell_blocks, 2, LANES).transpose(0, 2, 1, 3)
        return array.reshape(steps, 2, cells)

    fields = [view(state), view(dir_one), view(dir_two)]
    rows = send_rows.reshape(send_rows.shape[1:])
    counts = send_count
    cols = tile_cols.T
    feed = feed.reshape(cell_blocks, LANES)
    kill = kill.reshape(cell_blocks, LANES)

    vmem = pl.BlockSpec(memory_space=VMEM)
    smem = pl.BlockSpec(memory_space=SMEM)
    anywhere = pl.BlockSpec(memory_space=pl.ANY)
    params = pltpu.CompilerParams(vmem_limit_bytes=16 * 1024 * 1024)

    groups = tuple(range(steps // STEPS))
    late, middle, lead = groups[:1], groups[1:-1], groups[-1:]
    most = middle + lead
    wide, *narrow = slot_groups
    others = [slot for slots in narrow for slot in slots]

    def rows_of(part):
        return len(part) * FIELDS * 2 * STEPS

    def f32(*shape):
        return jax.ShapeDtypeStruct(shape, F32)

    def parts_of(part):
        return jax.ShapeDtypeStruct((cell_blocks, 2 * rows_of(part), LANES), BF16)

    def sends_of(part, chosen):
        return [f32(rows_of(part), len(slots) * slot_rows) for slots in chosen]

    def cost(flops, moved):
        return pl.CostEstimate(flops=flops, bytes_accessed=moved, transcendentals=0)

    def in_hbm(*arrays):
        return [pltpu.with_memory_space_constraint(array, pltpu.HBM) for array in arrays]

    def send_to(send, slots):
        return shift_along(send, "dom", OFFSETS[slots[0]])

    hbm = pl.BlockSpec(memory_space=pltpu.HBM)
    size = rows_of(groups)
    every = len(OFFSETS) * slot_rows
    wide_width = len(wide) * slot_rows
    send, held, listed, last = pl.pallas_call(
        functools.partial(first_kernel, lead, wide, cell_blocks),
        out_shape=[
            f32(rows_of(lead), wide_width),
            f32(FIELDS, steps * stride, LANES),
            jax.ShapeDtypeStruct(rows.shape, jnp.int32),
            f32(FIELDS * stride, LANES),
        ],
        in_specs=[hbm] * (FIELDS + 2),
        out_specs=[vmem] * 4,
        scratch_shapes=[
            VMEM(rows.shape, jnp.int32),
            VMEM(counts.shape, jnp.int32),
            pltpu.SemaphoreType.DMA((2 * FIELDS + 2,)),
        ],
        compiler_params=params,
        cost_estimate=cost(4 * rows_of(lead) * cells * wide_width, 8 * size * cells),
        name="gather_first",
    )(*in_hbm(*fields, rows, counts))
    wide_lead = send_to(send, wide)
    send, *sends, most_parts = pl.pallas_call(
        functools.partial(second_kernel, most, middle, wide, others, cell_blocks),
        out_shape=sends_of(middle, [wide]) + sends_of(most, narrow) + [parts_of(most)],
        in_specs=[vmem] * 2,
        out_specs=[vmem] * (len(narrow) + 2),
        scratch_shapes=[VMEM((cells, every), BF16)],
        compiler_params=params,
        cost_estimate=cost(4 * rows_of(most) * cells * every, 8 * size * cells),
        name="gather_second",
    )(held, listed)
    wide_middle = send_to(send, wide)
    prev = shift_along(last, "tm", 1)
    narrow_most = [send_to(part, slots) for part, slots in zip(sends, narrow)]
    *sends, late_parts = pl.pallas_call(
        functools.partial(third_kernel, late, wide, others, cell_blocks),
        out_shape=sends_of(late, slot_groups) + [parts_of(late)],
        in_specs=[vmem] * 3,
        out_specs=[vmem] * (len(slot_groups) + 1),
        scratch_shapes=[VMEM((cells, every), BF16)],
        compiler_params=params,
        cost_estimate=cost(4 * rows_of(late) * cells * every, 8 * size * cells),
        name="gather_third",
    )(held, prev, listed)
    base_most, base_late, split_tiles = pl.pallas_call(
        functools.partial(local_kernel, (most, late), cell_blocks),
        out_shape=[
            f32(cell_blocks, rows_of(most), LANES),
            f32(cell_blocks, rows_of(late), LANES),
            jax.ShapeDtypeStruct((blocks, per_row * LANES, 2 * LANES), BF16),
        ],
        in_specs=[vmem] * 2 + [hbm] * 3,
        out_specs=[vmem] * 3,
        scratch_shapes=[
            VMEM(feed.shape, F32),
            VMEM(kill.shape, F32),
            VMEM(tiles.shape, F32),
            pltpu.SemaphoreType.DMA((3,)),
        ],
        compiler_params=params,
        cost_estimate=cost(60 * size * cells, 8 * tiles.size),
        name="local_terms",
    )(held, prev, *in_hbm(feed, kill, tiles))

    arrived_late = [send_to(sends[0], wide)]
    sends[1], wide_lead = lax.optimization_barrier((sends[1], wide_lead))
    arrived_late.append(send_to(sends[1], slot_groups[1]))
    for number in range(2, len(sends)):
        sends[number], narrow_most[0], split_tiles = lax.optimization_barrier((sends[number], narrow_most[0], split_tiles))
        arrived_late.append(send_to(sends[number], slot_groups[number]))

    def apply(part, base, parts, transfers, outs):
        inputs = [cols, split_tiles, base, parts, *[array for array, _, _ in transfers]]
        received = [(slots, row) for _, slots, row in transfers]
        return pl.pallas_call(
            functools.partial(apply_kernel, part, received, cell_blocks, blocks, per_row, len(outs)),
            out_shape=[f32(steps * stride, LANES)] * FIELDS,
            in_specs=[vmem] * len(inputs) + [anywhere] * len(outs),
            out_specs=[anywhere] * FIELDS,
            input_output_aliases={len(inputs) + f: f for f in range(len(outs))},
            scratch_shapes=[
                VMEM((cell_blocks + every // LANES, 2 * rows_of(part), LANES), BF16),
                VMEM((FIELDS, len(part) * STEPS * stride, LANES), F32),
                pltpu.SemaphoreType.DMA((FIELDS,)),
            ],
            compiler_params=params,
            cost_estimate=cost(8 * rows_of(part) * blocks * per_row * LANES * LANES, 16 * rows_of(part) * cells),
            name="apply_tiles",
        )(*inputs, *outs)

    transfers = [(wide_middle, wide, 0), (wide_lead, wide, rows_of(middle))]
    transfers += [(array, slots, 0) for array, slots in zip(narrow_most, narrow)]
    outs = apply(most, base_most, most_parts, transfers, [])
    transfers = [(array, slots, 0) for array, slots in zip(arrived_late, slot_groups)]
    outs = apply(late, base_late, late_parts, transfers, outs)
    return tuple(unview(out) for out in outs)


def solution(mesh):
    fields = P(("group", "tm"), None, "dom")
    in_specs = (
        fields,
        fields,
        fields,
        P("dom"),
        P("dom"),
        P("dom", None, None, None),
        P("dom", None),
        P("dom", None, None),
        P("dom", None),
    )
    return jax.shard_map(
        per_device, mesh=mesh, in_specs=in_specs, out_specs=(fields, fields, fields), check_vma=False
    )
```
